32 devices in a mesh: section: 4 (over y, x), dp: 8 (over z, core).
Axes of the slice: x: 2, y: 2, z: 4, core: 2. Of those that a mesh axis runs over, the one named last changes fastest.
Arguments:
- features: bfloat16 [768, 8, 8, 256], P('dp'), may hold values from -6 to 6
- buckets: int32 [768], P('dp'), may hold values from 0 to 1
- micro_order: int32 [8, 96], P('dp'), may hold values from 0 to 95, each once within a row
- labels: int32 [768, 40], P('dp'), may hold values 0 or 1
- conv_first: bfloat16 [2304, 512], P('dp'), may hold values from -0.125 to 0.125
- conv_short: bfloat16 [256, 512], P('dp'), may hold values from -0.375 to 0.375
- conv_second: bfloat16 [4608, 512], P('dp'), may hold values from -0.09375 to 0.09375
- conv_third: bfloat16 [4608, 512], P('dp'), may hold values from -0.09375 to 0.09375
- conv_fourth: bfloat16 [4608, 512], P('dp'), may hold values from -0.09375 to 0.09375
- norm_gains: bfloat16 [5, 512], P(None, 'dp'), may hold values from 0.25 to 1.75
- norm_biases: bfloat16 [5, 512], P(None, 'dp'), may hold values from -2.5 to 2.5
- head_weight: bfloat16 [512, 40], P('dp'), may hold values from -1 to 1
- head_bias: bfloat16 [40], replicated, may hold values from -2.5 to 2.5
Outputs:
- pooled_z: float32 [768, 512], P('dp', 'section')
- input_grad: float32 [768, 8, 8, 256], P('dp', None, None, 'section')
- conv_first_grad: float32 [2304, 512], P('dp')
- conv_short_grad: float32 [256, 512], P('dp')
- conv_second_grad: float32 [4608, 512], P('dp')
- conv_third_grad: float32 [4608, 512], P('dp')
- conv_fourth_grad: float32 [4608, 512], P('dp')
- norm_gains_grad: float32 [5, 512], P(None, 'dp')
- norm_biases_grad: float32 [5, 512], P(None, 'dp')
- head_weight_grad: float32 [512, 40], P('dp')
- head_bias_grad: float32 [40], replicated
The draws below stay inside these ranges and needn't reach their ends.
Inputs may be any that keep to these rules, and one draw needn't show every extreme that they name: `micro_order`: each row holds every number from 0 to 95 once.
All inputs are finite; a program needn't handle non-finite values. No bound on the sum of `labels` on one device may be relied on, other than what follows from the above.
Results may differ from the reference program's by a relative error of at most 0.015.
Values may be sent and summed in bfloat16 or wider, within the bound.
No kernel may reach another device: no remote copies, remote signals or barrier semaphores. Data moves between devices by JAX's collectives and lax.ppermute only.
A program may use at most 192 MiB of HBM per device.

```python
import math
import jax
import jax.numpy as jnp
from jax import lax

C_IN = 256
C = 512
TASKS = 40
H_IN = 8
MICRO = 6
FW_STEPS = 20
MB = 16
IMG_DP = 96
GROUPS = 8
IMAGES = 768
N_DP = 8


def draw_head_weight(key, part):
    key = jax.random.fold_in(key, 11)
    scale_key, value_key = jax.random.split(key)
    scales = jnp.exp(jax.random.uniform(scale_key, (1, TASKS), jnp.float32, math.log(0.3), math.log(3.0)))
    base_draw = jax.random.truncated_normal(value_key, -3.0, 3.0, (C, TASKS), jnp.float32)
    return (base_draw * scales * (1.0 / math.sqrt(C))).astype(jnp.bfloat16)


def set_ends(array, rng, least, high):
    extent = array.shape
    index_at = [jax.random.randint(jax.random.fold_in(rng, axis), (), 0, extent[axis]) for axis in range(len(extent))]
    array = array.at[tuple(index_at)].set(least)
    longest = extent.index(max(extent))
    index_at[longest] = (index_at[longest] + 1) % extent[longest]
    return array.at[tuple(index_at)].set(high)


def level_of(own_key, dims, cuts, smallest, top_value):
    gain = 1.0
    for dim, shards_of in cuts:
        steps = jax.random.uniform(jax.random.fold_in(jax.random.fold_in(own_key, 6), dim), (shards_of,), jnp.float32, smallest / len(cuts), top_value / len(cuts))
        gain = gain * jnp.repeat(jnp.exp(steps), dims[dim] // shards_of).reshape((-1,) + (1,) * (len(dims) - 1 - dim))
    return gain


def bell_draw(rng, dims, scale, reach, cuts=(), kind=jnp.bfloat16):
    array = scale * jax.random.normal(rng, dims, jnp.float32)
    if cuts:
        array = array * level_of(rng, dims, cuts, -0.22, 0.18)
    return jnp.clip(array, -reach, reach).astype(kind)


def setup_inputs(seed: int = 0) -> dict:
    key_list = jax.random.split(jax.random.key(seed), 14)
    features = bell_draw(key_list[0], (IMAGES, H_IN, H_IN, C_IN), 1.0, 6.0, ((0, 8),))
    buckets = set_ends(jax.random.randint(key_list[1], (IMAGES,), 0, 2), jax.random.fold_in(key_list[1], 1), 0, 1).astype(jnp.int32)
    micro_order = jax.vmap(lambda own: jax.random.permutation(own, IMG_DP))(jax.random.split(key_list[2], GROUPS)).reshape((GROUPS, IMG_DP)).astype(jnp.int32)
    labels = set_ends((jax.random.randint(key_list[3], (IMAGES, TASKS), 0, 2) < 1).astype(jnp.int32), jax.random.fold_in(key_list[3], 1), 0, 1)
    conv_first = bell_draw(key_list[4], (9 * C_IN, C), (9 * C_IN) ** -0.5, 0.125, ((0, 8),))
    conv_short = bell_draw(key_list[5], (C_IN, C), C_IN ** -0.5, 0.375, ((0, 8),))
    conv_second = bell_draw(key_list[6], (9 * C, C), (9 * C) ** -0.5, 0.09375, ((0, 8),))
    conv_third = bell_draw(key_list[7], (9 * C, C), (9 * C) ** -0.5, 0.09375, ((0, 8),))
    conv_fourth = bell_draw(key_list[8], (9 * C, C), (9 * C) ** -0.5, 0.09375, ((0, 8),))
    norm_gains = jnp.clip(1.0 + 0.15 * jax.random.normal(key_list[9], (5, C), jnp.float32), 0.25, 1.75).astype(jnp.bfloat16)
    norm_biases = bell_draw(key_list[10], (5, C), 0.5, 2.5, ((1, 8),))
    head_weight = draw_head_weight(jax.random.fold_in(key_list[13], 71), 0)
    head_bias = bell_draw(key_list[12], (TASKS,), 0.5, 2.5)
    return dict(features=features, buckets=buckets, micro_order=micro_order, labels=labels, conv_first=conv_first, conv_short=conv_short, conv_second=conv_second, conv_third=conv_third, conv_fourth=conv_fourth, norm_gains=norm_gains, norm_biases=norm_biases, head_weight=head_weight, head_bias=head_bias)


EPSILON = 1e-05
SOFTMAX_HEAT = 0.01
MAXIMUM_ACCURACY = lax.Precision.HIGHEST

@jax.custom_vjp
def low(v):
    return lax.optimization_barrier(v.astype(jnp.bfloat16)).astype(jnp.float32)

@jax.custom_vjp
def low_back(v):
    return v

def low_keep(v):
    return (low(v), None)

def low_pass(kept, grad):
    return (grad,)

def back_keep(v):
    return (v, None)

def back_low(kept, grad):
    return (low(grad),)
low.defvjp(low_keep, low_pass)
low_back.defvjp(back_keep, back_low)

def valid_masks(side_in, grid_side):
    places = jnp.arange(grid_side, dtype=jnp.int32)
    half_places = places[:grid_side // 2]
    side_out = side_in // 2
    inner_mask = (places[None, :, None] < side_in[:, None, None]) & (places[None, None, :] < side_in[:, None, None])
    outer_mask = (half_places[None, :, None] < side_out[:, None, None]) & (half_places[None, None, :] < side_out[:, None, None])
    return (inner_mask.astype(jnp.float32)[..., None], outer_mask.astype(jnp.float32)[..., None])

def batch_norm(pre_act, norm_gain, norm_bias, valid_mask):
    total = jnp.sum(valid_mask)
    mean_val = lax.optimization_barrier(jnp.sum(pre_act * valid_mask, axis=(0, 1, 2))) / total
    centred = pre_act - mean_val
    spread = lax.optimization_barrier(jnp.sum(centred * centred * valid_mask, axis=(0, 1, 2))) / total
    return centred * lax.rsqrt(spread + EPSILON) * norm_gain + norm_bias

def conv_taps(activation, stride):
    grid_side = activation.shape[1]
    padded = jnp.pad(activation, ((0, 0), (1, 1), (1, 1), (0, 0)))
    tap_list = [padded[:, tap_row:tap_row + grid_side:stride, tap_col:tap_col + grid_side:stride, :] for tap_row in range(3) for tap_col in range(3)]
    return jnp.concatenate(tap_list, axis=-1)

def conv_ref(activation, weight, stride):
    return jnp.einsum('nhwk,kc->nhwc', conv_taps(activation, stride), weight, precision=MAXIMUM_ACCURACY)

def micro_forward(images, valid_in, valid_out, params):
    w_first, w_short, w_second, w_third, w_fourth, gains, biases = params
    images = images * valid_in
    pre_first = low_back(conv_ref(images, w_first, 2))
    pre_short = low_back(jnp.einsum('nhwk,kc->nhwc', images[:, ::2, ::2, :], w_short, precision=MAXIMUM_ACCURACY))
    hidden = low(low_back(jax.nn.silu(batch_norm(pre_first, gains[0], biases[0], valid_out)) * valid_out))
    branch = low(low_back(batch_norm(pre_short, gains[1], biases[1], valid_out) * valid_out))
    pre_second = low_back(conv_ref(hidden, w_second, 1))
    normed = low(low_back(batch_norm(pre_second, gains[2], biases[2], valid_out) * valid_out))
    joined = low(jax.nn.silu(normed + branch) * valid_out)
    pre_third = low_back(conv_ref(joined, w_third, 1))
    block_hidden = low(low_back(jax.nn.silu(batch_norm(pre_third, gains[3], biases[3], valid_out)) * valid_out))
    pre_fourth = low_back(conv_ref(block_hidden, w_fourth, 1))
    result = jax.nn.silu(batch_norm(pre_fourth, gains[4], biases[4], valid_out) + low_back(joined)) * valid_out
    return lax.optimization_barrier(jnp.sum(result, axis=(1, 2))) / lax.optimization_barrier(jnp.sum(valid_out, axis=(1, 2)))

def task_losses(pooled_z, head_w, head_b, targets):
    logits = jnp.dot(low(pooled_z), head_w, precision=MAXIMUM_ACCURACY) + head_b
    return lax.optimization_barrier(jnp.sum(jax.nn.softplus(logits) - targets * logits, axis=0))

def frank_wolfe(inner_product_matrix, step_count):
    start_weights = jnp.full((inner_product_matrix.shape[0],), 1.0 / inner_product_matrix.shape[0], dtype=inner_product_matrix.dtype)

    def advance(step_index, task_mixing_weights):
        simplex_corner = jax.nn.softmax(-jnp.dot(inner_product_matrix, task_mixing_weights, precision=MAXIMUM_ACCURACY) / SOFTMAX_HEAT)
        step_rate = 2.0 / (step_index.astype(inner_product_matrix.dtype) + 2.0)
        return (1.0 - step_rate) * task_mixing_weights + step_rate * simplex_corner
    return lax.fori_loop(0, step_count, advance, start_weights)

def reference(features, buckets, micro_order, labels, conv_first, conv_short, conv_second, conv_third, conv_fourth, norm_gains, norm_biases, head_weight, head_bias):
    floats = jnp.float32
    side_in = (H_IN // 2 * (1 + buckets)).astype(jnp.int32)
    valid_in, valid_out = valid_masks(side_in, H_IN)
    targets = labels.astype(floats)
    inverse = jnp.argsort(micro_order, axis=1).astype(jnp.int32)

    def grouped(values):
        values = values.reshape((N_DP, IMG_DP) + values.shape[1:])
        values = jax.vmap(lambda group_vals, group_order: group_vals[group_order])(values, micro_order.astype(jnp.int32))
        return values.reshape((N_DP * MICRO, MB) + values.shape[2:])
    masks_in = grouped(valid_in.astype(floats))
    masks_out = grouped(valid_out.astype(floats))
    step_fn = jax.checkpoint(micro_forward)

    def forward(feature_vals, w_first, w_short, w_second, w_third, w_fourth, gains, biases, head_w, head_b):
        params = (w_first, w_short, w_second, w_third, w_fourth, gains, biases)
        pooled = lax.map(lambda blocks: step_fn(blocks[0], blocks[1], blocks[2], params), (grouped(feature_vals), masks_in, masks_out))
        pooled = pooled.reshape(N_DP, IMG_DP, C)
        pooled = jax.vmap(lambda group_vals, group_order: group_vals[group_order])(pooled, inverse).reshape(IMAGES, C)
        return (pooled, task_losses(pooled, head_w, head_b, targets))
    inputs = [array_in.astype(floats) for array_in in (features, conv_first, conv_short, conv_second, conv_third, conv_fourth, norm_gains, norm_biases, head_weight, head_bias)]
    (pooled, losses), pullback = jax.vjp(forward, inputs[0], inputs[1], inputs[2], inputs[3], inputs[4], inputs[5], inputs[6], inputs[7], inputs[8], inputs[9])
    head_w32 = inputs[8]
    head_b32 = inputs[9]
    _, head_pull = jax.vjp(lambda pooled_rows: task_losses(pooled_rows, head_w32, head_b32, targets), pooled)
    jacobian = jax.vmap(lambda basis: head_pull(basis)[0])(jnp.eye(TASKS, dtype=floats))
    flat_rows = jacobian.reshape(TASKS, IMAGES * C)
    inner_product_matrix = jnp.dot(flat_rows, flat_rows.T, precision=MAXIMUM_ACCURACY) / IMAGES
    task_mixing_weights = frank_wolfe(inner_product_matrix, FW_STEPS)
    grads = pullback((jnp.zeros_like(pooled), task_mixing_weights))
    return (pooled, grads[0], grads[1], grads[2], grads[3], grads[4], grads[5], grads[6], grads[7], grads[8], grads[9])
```

```python
import functools

import jax
import jax.numpy as jnp
from jax import lax
from jax.experimental import pallas as pl
from jax.experimental.pallas import tpu as pltpu
from jax.sharding import Mesh, PartitionSpec as P

MICRO = 6
FW_STEPS = 20
EPSILON = 1e-05
SOFTMAX_HEAT = 0.01
HIGHEST = lax.Precision.HIGHEST
CHUNKS = 1

f32 = jnp.float32
bf16 = jnp.bfloat16
L = 128

PLANE_TAPS = ((4, -1), (3, 5), (1, 7), (0, 2, 6, 8))
FIRST_COLS = tuple(tap for taps in PLANE_TAPS for tap in taps)


def call(kernel, outs, args, scratch=(), scalars=1, flops=0, vmem_mb=56):
    specs = [pl.BlockSpec(memory_space=pltpu.SMEM)] * scalars
    specs += [pl.BlockSpec(memory_space=pltpu.VMEM)] * (len(args) - scalars)
    size = sum(a.size * a.dtype.itemsize for a in args)
    size += sum(o.size * o.dtype.itemsize for o in outs)
    return pl.pallas_call(
        kernel,
        out_shape=tuple(outs),
        in_specs=specs,
        out_specs=tuple(pl.BlockSpec(memory_space=pltpu.VMEM) for _ in outs),
        scratch_shapes=list(scratch),
        compiler_params=pltpu.CompilerParams(vmem_limit_bytes=vmem_mb << 20),
        cost_estimate=pl.CostEstimate(flops=int(flops), bytes_accessed=int(size), transcendentals=0),
    )(*args)


def sds(*shape, dtype=f32):
    return jax.ShapeDtypeStruct(shape, dtype)


def nt_dot(x, y):
    return lax.dot_general(x, y, (((1,), (1,)), ((), ())), preferred_element_type=f32)


def tn_dot(x, y):
    return lax.dot_general(x, y, (((0,), (0,)), ((), ())), preferred_element_type=f32)


def sigmoid(v):
    return 1.0 / (1.0 + jnp.exp(-v))


def pixel_mask(i, big):
    return None if (i // 4 < 2 and i % 4 < 2) else big


def masked(value, i, big):
    return value if pixel_mask(i, big) is None else value * big


def per_micro(value, nm):
    rows, lanes = value.shape
    return jnp.sum(value.reshape(nm, rows // nm, lanes), axis=1)


def spread_micro(value, im):
    nm, lanes = value.shape
    return jnp.broadcast_to(value[:, None, :], (nm, im // nm, lanes)).reshape(im, lanes)


def blk(ref, i, im):
    return ref[i * im : (i + 1) * im, :]


def norm_forward(p_ref, xhat_ref, inv_ref, big, nm):
    im = big.shape[0]
    total = per_micro(4.0 + 12.0 * big, nm)
    acc = jnp.zeros_like(big)
    for i in range(16):
        acc = acc + masked(blk(p_ref, i, im), i, big)
    mean = spread_micro(per_micro(acc, nm) / total, im)
    acc = jnp.zeros_like(big)
    for i in range(16):
        cen = blk(p_ref, i, im) - mean
        acc = acc + masked(cen * cen, i, big)
    inv = lax.rsqrt(per_micro(acc, nm) / total + EPSILON)
    inv = spread_micro(inv, im)
    inv_ref[...] = inv
    for i in range(16):
        xhat_ref[i * im : (i + 1) * im, :] = (blk(p_ref, i, im) - mean) * inv


def norm_backward(dy_ref, xhat_ref, inv_ref, gain, big, nm, out_ref):
    im = big.shape[0]
    total = per_micro(4.0 + 12.0 * big, nm)
    sum_dy = jnp.zeros_like(big)
    sum_dx = jnp.zeros_like(big)
    for i in range(16):
        dy = blk(dy_ref, i, im)
        sum_dy = sum_dy + dy
        sum_dx = sum_dx + dy * blk(xhat_ref, i, im)
    sum_dy = per_micro(sum_dy, nm)
    sum_dx = per_micro(sum_dx, nm)
    mean_dy = spread_micro(sum_dy / total, im)
    mean_dx = spread_micro(sum_dx / total, im)
    scale = inv_ref[...] * gain
    for i in range(16):
        off = masked(mean_dy + blk(xhat_ref, i, im) * mean_dx, i, big)
        grad = scale * (blk(dy_ref, i, im) - off)
        out_ref[i * im : (i + 1) * im, :] = grad.astype(bf16)
    return jnp.sum(sum_dx, axis=0, keepdims=True), jnp.sum(sum_dy, axis=0, keepdims=True)


def load_weights(q, w_ref, ws):
    channels = 4 * L
    for t in range(9):
        for j in range(4):
            start = pl.multiple_of(t * channels + (q ^ j) * L, L)
            ws[j * L : (j + 1) * L, t * L : (t + 1) * L] = w_ref[pl.ds(start, L), :]


def row_taps(r):
    return (3 * L if r == 3 else 0), (6 * L if r == 0 else 9 * L)


def conv_forward(q, x_refs, w_ref, xs, ws, y, p, im):
    for j in range(4):
        xs[:, j * L : (j + 1) * L] = x_refs[j][...]
    load_weights(q, w_ref, ws)
    for r in range(4):
        lo, hi = row_taps(r)
        rows = slice(r * 4 * im, (r + 1) * 4 * im)
        y[rows, lo:hi] = jnp.dot(xs[rows, :], ws[:, lo:hi], preferred_element_type=f32)
    for r in range(4):
        for c in range(4):
            acc = None
            for t in range(9):
                ri, ci = r + t // 3 - 1, c + t % 3 - 1
                if 0 <= ri < 4 and 0 <= ci < 4:
                    i = ri * 4 + ci
                    term = y[i * im : (i + 1) * im, t * L : (t + 1) * L]
                    acc = term if acc is None else acc + term
            p[(r * 4 + c) * im : (r * 4 + c + 1) * im, :] = acc


def spread_taps(dp_ref, d, im, rows_at, all_taps):
    for r in range(4):
        lo, hi = (0, 9 * L) if all_taps else row_taps(r)
        for c in range(4):
            at = rows_at + (r * 4 + c) * im
            for t in range(lo // L, hi // L):
                ro, co = r - t // 3 + 1, c - t % 3 + 1
                if 0 <= ro < 4 and 0 <= co < 4:
                    value = blk(dp_ref, ro * 4 + co, im)
                else:
                    value = jnp.zeros((im, L), bf16)
                d[at : at + im, t * L : (t + 1) * L] = value


def conv_back_input(q, dp_ref, w_ref, ws, d, outs, im):
    load_weights(q, w_ref, ws)
    spread_taps(dp_ref, d, im, 0, False)
    for r in range(4):
        lo, hi = row_taps(r)
        rows = slice(r * 4 * im, (r + 1) * 4 * im)
        dx = nt_dot(d[rows, lo:hi], ws[:, lo:hi])
        for j in range(4):
            outs[j][rows, :] = dx[:, j * L : (j + 1) * L].astype(outs[j].dtype)


def first_forward(nm, c_ref, x, w, w_short, params, big_ref, h, s, xh1, inv1, xh2, inv2, wsc, y, p1, p2):
    big = big_ref[...]
    im = big.shape[0]
    cin = 2 * L
    col = 0
    for k, taps in enumerate(PLANE_TAPS):
        for n, t in enumerate(taps):
            src = w_short[...] if t < 0 else w[t * cin : (t + 1) * cin, :]
            wsc[:, (col + n) * L : (col + n + 1) * L] = src
        cols = slice(col * L, (col + len(taps)) * L)
        y[:, cols] = jnp.dot(
            x[k * 16 * im : (k + 1) * 16 * im, :], wsc[:, cols], preferred_element_type=f32
        )
        col += len(taps)
    for r in range(4):
        for c in range(4):
            o = r * 4 + c
            acc = None
            for n, t in enumerate(FIRST_COLS):
                if t < 0:
                    p2[o * im : (o + 1) * im, :] = y[o * im : (o + 1) * im, n * L : (n + 1) * L]
                    continue
                ri = r - 1 if t // 3 == 0 else r
                ci = c - 1 if t % 3 == 0 else c
                if ri >= 0 and ci >= 0:
                    i = ri * 4 + ci
                    term = y[i * im : (i + 1) * im, n * L : (n + 1) * L]
                    acc = term if acc is None else acc + term
            p1[o * im : (o + 1) * im, :] = acc
    norm_forward(p1, xh1, inv1, big, nm)
    norm_forward(p2, xh2, inv2, big, nm)
    for i in range(16):
        rows = slice(i * im, (i + 1) * im)
        v = blk(xh1, i, im) * params[0:1, :] + params[5:6, :]
        h[rows, :] = masked(v * sigmoid(v), i, big).astype(bf16)
        v = blk(xh2, i, im) * params[1:2, :] + params[6:7, :]
        s[rows, :] = masked(v, i, big).astype(bf16)


def second_forward(nm, q_ref, x0, x1, x2, x3, w, params, big_ref, s, out, v_out, xh, inv, xs, ws, y, p):
    big = big_ref[...]
    im = big.shape[0]
    conv_forward(q_ref[0], (x0, x1, x2, x3), w, xs, ws, y, p, im)
    norm_forward(p, xh, inv, big, nm)
    for i in range(16):
        rows = slice(i * im, (i + 1) * im)
        u = blk(xh, i, im) * params[2:3, :] + params[7:8, :]
        u = masked(u, i, big).astype(bf16).astype(f32)
        v = u + s[rows, :].astype(f32)
        v_out[rows, :] = v
        out[rows, :] = masked(v * sigmoid(v), i, big).astype(bf16)


def third_forward(nm, q_ref, x0, x1, x2, x3, w, params, big_ref, out, xh, inv, xs, ws, y, p):
    big = big_ref[...]
    im = big.shape[0]
    conv_forward(q_ref[0], (x0, x1, x2, x3), w, xs, ws, y, p, im)
    norm_forward(p, xh, inv, big, nm)
    for i in range(16):
        rows = slice(i * im, (i + 1) * im)
        v = blk(xh, i, im) * params[3:4, :] + params[8:9, :]
        out[rows, :] = masked(v * sigmoid(v), i, big).astype(bf16)


def fourth_forward(
    nm, q_ref, x0, x1, x2, x3, w, params, big_ref, res, head, pooled, logits, xh, inv, xs, ws, y, p
):
    big = big_ref[...]
    im = big.shape[0]
    conv_forward(q_ref[0], (x0, x1, x2, x3), w, xs, ws, y, p, im)
    norm_forward(p, xh, inv, big, nm)
    acc = jnp.zeros_like(big)
    for i in range(16):
        rows = slice(i * im, (i + 1) * im)
        v = blk(xh, i, im) * params[4:5, :] + params[9:10, :] + res[rows, :].astype(f32)
        acc = acc + masked(v * sigmoid(v), i, big)
    pool = acc / (4.0 + 12.0 * big)
    pooled[...] = pool
    logits[...] = jnp.dot(pool.astype(bf16), head[...], preferred_element_type=f32)


def head_errors(mine, other, bias, labels, tasks, errors, stats):
    logits = mine[...] + other[...] + bias[0:1, :]
    lane = lax.broadcasted_iota(jnp.int32, logits.shape, 1)
    err = jnp.where(lane < tasks, sigmoid(logits) - labels[...], 0.0)
    errors[...] = err
    gram = lax.dot_general(err, err, (((0,), (0,)), ((), ())), precision=HIGHEST, preferred_element_type=f32)
    stats[0:tasks, :] = gram[0:tasks, :]
    stats[tasks:, :] = jnp.broadcast_to(jnp.sum(err, axis=0, keepdims=True), (stats.shape[0] - tasks, L))


def head_weights(count, tasks, stats, errors, head_all, head_mine, pooled, dz, bias_grad, head_grad):
    inner = tn_dot(head_all[...], head_all[...])
    gram = stats[0:tasks, :] * inner[0:tasks, :] / count
    rest = jnp.zeros((L - tasks, L), f32)

    def advance(step, weights):
        full = jnp.concatenate([weights, rest], axis=0)
        score = -jnp.dot(gram, full, precision=HIGHEST, preferred_element_type=f32) / SOFTMAX_HEAT
        power = jnp.exp(score - jnp.max(score, axis=0, keepdims=True))
        corner = power / jnp.sum(power, axis=0, keepdims=True)
        rate = 2.0 / (step.astype(f32) + 2.0)
        return (1.0 - rate) * weights + rate * corner

    weights = lax.fori_loop(0, FW_STEPS, advance, jnp.full((tasks, L), 1.0 / tasks, f32))
    row = lax.broadcasted_iota(jnp.int32, (tasks, L), 0)
    lane = lax.broadcasted_iota(jnp.int32, (tasks, L), 1)
    weight_row = jnp.sum(jnp.where(row == lane, weights, 0.0), axis=0, keepdims=True)
    scaled = errors[...] * weight_row
    dz[...] = lax.dot_general(
        scaled,
        head_mine[...].astype(f32),
        (((1,), (1,)), ((), ())),
        precision=HIGHEST,
        preferred_element_type=f32,
    )
    bias_grad[...] = jnp.broadcast_to(weight_row * stats[tasks : tasks + 1, :], bias_grad.shape)
    grad = lax.dot_general(
        scaled,
        pooled[...].astype(bf16).astype(f32),
        (((0,), (0,)), ((), ())),
        precision=HIGHEST,
        preferred_element_type=f32,
    )
    head_grad[...] = grad[0:tasks, :]


def fourth_backward(
    nm, q_ref, dz, xh, inv, res, w, params, big_ref, o0, o1, o2, o3, dp, d_res, norm, ws, d, dy
):
    big = big_ref[...]
    im = big.shape[0]
    out_grad = dz[...] / (4.0 + 12.0 * big)
    for i in range(16):
        rows = slice(i * im, (i + 1) * im)
        v = blk(xh, i, im) * params[4:5, :] + params[9:10, :] + res[rows, :].astype(f32)
        sig = sigmoid(v)
        grad = masked(out_grad * (sig * (1.0 + v * (1.0 - sig))), i, big)
        dy[rows, :] = grad
        d_res[rows, :] = grad.astype(bf16)
    dgain, dbias = norm_backward(dy, xh, inv, params[4:5, :], big, nm, dp)
    norm[...] = jnp.concatenate([dgain, dbias, jnp.zeros((6, L), f32)], axis=0)
    conv_back_input(q_ref[0], dp, w, ws, d, (o0, o1, o2, o3), im)


def third_backward(
    nm, q_ref, g0, g1, g2, xh, inv, w, params, big_ref, o0, o1, o2, o3, dp, norm, ws, d, dy
):
    big = big_ref[...]
    im = big.shape[0]
    for i in range(16):
        rows = slice(i * im, (i + 1) * im)
        grad = g0[rows, :] + g1[rows, :].astype(f32) + g2[rows, :].astype(f32)
        grad = grad.astype(bf16).astype(f32)
        v = blk(xh, i, im) * params[3:4, :] + params[8:9, :]
        sig = sigmoid(v)
        dy[rows, :] = masked(grad * (sig * (1.0 + v * (1.0 - sig))), i, big)
    dgain, dbias = norm_backward(dy, xh, inv, params[3:4, :], big, nm, dp)
    norm[...] = jnp.concatenate([dgain, dbias, jnp.zeros((6, L), f32)], axis=0)
    conv_back_input(q_ref[0], dp, w, ws, d, (o0, o1, o2, o3), im)


def second_backward(
    nm, q_ref, g0, g1, g2, d_res, v_in, xh, inv, w, params, big_ref, o0, o1, o2, o3, dp, ds, norm, ws, d, dy
):
    big = big_ref[...]
    im = big.shape[0]
    for i in range(16):
        rows = slice(i * im, (i + 1) * im)
        grad = g0[rows, :] + g1[rows, :].astype(f32) + g2[rows, :].astype(f32)
        grad = grad + d_res[rows, :].astype(f32)
        v = v_in[rows, :]
        sig = sigmoid(v)
        grad = masked(grad * (sig * (1.0 + v * (1.0 - sig))), i, big).astype(bf16)
        ds[rows, :] = grad
        dy[rows, :] = grad.astype(f32)
    dgain, dbias = norm_backward(dy, xh, inv, params[2:3, :], big, nm, dp)
    norm[...] = jnp.concatenate([dgain, dbias, jnp.zeros((6, L), f32)], axis=0)
    conv_back_input(q_ref[0], dp, w, ws, d, (o0, o1, o2, o3), im)


def spread_first(dp1, dps, d, im, rows_at):
    for i in range(16):
        r, c = i // 4, i % 4
        at = rows_at + i * im
        for n, t in enumerate(FIRST_COLS):
            if t < 0:
                value = blk(dps, i, im)
            else:
                ro = r + 1 if t // 3 == 0 else r
                co = c + 1 if t % 3 == 0 else c
                value = blk(dp1, ro * 4 + co, im) if ro < 4 and co < 4 else jnp.zeros((im, L), bf16)
            d[at : at + im, n * L : (n + 1) * L] = value


def first_backward(
    nm, c_ref, g0, g1, g2, ds, xh1, inv1, xh2, inv2, w, w_short, params, big_ref,
    keep, give, dp1, dps, norm, ws, d, dy,
):
    big = big_ref[...]
    im = big.shape[0]
    half = c_ref[0]
    cin = 2 * L
    for i in range(16):
        rows = slice(i * im, (i + 1) * im)
        grad = g0[rows, :] + g1[rows, :].astype(f32) + g2[rows, :].astype(f32)
        grad = grad.astype(bf16).astype(f32)
        v = blk(xh1, i, im) * params[0:1, :] + params[5:6, :]
        sig = sigmoid(v)
        dy[rows, :] = masked(grad * (sig * (1.0 + v * (1.0 - sig))), i, big)
    gain1, bias1 = norm_backward(dy, xh1, inv1, params[0:1, :], big, nm, dp1)
    for i in range(16):
        rows = slice(i * im, (i + 1) * im)
        dy[rows, :] = masked(ds[rows, :].astype(f32), i, big)
    gain2, bias2 = norm_backward(dy, xh2, inv2, params[1:2, :], big, nm, dps)
    norm[...] = jnp.concatenate([gain1, bias1, gain2, bias2, jnp.zeros((4, L), f32)], axis=0)
    for n, t in enumerate(FIRST_COLS):
        for j in range(2):
            if t < 0:
                src = w_short[pl.ds(pl.multiple_of((half ^ j) * L, L), L), :]
            else:
                src = w[pl.ds(pl.multiple_of(t * cin + (half ^ j) * L, L), L), :]
            ws[j * L : (j + 1) * L, n * L : (n + 1) * L] = src
    spread_first(dp1, dps, d, im, 0)
    col = 0
    for k, taps in enumerate(PLANE_TAPS):
        cols = slice(col * L, (col + len(taps)) * L)
        dx = nt_dot(d[:, cols], ws[:, cols]).astype(bf16)
        rows = slice(k * 16 * im, (k + 1) * 16 * im)
        keep[rows, :] = dx[:, :L]
        give[rows, :] = dx[:, L:]
        col += len(taps)


def weight_grad(chunks, q_ref, *refs):
    x_refs = refs[: 4 * chunks]
    dp_refs = refs[4 * chunks : 5 * chunks]
    out, xs, d = refs[5 * chunks :]
    q = q_ref[0]
    rows = dp_refs[0].shape[0]
    im = rows // 16
    for k in range(chunks):
        for j in range(4):
            xs[k * rows : (k + 1) * rows, j * L : (j + 1) * L] = x_refs[4 * k + j][...]
        spread_taps(dp_refs[k], d, im, k * rows, True)
    for n in range(3):
        cols = slice(n * 3 * L, (n + 1) * 3 * L)
        grad = tn_dot(xs[...], d[:, cols]).astype(bf16)
        for t in range(3):
            for j in range(4):
                start = pl.multiple_of((3 * n + t) * 4 * L + (q ^ j) * L, L)
                out[pl.ds(start, L), :] = grad[j * L : (j + 1) * L, t * L : (t + 1) * L]


def first_weight_grad(chunks, *refs):
    x_refs = refs[:chunks]
    dp1_refs = refs[chunks : 2 * chunks]
    dps_refs = refs[2 * chunks : 3 * chunks]
    out, out_short, d = refs[3 * chunks :]
    rows = dp1_refs[0].shape[0]
    im = rows // 16
    cin = 2 * L
    for k in range(chunks):
        spread_first(dp1_refs[k], dps_refs[k], d, im, k * rows)
    col = 0
    for k, taps in enumerate(PLANE_TAPS):
        cols = slice(col * L, (col + len(taps)) * L)
        grad = None
        for m in range(chunks):
            x = x_refs[m][k * rows : (k + 1) * rows, :]
            term = tn_dot(x, d[m * rows : (m + 1) * rows, cols])
            grad = term if grad is None else grad + term
        grad = grad.astype(bf16)
        for n, t in enumerate(taps):
            value = grad[:, n * L : (n + 1) * L]
            if t < 0:
                out_short[...] = value
            else:
                out[t * cin : (t + 1) * cin, :] = value
        col += len(taps)


def flip(value, axis):
    return lax.ppermute(value, axis, [(i, i ^ 1) for i in range(lax.axis_size(axis))])


def swap_ac(value):
    return lax.ppermute(value, ("a", "c"), [(2 * i + j, 2 * j + i) for i in range(2) for j in range(2)])


def sum_over(value, axis):
    count = lax.axis_size(axis)
    if count & (count - 1):
        return lax.psum(value, axis)
    step = 1
    while step < count:
        value = value + lax.ppermute(value, axis, [(i, i ^ step) for i in range(count)])
        step *= 2
    return value


def gather_quarters(h):
    from_b = flip(h, "b")
    from_c = flip(h, "c")
    return (h, from_c, from_b, flip(from_b, "c"))


def scatter_quarters(parts):
    p0, p1, p2, p3 = parts
    first = flip(p1, "c")
    second = flip(p3, "c")
    across = flip((p2 + second.astype(f32)).astype(bf16), "b")
    return (p0, first, across)


def body(
    features, buckets, micro_order, labels, conv_first, conv_short, conv_second, conv_third, conv_fourth,
    norm_gains, norm_biases, head_weight, head_bias,
):
    ia, ib, iz, ic = (lax.axis_index(n) for n in ("a", "b", "z", "c"))
    n_group = lax.axis_size("z") * lax.axis_size("c")
    images, grid, _, cin = features.shape
    channels = conv_second.shape[1]
    tasks = head_weight.shape[1]
    quarter = 2 * ib + ic
    shared = 2 * ib + ia
    im = images // CHUNKS
    nm = MICRO // CHUNKS
    rows = 16 * im
    q_arr = quarter[None].astype(jnp.int32)
    c_arr = ic[None].astype(jnp.int32)

    block = channels // n_group
    r_first, r_short = conv_first.shape[0], conv_short.shape[0]

    def pad16(a):
        short = -a.shape[0] % 16
        return jnp.pad(a, ((0, short), (0, 2 * L - a.shape[1])))

    halves = lax.dynamic_slice_in_dim(
        jnp.concatenate([conv_first, conv_short], axis=0), ib * 2 * L, 2 * L, 1
    )
    small = [pad16(norm_gains), pad16(norm_biases), pad16(head_weight)]
    packed = jnp.concatenate([halves] + small, axis=0)
    packed = lax.all_gather(packed, ("z", "c"), axis=0)
    rest = [
        lax.dynamic_slice_in_dim(w, shared * L, L, 1) for w in (conv_second, conv_third, conv_fourth)
    ]
    rest = lax.optimization_barrier((packed, *rest))
    packed, rest = rest[0], rest[1:]
    w_second, w_third, w_fourth = [
        swap_ac(lax.all_gather(w, ("z", "c"), axis=0, tiled=True)) for w in rest
    ]
    mine = lax.dynamic_slice_in_dim(packed[:, : r_first + r_short], ic * L, L, 2)
    w_first = mine[:, :r_first].reshape(n_group * r_first, L)
    w_short = mine[:, r_first:].reshape(n_group * r_short, L)
    at = r_first + r_short
    gains = packed[:, at : at + 5, :block].transpose(1, 0, 2).reshape(5, channels)
    at += 16
    biases = packed[:, at : at + 5, :block].transpose(1, 0, 2).reshape(5, channels)
    at += 16
    head_all = packed[:, at : at + block, :L].reshape(channels, L)
    head_mine = lax.dynamic_slice_in_dim(head_all, quarter * L, L, 0)
    params = jnp.concatenate([gains, biases, jnp.zeros((6, channels), bf16)], axis=0)
    params = lax.dynamic_slice_in_dim(params, quarter * L, L, 1).astype(f32)
    bias_row = jnp.broadcast_to(
        jnp.pad(head_bias.astype(f32), (0, L - tasks))[None, :], (8, L)
    )

    own = ia == ic
    ints = jnp.concatenate(
        [labels, buckets[:, None], micro_order.reshape(images, 1), jnp.zeros((images, L - tasks - 2), jnp.int32)],
        axis=1,
    )
    ints = jnp.where(own, ints, flip(ints, "c"))
    order = ints[:, tasks + 1]
    ints = ints[order]
    label_rows = ints.astype(f32)
    big = jnp.broadcast_to(ints[:, tasks : tasks + 1].astype(f32), (images, L))
    feats = jnp.where(own, features, flip(features, "c"))[order]
    side = grid // 2 * (1 + ints[:, tasks])
    places = jnp.arange(grid, dtype=jnp.int32)
    valid = (places[None, :, None] < side[:, None, None]) & (places[None, None, :] < side[:, None, None])
    feats = jnp.where(valid[..., None], feats, jnp.zeros_like(feats))
    feats = feats.reshape(CHUNKS, im, grid // 2, 2, grid // 2, 2, cin).transpose(0, 3, 5, 2, 4, 1, 6)
    feats = feats.reshape(CHUNKS, 4 * rows, cin)

    act = sds(rows, L, dtype=bf16)
    full = sds(rows, L)
    img = sds(im, L)
    vm = pltpu.VMEM
    conv_scratch = [vm((rows, 4 * L), bf16), vm((4 * L, 9 * L), bf16), vm((rows, 9 * L), f32), vm((rows, L), f32)]
    back_scratch = [vm((4 * L, 9 * L), bf16), vm((rows, 9 * L), bf16), vm((rows, L), f32)]
    flops_conv = 2 * rows * 4 * L * 9 * L

    bigs = [big[k * im : (k + 1) * im] for k in range(CHUNKS)]
    xs = [feats[k] for k in range(CHUNKS)]
    every = range(CHUNKS)

    def run(kernel, outs, args, scratch, flops=flops_conv):
        return call(functools.partial(kernel, nm), outs, args, scratch, 1, flops)

    first = [
        run(
            first_forward,
            [act, act, full, img, full, img],
            (c_arr, xs[k], w_first, w_short, params, bigs[k]),
            [vm((cin, 10 * L), bf16), vm((rows, 10 * L), f32), vm((rows, L), f32), vm((rows, L), f32)],
        )
        for k in every
    ]
    h1 = [gather_quarters(first[k][0]) for k in every]
    second = [
        run(
            second_forward,
            [act, full, full, img],
            (q_arr, *h1[k], w_second, params, bigs[k], first[k][1]),
            conv_scratch,
        )
        for k in every
    ]
    x2 = [gather_quarters(second[k][0]) for k in every]
    third = [
        run(third_forward, [act, full, img], (q_arr, *x2[k], w_third, params, bigs[k]), conv_scratch)
        for k in every
    ]
    h3 = [gather_quarters(third[k][0]) for k in every]
    fourth = [
        run(
            fourth_forward,
            [img, img, full, img],
            (q_arr, *h3[k], w_fourth, params, bigs[k], second[k][0], head_mine),
            conv_scratch,
        )
        for k in every
    ]
    pooled = jnp.concatenate([fourth[k][0] for k in every], axis=0)
    logits = jnp.concatenate([fourth[k][1] for k in every], axis=0)

    logits = logits + flip(logits, "c")
    stat_rows = tasks + 8
    errors, stats = call(
        lambda mine, other, bias, lab, err, st: head_errors(mine, other, bias, lab, tasks, err, st),
        [sds(images, L), sds(stat_rows, L)],
        (logits, flip(logits, "b"), bias_row, label_rows),
        scalars=0,
    )
    stats = sum_over(sum_over(stats, "a"), "z")
    dz, bias_grad, head_grad = call(
        functools.partial(head_weights, float(images * n_group), tasks),
        [sds(images, L), sds(8, L), sds(tasks, L)],
        (stats, errors, head_all, head_mine, pooled),
        scalars=0,
    )

    quads = [full, act, full, act]
    b4 = [
        run(
            fourth_backward,
            [*quads, act, act, sds(8, L)],
            (q_arr, dz[k * im : (k + 1) * im], fourth[k][2], fourth[k][3], second[k][0], w_fourth, params, bigs[k]),
            back_scratch,
        )
        for k in every
    ]
    g3 = [scatter_quarters(b4[k][:4]) for k in every]

    def grad_of(acts, grads):
        args = [q_arr] + [a for quad in acts for a in quad] + list(grads)
        return call(
            functools.partial(weight_grad, CHUNKS),
            [sds(9 * channels, L, dtype=bf16)],
            args,
            [vm((CHUNKS * rows, 4 * L), bf16), vm((CHUNKS * rows, 9 * L), bf16)],
            1,
            flops_conv * CHUNKS,
        )[0]

    dw4 = grad_of(h3, [b4[k][4] for k in every])
    b3 = [
        run(
            third_backward,
            [*quads, act, sds(8, L)],
            (q_arr, *g3[k], third[k][1], third[k][2], w_third, params, bigs[k]),
            back_scratch,
        )
        for k in every
    ]
    g2 = [scatter_quarters(b3[k][:4]) for k in every]
    dw3 = grad_of(x2, [b3[k][4] for k in every])
    b2 = [
        run(
            second_backward,
            [*quads, act, act, sds(8, L)],
            (q_arr, *g2[k], b4[k][5], second[k][1], second[k][2], second[k][3], w_second, params, bigs[k]),
            back_scratch,
        )
        for k in every
    ]
    g1 = [scatter_quarters(b2[k][:4]) for k in every]
    dw2 = grad_of(h1, [b2[k][4] for k in every])
    half = sds(4 * rows, L, dtype=bf16)
    b1 = [
        run(
            first_backward,
            [half, half, act, act, sds(8, L)],
            (c_arr, *g1[k], b2[k][5], *first[k][2:], w_first, w_short, params, bigs[k]),
            [vm((cin, 10 * L), bf16), vm((rows, 10 * L), bf16), vm((rows, L), f32)],
        )
        for k in every
    ]
    dw1, dws = call(
        functools.partial(first_weight_grad, CHUNKS),
        [sds(9 * cin, L, dtype=bf16), sds(cin, L, dtype=bf16)],
        [xs[k] for k in every] + [b1[k][2] for k in every] + [b1[k][3] for k in every],
        [vm((CHUNKS * rows, 10 * L), bf16)],
        0,
        flops_conv * CHUNKS,
    )

    pieces = []
    wide = cin // 4
    for k in every:
        keep, give = b1[k][0], b1[k][1]
        part = keep.astype(f32) + flip(give, "c").astype(f32)
        mine_part = lax.dynamic_slice_in_dim(part, ib * wide, wide, 1)
        send = lax.dynamic_slice_in_dim(part, (1 - ib) * wide, wide, 1).astype(bf16)
        send = jnp.concatenate([send[: 2 * rows], send[2 * rows :]], axis=1)
        got = flip(send, "b")
        got = jnp.concatenate([got[:, :wide], got[:, wide:]], axis=0)
        total = (mine_part + got.astype(f32)).astype(bf16)
        total = jnp.concatenate([total[: 2 * rows], total[2 * rows :]], axis=1)
        total = swap_ac(total)
        total = jnp.concatenate([total[:, :wide], total[:, wide:]], axis=0)
        pieces.append(total.reshape(2, 2, grid // 2, grid // 2, im, wide))
    grad = jnp.stack(pieces)
    grad = grad.transpose(0, 5, 3, 1, 4, 2, 6).reshape(images, grid, grid, wide)
    spots = jnp.arange(images, dtype=jnp.int32)
    inverse = jnp.sum(
        jnp.where(micro_order[0][None, :] == spots[:, None], spots[None, :], 0), axis=1
    )
    input_grad = grad[inverse].astype(f32)

    moved = lax.ppermute(
        pooled,
        ("a", "b", "c"),
        [(4 * i + 2 * j + k, 4 * j + 2 * k + i) for i in range(2) for j in range(2) for k in range(2)],
    )
    pooled_out = moved[inverse]

    def reduced(grad, per_group):
        grad = swap_ac(grad)
        return lax.psum_scatter(grad, ("z", "c"), scatter_dimension=0, tiled=True)

    def columns(shard):
        shard = shard.astype(bf16)
        parts = [shard, flip(shard, "a")]
        parts += [flip(p, "b") for p in parts]
        out = jnp.zeros((shard.shape[0], channels), f32)
        for j, part in enumerate(parts):
            out = lax.dynamic_update_slice_in_dim(out, part.astype(f32), (shared ^ j) * L, 1)
        return out

    conv_fourth_grad = columns(reduced(dw4, 9 * channels // n_group))
    conv_third_grad = columns(reduced(dw3, 9 * channels // n_group))
    conv_second_grad = columns(reduced(dw2, 9 * channels // n_group))
    slot = jnp.concatenate([dw1.reshape(n_group, r_first, L), dws.reshape(n_group, r_short, L)], axis=1)
    slot = reduced(slot.reshape(-1, L), r_first + r_short)
    slot = columns(slot)
    conv_first_grad = slot[:r_first]
    conv_short_grad = slot[r_first:]

    norm = [sum(b[k][-1] for k in every) for b in (b1, b2, b3, b4)]
    small = jnp.concatenate([head_grad] + norm, axis=0)
    small = sum_over(sum_over(small, "a"), "z")
    quads_small = gather_quarters(small)
    wide_small = jnp.zeros((small.shape[0], channels), f32)
    for j, part in enumerate(quads_small):
        wide_small = lax.dynamic_update_slice_in_dim(wide_small, part, (quarter ^ j) * L, 1)
    group = 2 * iz + ic
    own_small = lax.dynamic_slice_in_dim(wide_small, group * block, block, 1)
    head_weight_grad = own_small[:tasks].T
    n1, n2, n3, n4 = (own_small[tasks + 8 * i : tasks + 8 * (i + 1)] for i in range(4))
    gains_grad = jnp.stack([n1[0], n1[2], n2[0], n3[0], n4[0]])
    biases_grad = jnp.stack([n1[1], n1[3], n2[1], n3[1], n4[1]])
    return (
        pooled_out,
        input_grad,
        conv_first_grad,
        conv_short_grad,
        conv_second_grad,
        conv_third_grad,
        conv_fourth_grad,
        gains_grad,
        biases_grad,
        head_weight_grad,
        bias_grad[0, :tasks],
    )


def solution(mesh):
    sections, groups = mesh.shape["section"], mesh.shape["dp"]
    fine = Mesh(mesh.devices.reshape(2, sections // 2, groups // 2, 2), ("a", "b", "z", "c"))
    dp, section = ("z", "c"), ("a", "b")
    return jax.shard_map(
        body,
        mesh=fine,
        in_specs=(
            P(dp, None, None, None),
            P(dp),
            P(dp, None),
            P(dp, None),
            P(dp, None),
            P(dp, None),
            P(dp, None),
            P(dp, None),
            P(dp, None),
            P(None, dp),
            P(None, dp),
            P(dp, None),
            P(),
        ),
        out_specs=(
            P(dp, section),
            P(dp, None, None, section),
            P(dp, None),
            P(dp, None),
            P(dp, None),
            P(dp, None),
            P(dp, None),
            P(None, dp),
            P(None, dp),
            P(dp, None),
            P(),
        ),
        check_vma=False,
    )
```

```python
import functools

import jax
import jax.numpy as jnp
from jax import lax
from jax.experimental import pallas as pl
from jax.experimental.pallas import tpu as pltpu
from jax.sharding import Mesh, PartitionSpec as P

MICRO = 6
FW_STEPS = 20
EPSILON = 1e-05
SOFTMAX_HEAT = 0.01
HIGHEST = lax.Precision.HIGHEST
CHUNKS = 1

f32 = jnp.float32
bf16 = jnp.bfloat16
L = 128

PLANE_TAPS = ((4, -1), (3, 5), (1, 7), (0, 2, 6, 8))
FIRST_COLS = tuple(tap for taps in PLANE_TAPS for tap in taps)


def call(kernel, outs, args, scratch=(), scalars=1, flops=0, ties=()):
    specs = [pl.BlockSpec(memory_space=pltpu.SMEM)] * scalars
    specs += [pl.BlockSpec(memory_space=pltpu.VMEM)] * (len(args) - scalars)
    specs += [pl.BlockSpec(memory_space=pl.ANY)] * len(ties)
    size = sum(a.size * a.dtype.itemsize for a in args)
    size += sum(o.size * o.dtype.itemsize for o in outs)

    def run(*refs):
        kernel(*refs[: len(args)], *refs[len(args) + len(ties) :])

    return pl.pallas_call(
        run,
        out_shape=tuple(outs),
        in_specs=specs,
        out_specs=tuple(pl.BlockSpec(memory_space=pltpu.VMEM) for _ in outs),
        scratch_shapes=list(scratch),
        compiler_params=pltpu.CompilerParams(vmem_limit_bytes=56 << 20),
        cost_estimate=pl.CostEstimate(flops=int(flops), bytes_accessed=int(size), transcendentals=0),
    )(*args, *ties)


def sds(*shape, dtype=f32):
    return jax.ShapeDtypeStruct(shape, dtype)


def nt_dot(x, y):
    return lax.dot_general(x, y, (((1,), (1,)), ((), ())), preferred_element_type=f32)


def tn_dot(x, y):
    return lax.dot_general(x, y, (((0,), (0,)), ((), ())), preferred_element_type=f32)


def sigmoid(v):
    return 1.0 / (1.0 + jnp.exp(-v))


def pixel_mask(i, big):
    return None if (i // 4 < 2 and i % 4 < 2) else big


def masked(value, i, big):
    return value if pixel_mask(i, big) is None else value * big


def per_micro(value, nm):
    rows, lanes = value.shape
    return jnp.sum(value.reshape(nm, rows // nm, lanes), axis=1)


def spread_micro(value, im):
    nm, lanes = value.shape
    return jnp.broadcast_to(value[:, None, :], (nm, im // nm, lanes)).reshape(im, lanes)


def blk(ref, i, im):
    return ref[i * im : (i + 1) * im, :]


def norm_forward(p_ref, xhat_ref, inv_ref, big, nm):
    im = big.shape[0]
    total = per_micro(4.0 + 12.0 * big, nm)
    acc = jnp.zeros_like(big)
    for i in range(16):
        acc = acc + masked(blk(p_ref, i, im), i, big)
    mean = spread_micro(per_micro(acc, nm) / total, im)
    acc = jnp.zeros_like(big)
    for i in range(16):
        cen = blk(p_ref, i, im) - mean
        acc = acc + masked(cen * cen, i, big)
    inv = lax.rsqrt(per_micro(acc, nm) / total + EPSILON)
    inv = spread_micro(inv, im)
    inv_ref[...] = inv
    for i in range(16):
        xhat_ref[i * im : (i + 1) * im, :] = (blk(p_ref, i, im) - mean) * inv


def norm_backward(dy_ref, xhat_ref, inv_ref, gain, big, nm, out_ref):
    im = big.shape[0]
    total = per_micro(4.0 + 12.0 * big, nm)
    sum_dy = jnp.zeros_like(big)
    sum_dx = jnp.zeros_like(big)
    for i in range(16):
        dy = blk(dy_ref, i, im)
        sum_dy = sum_dy + dy
        sum_dx = sum_dx + dy * blk(xhat_ref, i, im)
    sum_dy = per_micro(sum_dy, nm)
    sum_dx = per_micro(sum_dx, nm)
    mean_dy = spread_micro(sum_dy / total, im)
    mean_dx = spread_micro(sum_dx / total, im)
    scale = inv_ref[...] * gain
    for i in range(16):
        off = masked(mean_dy + blk(xhat_ref, i, im) * mean_dx, i, big)
        grad = scale * (blk(dy_ref, i, im) - off)
        out_ref[i * im : (i + 1) * im, :] = grad.astype(bf16)
    return jnp.sum(sum_dx, axis=0, keepdims=True), jnp.sum(sum_dy, axis=0, keepdims=True)


def load_weights(q_ref, w_refs, ws):
    channels = 4 * L
    q = q_ref[0]

    def load(w_ref):
        for t in range(9):
            for j in range(4):
                start = pl.multiple_of(t * channels + (q ^ j) * L, L)
                ws[j * L : (j + 1) * L, t * L : (t + 1) * L] = w_ref[pl.ds(start, L), :]

    pl.when(q_ref[1] == 1)(lambda: load(w_refs[0]))
    pl.when(q_ref[1] == 0)(lambda: load(w_refs[1]))


def row_taps(r):
    return (3 * L if r == 3 else 0), (6 * L if r == 0 else 9 * L)


def conv_forward(q_ref, x_refs, w_refs, xs, ws, y, p, im):
    for j in range(4):
        xs[:, j * L : (j + 1) * L] = x_refs[j][...]
    load_weights(q_ref, w_refs, ws)
    for r in range(4):
        lo, hi = row_taps(r)
        rows = slice(r * 4 * im, (r + 1) * 4 * im)
        y[rows, lo:hi] = jnp.dot(xs[rows, :], ws[:, lo:hi], preferred_element_type=f32)
    for r in range(4):
        for c in range(4):
            acc = None
            for t in range(9):
                ri, ci = r + t // 3 - 1, c + t % 3 - 1
                if 0 <= ri < 4 and 0 <= ci < 4:
                    i = ri * 4 + ci
                    term = y[i * im : (i + 1) * im, t * L : (t + 1) * L]
                    acc = term if acc is None else acc + term
            p[(r * 4 + c) * im : (r * 4 + c + 1) * im, :] = acc


def spread_taps(dp_ref, d, im, rows_at, all_taps):
    for r in range(4):
        lo, hi = (0, 9 * L) if all_taps else row_taps(r)
        for c in range(4):
            at = rows_at + (r * 4 + c) * im
            for t in range(lo // L, hi // L):
                ro, co = r - t // 3 + 1, c - t % 3 + 1
                if 0 <= ro < 4 and 0 <= co < 4:
                    value = blk(dp_ref, ro * 4 + co, im)
                else:
                    value = jnp.zeros((im, L), bf16)
                d[at : at + im, t * L : (t + 1) * L] = value


def conv_back_input(q_ref, dp_ref, w_refs, ws, d, outs, im):
    load_weights(q_ref, w_refs, ws)
    spread_taps(dp_ref, d, im, 0, False)
    for r in range(4):
        lo, hi = row_taps(r)
        rows = slice(r * 4 * im, (r + 1) * 4 * im)
        dx = nt_dot(d[rows, lo:hi], ws[:, lo:hi])
        for j in range(4):
            outs[j][rows, :] = dx[:, j * L : (j + 1) * L].astype(outs[j].dtype)


def load_plane(x, k, big, xs, im):
    wide = jnp.concatenate([big, big], axis=1).astype(bf16)
    for i in range(16):
        pixel = (2 * (i // 4) + k // 2) * 8 + 2 * (i % 4) + k % 2
        xs[i * im : (i + 1) * im, :] = masked(blk(x, pixel, im), i, wide)


def first_forward(nm, c_ref, x, w, w_short, params, big_ref, h, s, xh1, inv1, xh2, inv2, xs, wsc, y, p1, p2):
    big = big_ref[...]
    im = big.shape[0]
    cin = 2 * L
    col = 0
    for k, taps in enumerate(PLANE_TAPS):
        for n, t in enumerate(taps):
            src = w_short[...] if t < 0 else w[t * cin : (t + 1) * cin, :]
            wsc[:, (col + n) * L : (col + n + 1) * L] = src
        cols = slice(col * L, (col + len(taps)) * L)
        load_plane(x, k, big, xs, im)
        y[:, cols] = jnp.dot(xs[...], wsc[:, cols], preferred_element_type=f32)
        col += len(taps)
    for r in range(4):
        for c in range(4):
            o = r * 4 + c
            acc = None
            for n, t in enumerate(FIRST_COLS):
                if t < 0:
                    p2[o * im : (o + 1) * im, :] = y[o * im : (o + 1) * im, n * L : (n + 1) * L]
                    continue
                ri = r - 1 if t // 3 == 0 else r
                ci = c - 1 if t % 3 == 0 else c
                if ri >= 0 and ci >= 0:
                    i = ri * 4 + ci
                    term = y[i * im : (i + 1) * im, n * L : (n + 1) * L]
                    acc = term if acc is None else acc + term
            p1[o * im : (o + 1) * im, :] = acc
    norm_forward(p1, xh1, inv1, big, nm)
    norm_forward(p2, xh2, inv2, big, nm)
    for i in range(16):
        rows = slice(i * im, (i + 1) * im)
        v = blk(xh1, i, im) * params[0:1, :] + params[5:6, :]
        h[rows, :] = masked(v * sigmoid(v), i, big).astype(bf16)
        v = blk(xh2, i, im) * params[1:2, :] + params[6:7, :]
        s[rows, :] = masked(v, i, big).astype(bf16)


def second_forward(nm, q_ref, x0, x1, x2, x3, w, w_swap, params, big_ref, s, out, v_out, xh, inv, xs, ws, y, p):
    big = big_ref[...]
    im = big.shape[0]
    conv_forward(q_ref, (x0, x1, x2, x3), (w, w_swap), xs, ws, y, p, im)
    norm_forward(p, xh, inv, big, nm)
    for i in range(16):
        rows = slice(i * im, (i + 1) * im)
        u = blk(xh, i, im) * params[2:3, :] + params[7:8, :]
        u = masked(u, i, big).astype(bf16).astype(f32)
        v = u + s[rows, :].astype(f32)
        v_out[rows, :] = v
        out[rows, :] = masked(v * sigmoid(v), i, big).astype(bf16)


def third_forward(nm, q_ref, x0, x1, x2, x3, w, w_swap, params, big_ref, out, xh, inv, xs, ws, y, p):
    big = big_ref[...]
    im = big.shape[0]
    conv_forward(q_ref, (x0, x1, x2, x3), (w, w_swap), xs, ws, y, p, im)
    norm_forward(p, xh, inv, big, nm)
    for i in range(16):
        rows = slice(i * im, (i + 1) * im)
        v = blk(xh, i, im) * params[3:4, :] + params[8:9, :]
        out[rows, :] = masked(v * sigmoid(v), i, big).astype(bf16)


def fourth_forward(
    nm, q_ref, x0, x1, x2, x3, w, w_swap, params, big_ref, res, head, pooled, logits, xh, inv, xs, ws, y, p
):
    big = big_ref[...]
    im = big.shape[0]
    conv_forward(q_ref, (x0, x1, x2, x3), (w, w_swap), xs, ws, y, p, im)
    norm_forward(p, xh, inv, big, nm)
    acc = jnp.zeros_like(big)
    for i in range(16):
        rows = slice(i * im, (i + 1) * im)
        v = blk(xh, i, im) * params[4:5, :] + params[9:10, :] + res[rows, :].astype(f32)
        acc = acc + masked(v * sigmoid(v), i, big)
    pool = acc / (4.0 + 12.0 * big)
    pooled[...] = pool
    logits[...] = jnp.dot(pool.astype(bf16), head[...], preferred_element_type=f32)


def head_errors(mine, other, bias, labels, tasks, errors, stats):
    logits = mine[...] + other[...] + bias[0:1, :]
    lane = lax.broadcasted_iota(jnp.int32, logits.shape, 1)
    err = jnp.where(lane < tasks, sigmoid(logits) - labels[...], 0.0)
    errors[...] = err
    gram = lax.dot_general(err, err, (((0,), (0,)), ((), ())), precision=HIGHEST, preferred_element_type=f32)
    stats[0:tasks, :] = gram[0:tasks, :]
    stats[tasks:, :] = jnp.broadcast_to(jnp.sum(err, axis=0, keepdims=True), (stats.shape[0] - tasks, L))


def head_weights(count, tasks, stats, errors, head_all, head_mine, pooled, dz, bias_grad, head_grad):
    inner = tn_dot(head_all[...], head_all[...])
    gram = stats[0:tasks, :] * inner[0:tasks, :] / count
    rest = jnp.zeros((L - tasks, L), f32)

    def advance(step, weights):
        full = jnp.concatenate([weights, rest], axis=0)
        score = -jnp.dot(gram, full, precision=HIGHEST, preferred_element_type=f32) / SOFTMAX_HEAT
        power = jnp.exp(score - jnp.max(score, axis=0, keepdims=True))
        corner = power / jnp.sum(power, axis=0, keepdims=True)
        rate = 2.0 / (step.astype(f32) + 2.0)
        return (1.0 - rate) * weights + rate * corner

    weights = lax.fori_loop(0, FW_STEPS, advance, jnp.full((tasks, L), 1.0 / tasks, f32))
    row = lax.broadcasted_iota(jnp.int32, (tasks, L), 0)
    lane = lax.broadcasted_iota(jnp.int32, (tasks, L), 1)
    weight_row = jnp.sum(jnp.where(row == lane, weights, 0.0), axis=0, keepdims=True)
    scaled = errors[...] * weight_row
    dz[...] = lax.dot_general(
        scaled,
        head_mine[...].astype(f32),
        (((1,), (1,)), ((), ())),
        precision=HIGHEST,
        preferred_element_type=f32,
    )
    bias_grad[...] = jnp.broadcast_to(weight_row * stats[tasks : tasks + 1, :], bias_grad.shape)
    grad = lax.dot_general(
        scaled,
        pooled[...].astype(bf16).astype(f32),
        (((0,), (0,)), ((), ())),
        precision=HIGHEST,
        preferred_element_type=f32,
    )
    head_grad[...] = grad[0:tasks, :]


def fourth_backward(
    nm, q_ref, dz, xh, inv, res, w, w_swap, params, big_ref, o0, o1, o2, o3, dp, d_res, norm, ws, d, dy
):
    big = big_ref[...]
    im = big.shape[0]
    out_grad = dz[...] / (4.0 + 12.0 * big)
    for i in range(16):
        rows = slice(i * im, (i + 1) * im)
        v = blk(xh, i, im) * params[4:5, :] + params[9:10, :] + res[rows, :].astype(f32)
        sig = sigmoid(v)
        grad = masked(out_grad * (sig * (1.0 + v * (1.0 - sig))), i, big)
        dy[rows, :] = grad
        d_res[rows, :] = grad.astype(bf16)
    dgain, dbias = norm_backward(dy, xh, inv, params[4:5, :], big, nm, dp)
    norm[...] = jnp.concatenate([dgain, dbias, jnp.zeros((6, L), f32)], axis=0)
    conv_back_input(q_ref, dp, (w, w_swap), ws, d, (o0, o1, o2, o3), im)


def third_backward(
    nm, q_ref, g0, g1, g2, xh, inv, w, w_swap, params, big_ref, o0, o1, o2, o3, dp, norm, ws, d, dy
):
    big = big_ref[...]
    im = big.shape[0]
    for i in range(16):
        rows = slice(i * im, (i + 1) * im)
        grad = g0[rows, :] + g1[rows, :].astype(f32) + g2[rows, :].astype(f32)
        grad = grad.astype(bf16).astype(f32)
        v = blk(xh, i, im) * params[3:4, :] + params[8:9, :]
        sig = sigmoid(v)
        dy[rows, :] = masked(grad * (sig * (1.0 + v * (1.0 - sig))), i, big)
    dgain, dbias = norm_backward(dy, xh, inv, params[3:4, :], big, nm, dp)
    norm[...] = jnp.concatenate([dgain, dbias, jnp.zeros((6, L), f32)], axis=0)
    conv_back_input(q_ref, dp, (w, w_swap), ws, d, (o0, o1, o2, o3), im)


def second_backward(
    nm, q_ref, g0, g1, g2, d_res, v_in, xh, inv, w, w_swap, params, big_ref, o0, o1, o2, o3, dp, ds, norm, ws, d, dy
):
    big = big_ref[...]
    im = big.shape[0]
    for i in range(16):
        rows = slice(i * im, (i + 1) * im)
        grad = g0[rows, :] + g1[rows, :].astype(f32) + g2[rows, :].astype(f32)
        grad = grad + d_res[rows, :].astype(f32)
        v = v_in[rows, :]
        sig = sigmoid(v)
        grad = masked(grad * (sig * (1.0 + v * (1.0 - sig))), i, big).astype(bf16)
        ds[rows, :] = grad
        dy[rows, :] = grad.astype(f32)
    dgain, dbias = norm_backward(dy, xh, inv, params[2:3, :], big, nm, dp)
    norm[...] = jnp.concatenate([dgain, dbias, jnp.zeros((6, L), f32)], axis=0)
    conv_back_input(q_ref, dp, (w, w_swap), ws, d, (o0, o1, o2, o3), im)


def spread_first(dp1, dps, d, im, rows_at):
    for i in range(16):
        r, c = i // 4, i % 4
        at = rows_at + i * im
        for n, t in enumerate(FIRST_COLS):
            if t < 0:
                value = blk(dps, i, im)
            else:
                ro = r + 1 if t // 3 == 0 else r
                co = c + 1 if t % 3 == 0 else c
                value = blk(dp1, ro * 4 + co, im) if ro < 4 and co < 4 else jnp.zeros((im, L), bf16)
            d[at : at + im, n * L : (n + 1) * L] = value


def first_backward(
    nm, c_ref, g0, g1, g2, ds, xh1, inv1, xh2, inv2, w, w_short, params, big_ref, *refs,
):
    outs, (dp1, dps, norm, ws, d, dy) = refs[:8], refs[8:]
    big = big_ref[...]
    im = big.shape[0]
    half, part = c_ref[0], c_ref[1]
    cin = 2 * L
    for i in range(16):
        rows = slice(i * im, (i + 1) * im)
        grad = g0[rows, :] + g1[rows, :].astype(f32) + g2[rows, :].astype(f32)
        grad = grad.astype(bf16).astype(f32)
        v = blk(xh1, i, im) * params[0:1, :] + params[5:6, :]
        sig = sigmoid(v)
        dy[rows, :] = masked(grad * (sig * (1.0 + v * (1.0 - sig))), i, big)
    gain1, bias1 = norm_backward(dy, xh1, inv1, params[0:1, :], big, nm, dp1)
    for i in range(16):
        rows = slice(i * im, (i + 1) * im)
        dy[rows, :] = masked(ds[rows, :].astype(f32), i, big)
    gain2, bias2 = norm_backward(dy, xh2, inv2, params[1:2, :], big, nm, dps)
    norm[...] = jnp.concatenate([gain1, bias1, gain2, bias2, jnp.zeros((4, L), f32)], axis=0)
    wide = cin // 4
    for n, t in enumerate(FIRST_COLS):
        for j in range(4):
            start = (half ^ (j & 1)) * 2 * wide + (part ^ (j >> 1)) * wide
            if t < 0:
                src = w_short[pl.ds(pl.multiple_of(start, wide), wide), :]
            else:
                src = w[pl.ds(pl.multiple_of(t * cin + start, wide), wide), :]
            ws[j * wide : (j + 1) * wide, n * L : (n + 1) * L] = src
    spread_first(dp1, dps, d, im, 0)
    col = 0
    for k, taps in enumerate(PLANE_TAPS):
        cols = slice(col * L, (col + len(taps)) * L)
        dx = nt_dot(d[:, cols], ws[:, cols])
        pair, side = k // 2, k % 2
        for j in range(4):
            ref = outs[4 * pair + j]
            ref[:, side * wide : (side + 1) * wide] = dx[:, j * wide : (j + 1) * wide].astype(ref.dtype)
        col += len(taps)


def weight_grad(chunks, q_ref, *refs):
    x_refs = refs[: 4 * chunks]
    dp_refs = refs[4 * chunks : 5 * chunks]
    out, xs, d = refs[5 * chunks :]
    q = q_ref[0]
    rows = dp_refs[0].shape[0]
    im = rows // 16
    for k in range(chunks):
        for j in range(4):
            xs[k * rows : (k + 1) * rows, j * L : (j + 1) * L] = x_refs[4 * k + j][...]
        spread_taps(dp_refs[k], d, im, k * rows, True)
    for n in range(3):
        cols = slice(n * 3 * L, (n + 1) * 3 * L)
        grad = tn_dot(xs[...], d[:, cols]).astype(bf16)
        for t in range(3):
            for j in range(4):
                start = pl.multiple_of((3 * n + t) * 4 * L + (q ^ j) * L, L)
                out[pl.ds(start, L), :] = grad[j * L : (j + 1) * L, t * L : (t + 1) * L]


def first_weight_grad(chunks, *refs):
    x_refs = refs[:chunks]
    dp1_refs = refs[chunks : 2 * chunks]
    dps_refs = refs[2 * chunks : 3 * chunks]
    big_refs = refs[3 * chunks : 4 * chunks]
    out, out_short, xs, d = refs[4 * chunks :]
    rows = dp1_refs[0].shape[0]
    im = rows // 16
    cin = 2 * L
    for k in range(chunks):
        spread_first(dp1_refs[k], dps_refs[k], d, im, k * rows)
    col = 0
    for k, taps in enumerate(PLANE_TAPS):
        cols = slice(col * L, (col + len(taps)) * L)
        grad = None
        for m in range(chunks):
            load_plane(x_refs[m], k, big_refs[m][...], xs, im)
            term = tn_dot(xs[...], d[m * rows : (m + 1) * rows, cols])
            grad = term if grad is None else grad + term
        grad = grad.astype(bf16)
        for n, t in enumerate(taps):
            value = grad[:, n * L : (n + 1) * L]
            if t < 0:
                out_short[...] = value
            else:
                out[t * cin : (t + 1) * cin, :] = value
        col += len(taps)


def flip(value, axis):
    return lax.ppermute(value, axis, [(i, i ^ 1) for i in range(lax.axis_size(axis))])


def swap_ac(value):
    return lax.ppermute(value, ("a", "c"), [(1, 2), (2, 1)])


def sum_over(value, axis):
    count = lax.axis_size(axis)
    if count & (count - 1):
        return lax.psum(value, axis)
    step = 1
    while step < count:
        value = value + lax.ppermute(value, axis, [(i, i ^ step) for i in range(count)])
        step *= 2
    return value


def gather_quarters(h):
    from_b = flip(h, "b")
    from_c = flip(h, "c")
    return (h, from_c, from_b, flip(from_b, "c"))


def scatter_quarters(parts):
    p0, p1, p2, p3 = parts
    first = flip(p1, "c")
    second = flip(p3, "c")
    send = (p2 + second.astype(f32)).astype(bf16)
    return (p0, first, flip(send, "b"), send)


def pack(q_ref, first, short, norms, heads, second, third, fourth, mine, give, *rest):
    q, shared = q_ref[0], q_ref[1]
    n1, n2 = first.shape[0], short.shape[0]
    for out, part in ((mine, q), (give, q ^ 1)):
        cols = pl.ds(pl.multiple_of(part * L, L), L)
        out[0:n1, :] = first[:, cols]
        out[n1 : n1 + n2, :] = short[:, cols]
        out[n1 + n2 :, :] = heads[...]
        out[n1 + n2 : n1 + n2 + norms.shape[0], L - norms.shape[1] :] = norms[...]
    cols = pl.ds(pl.multiple_of(shared * L, L), L)
    for out, src in zip(rest, (second, third, fourth)):
        out[...] = src[:, cols]


def unpack(n1, n2, block, k_ref, *refs):
    pieces, (first, short, params, heads) = refs[:8], refs[8:]
    here, q = k_ref[0], k_ref[1]
    for k, piece in enumerate(pieces):
        at = here ^ k
        first[pl.ds(pl.multiple_of(at * n1, 32), n1), :] = piece[0:n1, :]
        short[pl.ds(pl.multiple_of(at * n2, 32), n2), :] = piece[n1 : n1 + n2, :]
        head = piece[n1 + n2 : n1 + n2 + block, :]
        lane = lax.broadcasted_iota(jnp.int32, head.shape, 1)
        heads[pl.ds(pl.multiple_of(at * block, 32), block), :] = jnp.where(
            lane < L - block, head, jnp.zeros_like(head)
        )
        for side in range(L // block):
            @pl.when(at == q * (L // block) + side)
            def _():
                value = piece[n1 + n2 : n1 + n2 + 16, L - block :].astype(f32)
                params[:, side * block : (side + 1) * block] = value


def assemble(q_ref, p0, p1, p2, p3, *outs):
    q = q_ref[0]
    for j, part in enumerate((p0, p1, p2, p3)):
        cols = pl.ds(pl.multiple_of((q ^ j) * L, L), L)
        at = 0
        for out in outs:
            out[:, cols] = part[at : at + out.shape[0], :].astype(f32)
            at += out.shape[0]


def input_grad_kernel(order_ref, big_ref, *refs):
    pairs, out = refs[:-1], refs[-1]
    images = order_ref.shape[1]
    im = pairs[0].shape[0] // 16
    chunks = len(pairs) // 2
    wide = out.shape[1]
    spot = lax.broadcasted_iota(jnp.int32, (images, images), 1)
    pick = jnp.where(spot == jnp.transpose(jnp.broadcast_to(order_ref[0:1, :], (images, images))), 1.0, 0.0)
    pick = pick.astype(bf16)
    big = big_ref[0:1, :]
    for pr in range(2):
        for i in range(16):
            rows = [blk(pairs[2 * k + pr], i, im) for k in range(chunks)]
            rows = rows[0] if chunks == 1 else jnp.concatenate(rows, axis=0)
            value = masked(tn_dot(rows, pick), i, big)
            for pc in range(2):
                pixel = (2 * (i // 4) + pr) * 8 + 2 * (i % 4) + pc
                out[pixel, :, :] = value[pc * wide : (pc + 1) * wide, :]


def body(
    features, buckets, micro_order, labels, conv_first, conv_short, conv_second, conv_third, conv_fourth,
    norm_gains, norm_biases, head_weight, head_bias,
):
    ia, ib, iz, ic = (lax.axis_index(n) for n in ("a", "b", "z", "c"))
    n_group = lax.axis_size("z") * lax.axis_size("c")
    images, grid, _, cin = features.shape
    channels = conv_second.shape[1]
    tasks = head_weight.shape[1]
    quarter = 2 * ib + ic
    shared = 2 * ib + ia
    im = images // CHUNKS
    nm = MICRO // CHUNKS
    rows = 16 * im
    own = ia == ic
    q_arr = jnp.stack([quarter, own]).astype(jnp.int32)
    c_arr = jnp.stack([ic, ib]).astype(jnp.int32)

    block = channels // n_group
    r_first, r_short = conv_first.shape[0], conv_short.shape[0]
    n_z = lax.axis_size("z")

    small_rows = max(16, block)
    norms = jnp.concatenate([norm_gains, norm_biases], axis=0)
    norms = jnp.pad(norms, ((0, 6), (0, 0)))
    heads = jnp.pad(head_weight, ((0, small_rows - block), (0, L - tasks)))
    slot_rows = r_first + r_short + small_rows
    piece_t = sds(slot_rows, L, dtype=bf16)
    quarter_t = sds(conv_second.shape[0], L, dtype=bf16)
    mine, give, *rest = call(
        pack,
        [piece_t, piece_t] + [quarter_t] * 3,
        (
            jnp.stack([quarter, shared]).astype(jnp.int32),
            conv_first, conv_short, norms, heads, conv_second, conv_third, conv_fourth,
        ),
    )
    rest = [lax.all_gather(w, ("z", "c"), axis=0, tiled=True) for w in rest]
    w_second, w_third, w_fourth = [(w, swap_ac(w)) for w in rest]

    piece = jnp.where(own, mine, flip(give, "c"))

    order = jnp.where(piece[-1, -1] == 0, micro_order[0], 0)
    ints = jnp.concatenate(
        [labels, buckets[:, None], jnp.zeros((images, L - tasks - 1), jnp.int32)], axis=1
    )[order]
    feats = features[order].reshape(CHUNKS, im, grid * grid, cin).transpose(0, 2, 1, 3)
    feats = feats.reshape(CHUNKS, 4 * rows, cin)
    feats = jnp.where(own, feats, flip(feats, "c"))

    if n_z == 4:
        parts = [piece] + [
            lax.ppermute(piece, "z", [(i, i ^ m) for i in range(n_z)]) for m in range(1, n_z)
        ]
        parts = [x for p in parts for x in (p, flip(p, "a"))]
        w_first, w_short, params, head_all = call(
            functools.partial(unpack, r_first, r_short, block),
            [
                sds(n_group * r_first, L, dtype=bf16),
                sds(n_group * r_short, L, dtype=bf16),
                sds(16, L),
                sds(channels, L, dtype=bf16),
            ],
            (jnp.stack([2 * iz + ia, quarter]).astype(jnp.int32), *parts),
            ties=(feats,),
        )
    else:
        packed = lax.all_gather(piece, ("z", "a"), axis=0)
        w_first = packed[:, :r_first].reshape(n_group * r_first, L)
        w_short = packed[:, r_first : r_first + r_short].reshape(n_group * r_short, L)
        small = packed[:, r_first + r_short :]
        head_all = small[:, :block].reshape(channels, L)
        lane = lax.broadcasted_iota(jnp.int32, head_all.shape, 1)
        head_all = jnp.where(lane < tasks, head_all, jnp.zeros_like(head_all))
        params = small[:, :16, L - block :].transpose(1, 0, 2).reshape(16, channels)
        params = lax.dynamic_slice_in_dim(params, quarter * L, L, 1).astype(f32)
    head_mine = lax.dynamic_slice_in_dim(head_all, quarter * L, L, 0)
    bias_row = jnp.broadcast_to(
        jnp.pad(head_bias.astype(f32), (0, L - tasks))[None, :], (8, L)
    )

    own_big = jnp.broadcast_to(buckets[None, :].astype(f32), (8, images))
    ints = jnp.where(own, ints, flip(ints, "c"))
    label_rows = ints.astype(f32)
    big = jnp.broadcast_to(ints[:, tasks : tasks + 1].astype(f32), (images, L))

    act = sds(rows, L, dtype=bf16)
    full = sds(rows, L)
    img = sds(im, L)
    vm = pltpu.VMEM
    conv_scratch = [vm((rows, 4 * L), bf16), vm((4 * L, 9 * L), bf16), vm((rows, 9 * L), f32), vm((rows, L), f32)]
    back_scratch = [vm((4 * L, 9 * L), bf16), vm((rows, 9 * L), bf16), vm((rows, L), f32)]
    flops_conv = 2 * rows * 4 * L * 9 * L

    bigs = [big[k * im : (k + 1) * im] for k in range(CHUNKS)]
    xs = [feats[k] for k in range(CHUNKS)]
    every = range(CHUNKS)

    def run(kernel, outs, args, scratch, flops=flops_conv, ties=()):
        return call(functools.partial(kernel, nm), outs, args, scratch, 1, flops, ties)

    first = [
        run(
            first_forward,
            [act, act, full, img, full, img],
            (c_arr, xs[k], w_first, w_short, params, bigs[k]),
            [vm((rows, cin), bf16), vm((cin, 10 * L), bf16), vm((rows, 10 * L), f32), vm((rows, L), f32), vm((rows, L), f32)],
        )
        for k in every
    ]
    h1 = [gather_quarters(first[k][0]) for k in every]
    second = [
        run(
            second_forward,
            [act, full, full, img],
            (q_arr, *h1[k], *w_second, params, bigs[k], first[k][1]),
            conv_scratch,
        )
        for k in every
    ]
    x2 = [gather_quarters(second[k][0]) for k in every]
    third = [
        run(third_forward, [act, full, img], (q_arr, *x2[k], *w_third, params, bigs[k]), conv_scratch)
        for k in every
    ]
    h3 = [gather_quarters(third[k][0]) for k in every]
    fourth = [
        run(
            fourth_forward,
            [img, img, full, img],
            (q_arr, *h3[k], *w_fourth, params, bigs[k], second[k][0], head_mine),
            conv_scratch,
        )
        for k in every
    ]
    pooled = jnp.concatenate([fourth[k][0] for k in every], axis=0)
    logits = jnp.concatenate([fourth[k][1] for k in every], axis=0)

    logits = logits + flip(logits, "c")
    stat_rows = tasks + 8
    errors, stats = call(
        lambda mine, other, bias, lab, err, st: head_errors(mine, other, bias, lab, tasks, err, st),
        [sds(images, L), sds(stat_rows, L)],
        (logits, flip(logits, "b"), bias_row, label_rows),
        scalars=0,
    )
    stats = sum_over(sum_over(stats, "a"), "z")
    dz, bias_grad, head_grad = call(
        functools.partial(head_weights, float(images * n_group), tasks),
        [sds(images, L), sds(8, L), sds(tasks, L)],
        (stats, errors, head_all, head_mine, pooled),
        scalars=0,
    )

    quads = [full, act, full, act]

    def grad_of(acts, grads, ties):
        args = [q_arr] + [a for quad in acts for a in quad] + list(grads)
        return call(
            functools.partial(weight_grad, CHUNKS),
            [sds(9 * channels, L, dtype=bf16)],
            args,
            [vm((CHUNKS * rows, 4 * L), bf16), vm((CHUNKS * rows, 9 * L), bf16)],
            1,
            flops_conv * CHUNKS,
            ties,
        )[0]

    def summand(grad, got, norm):
        return jnp.where(own & (norm[-1, -1] == 0), grad, got)

    def reduced(grad):
        return lax.psum_scatter(grad, ("z", "c"), scatter_dimension=0, tiled=True)

    def from_sections(shard):
        shard = shard.astype(bf16)
        both = lax.ppermute(shard, ("a", "b"), [(i, i ^ 3) for i in range(4)])
        return (shard, flip(shard, "a"), flip(shard, "b"), both)

    def row_halves(blocks):
        blocks = blocks.reshape(n_z, 2, -1, L)
        return tuple(lax.dynamic_index_in_dim(blocks, k, 1, keepdims=False) for k in (ia, 1 - ia))

    def sum_z(mine, got):
        total = mine.astype(f32) + got.astype(f32)
        if n_z != 4:
            return lax.psum_scatter(total, "z", scatter_dimension=0)
        low = total.astype(bf16)
        shard = lax.dynamic_index_in_dim(total, iz, 0, keepdims=False)
        parts = [
            lax.ppermute(
                lax.dynamic_index_in_dim(low, iz ^ m, 0, keepdims=False),
                "z",
                [(i, i ^ m) for i in range(n_z)],
            )
            for m in range(1, n_z)
        ]
        return (shard, *parts)

    def added(parts):
        return sum(p.astype(f32) for p in parts).astype(bf16) if isinstance(parts, tuple) else parts.astype(bf16)

    def to_places(shard):
        parts = []
        for m in range(4):
            pairs = [
                (4 * i + 2 * j + k, 4 * (k ^ (m & 1)) + 2 * (j ^ (m >> 1)) + i)
                for i in range(2)
                for j in range(2)
                for k in range(2)
            ]
            parts.append(lax.ppermute(shard, ("a", "b", "c"), pairs))
        return parts

    shared_arr = shared[None].astype(jnp.int32)

    b4 = [
        run(
            fourth_backward,
            [*quads, act, act, sds(8, L)],
            (q_arr, dz[k * im : (k + 1) * im], fourth[k][2], fourth[k][3], second[k][0], *w_fourth, params, bigs[k]),
            back_scratch,
        )
        for k in every
    ]
    g3 = [scatter_quarters(b4[k][:4]) for k in every]
    dw4 = grad_of(h3, [b4[k][4] for k in every], [g3[k][3] for k in every])
    s4 = swap_ac(dw4)
    b3 = [
        run(
            third_backward,
            [*quads, act, sds(8, L)],
            (q_arr, *g3[k][:3], third[k][1], third[k][2], *w_third, params, bigs[k]),
            back_scratch,
            ties=(dw4,),
        )
        for k in every
    ]
    g2 = [scatter_quarters(b3[k][:4]) for k in every]
    d4 = summand(dw4, s4, b3[-1][-1])
    r4 = reduced(d4)
    dw3 = grad_of(x2, [b3[k][4] for k in every], [g2[k][3] for k in every] + [d4])
    s3 = swap_ac(dw3)
    b2 = [
        run(
            second_backward,
            [*quads, act, act, sds(8, L)],
            (q_arr, *g2[k][:3], b4[k][5], second[k][1], second[k][2], second[k][3], *w_second, params, bigs[k]),
            back_scratch,
            ties=(dw3,),
        )
        for k in every
    ]
    g1 = [scatter_quarters(b2[k][:4]) for k in every]
    d3 = summand(dw3, s3, b2[-1][-1])
    r3 = reduced(d3)
    dw2 = grad_of(h1, [b2[k][4] for k in every], [g1[k][3] for k in every] + [d3])
    dw2 = dw2.reshape(n_group, -1, L)
    keep2, give2 = row_halves(dw2)
    got2 = flip(give2, "a")
    b1 = [
        run(
            first_backward,
            [*quads, *quads, act, act, sds(8, L)],
            (c_arr, *g1[k][:3], b2[k][5], *first[k][2:], w_first, w_short, params, bigs[k]),
            [vm((cin, 10 * L), bf16), vm((rows, 10 * L), bf16), vm((rows, L), f32)],
            ties=(give2,),
        )
        for k in every
    ]
    sums = [[scatter_quarters(b1[k][4 * pair : 4 * pair + 4]) for pair in range(2)] for k in every]
    tied = [sums[k][pair][3] for pair in range(2) for k in every]
    dw1, dws = call(
        functools.partial(first_weight_grad, CHUNKS),
        [sds(9 * cin, L, dtype=bf16), sds(cin, L, dtype=bf16)],
        [xs[k] for k in every] + [b1[k][8] for k in every] + [b1[k][9] for k in every] + bigs,
        [vm((rows, cin), bf16), vm((CHUNKS * rows, 10 * L), bf16)],
        0,
        flops_conv * CHUNKS,
        tied,
    )

    norm = [sum(b[k][-1] for k in every) for b in (b1, b2, b3, b4)]
    small = jnp.concatenate([head_grad] + norm, axis=0).astype(bf16)
    pad = -small.shape[0] % 16
    small = jnp.pad(small, ((0, pad), (0, 0)))
    slot = jnp.concatenate(
        [
            dw1.reshape(n_group, r_first, L),
            dws.reshape(n_group, r_short, L),
            jnp.broadcast_to(small[None], (n_group, *small.shape)),
        ],
        axis=1,
    )
    keep1, give1 = row_halves(slot)
    got1 = flip(give1, "a")
    parts2 = sum_z(keep2, got2)
    f4 = from_sections(r4)
    parts1 = sum_z(keep1, got1)
    places2 = to_places(added(parts2))
    places1 = to_places(added(parts1))
    f3 = from_sections(r3)

    outs = []
    for parts in (f4, f3, places2):
        outs += call(assemble, [sds(9 * channels // n_group, channels)], (shared_arr, *parts))
    conv_fourth_grad, conv_third_grad, conv_second_grad = outs
    conv_first_grad, conv_short_grad, wide_small = call(
        assemble,
        [sds(r_first, channels), sds(r_short, channels), sds(small.shape[0], channels)],
        (shared_arr, *places1),
    )

    pairs = []
    for k in every:
        for p0, p1, p2, _ in sums[k]:
            total = (p0 + p1.astype(f32) + p2.astype(f32)).astype(bf16)
            pairs.append(jnp.where(own, total, swap_ac(total)))
    input_grad = call(
        input_grad_kernel,
        [sds(grid * grid, cin // 4, images)],
        (micro_order, own_big, *pairs),
        scalars=0,
    )[0].reshape(grid, grid, cin // 4, images).transpose(3, 0, 1, 2)

    moved = lax.ppermute(
        pooled,
        ("a", "b", "c"),
        [(4 * i + 2 * j + k, 4 * j + 2 * k + i) for i in range(2) for j in range(2) for k in range(2)],
    )
    spots = jnp.arange(images, dtype=jnp.int32)
    inverse = jnp.sum(
        jnp.where(micro_order[0][None, :] == spots[:, None], spots[None, :], 0), axis=1
    )
    pooled_out = moved[inverse]

    group = 2 * iz + ic
    own_small = lax.dynamic_slice_in_dim(wide_small, group * block, block, 1)
    head_weight_grad = own_small[:tasks].T
    n1, n2, n3, n4 = (own_small[tasks + 8 * i : tasks + 8 * (i + 1)] for i in range(4))
    gains_grad = jnp.stack([n1[0], n1[2], n2[0], n3[0], n4[0]])
    biases_grad = jnp.stack([n1[1], n1[3], n2[1], n3[1], n4[1]])
    return (
        pooled_out,
        input_grad,
        conv_first_grad,
        conv_short_grad,
        conv_second_grad,
        conv_third_grad,
        conv_fourth_grad,
        gains_grad,
        biases_grad,
        head_weight_grad,
        bias_grad[0, :tasks],
    )


def solution(mesh):
    sections, groups = mesh.shape["section"], mesh.shape["dp"]
    fine = Mesh(mesh.devices.reshape(2, sections // 2, groups // 2, 2), ("a", "b", "z", "c"))
    dp, section = ("z", "c"), ("a", "b")
    return jax.shard_map(
        body,
        mesh=fine,
        in_specs=(
            P(dp, None, None, None),
            P(dp),
            P(dp, None),
            P(dp, None),
            P(dp, None),
            P(dp, None),
            P(dp, None),
            P(dp, None),
            P(dp, None),
            P(None, dp),
            P(None, dp),
            P(dp, None),
            P(),
        ),
        out_specs=(
            P(dp, section),
            P(dp, None, None, section),
            P(dp, None),
            P(dp, None),
            P(dp, None),
            P(dp, None),
            P(dp, None),
            P(None, dp),
            P(None, dp),
            P(dp, None),
            P(),
        ),
        check_vma=False,
    )
```

```python
import functools

import jax
import jax.numpy as jnp
from jax import lax
from jax.experimental import pallas as pl
from jax.experimental.pallas import tpu as pltpu
from jax.sharding import Mesh, PartitionSpec as P

MICRO = 6
FW_STEPS = 20
EPSILON = 1e-05
SOFTMAX_HEAT = 0.01
HIGHEST = lax.Precision.HIGHEST

f32 = jnp.float32
bf16 = jnp.bfloat16
L = 128

PLANE_TAPS = ((4, -1), (3, 5), (1, 7), (0, 2, 6, 8))
FIRST_COLS = tuple(tap for taps in PLANE_TAPS for tap in taps)


VMEM_MB = 52


class Keep:
    def __init__(self, *shape, dtype=f32):
        self.shape, self.dtype = shape, dtype


class Pick:
    def __init__(self, first, other):
        self.first, self.other = first, other
        self.shape, self.dtype, self.size = first.shape, first.dtype, first.size


class Buf:
    def __init__(self, ref, start, wait, out=False):
        self.ref, self.start, self.wait = ref, start, wait
        self.out, self.started, self.ready = out, not out, out
        self.shape, self.dtype = ref.shape, ref.dtype
        if not out:
            start()

    def get(self):
        if not self.ready:
            self.wait()
            self.ready = True

    def __getitem__(self, at):
        self.get()
        return self.ref[at]

    def __setitem__(self, at, value):
        self.ref[at] = value

    def send(self):
        if not self.started:
            self.start()
            self.started = True


def call(kernel, outs, args, scratch=(), scalars=1, flops=0, ties=(), through=()):
    def far(a):
        return isinstance(a, (Pick, Keep))

    flat, specs, places = [], [], []
    for k, a in enumerate(args):
        places.append(len(flat))
        if k < scalars:
            space = pltpu.SMEM
        else:
            space = pltpu.HBM if far(a) else pltpu.VMEM
        for x in (a.first, a.other) if isinstance(a, Pick) else (a,):
            flat.append(x)
            specs.append(pl.BlockSpec(memory_space=space))
    n_args = len(flat)
    specs += [pl.BlockSpec(memory_space=pl.ANY)] * (len(ties) + len(through))
    far_in = [k for k, a in enumerate(args) if k >= scalars and far(a)]
    far_out = [k for k, o in enumerate(outs) if far(o)]
    buffers = [pltpu.VMEM(args[k].shape, args[k].dtype) for k in far_in]
    buffers += [pltpu.VMEM(outs[k].shape, outs[k].dtype) for k in far_out]
    n_in = n_args + len(ties) + len(through)
    n_outs = len(outs)
    n_bufs = len(buffers)

    def run(*refs):
        ins, results = list(refs[:n_args]), list(refs[n_in : n_in + n_outs])
        rest = refs[n_in + n_outs + len(through) :]
        temps, sems, rest = rest[:n_bufs], rest[n_bufs], rest[n_bufs + 1 :]
        given = []
        for k in range(len(args)):
            src = ins[places[k]]
            if k in far_in:
                n = far_in.index(k)
                copy = pltpu.make_async_copy(src, temps[n], sems.at[n])
                start = copy.start
                if isinstance(args[k], Pick):
                    second = pltpu.make_async_copy(ins[places[k] + 1], temps[n], sems.at[n])

                    def start(copy=copy, second=second):
                        pl.when(ins[0][1] == 1)(copy.start)
                        pl.when(ins[0][1] == 0)(second.start)

                src = Buf(temps[n], start, copy.wait)
            given.append(src)
        made = []
        for k in range(n_outs):
            out = results[k]
            if k in far_out:
                n = len(far_in) + far_out.index(k)
                copy = pltpu.make_async_copy(temps[n], out, sems.at[n])
                out = Buf(temps[n], copy.start, copy.wait, out=True)
            made.append(out)
        kernel(*given, *made, *rest)
        for x in given:
            if isinstance(x, Buf):
                x.get()
        made = [x for x in made if isinstance(x, Buf)]
        for x in made:
            x.send()
        for x in made:
            x.wait()

    outs = [sds(*o.shape, dtype=o.dtype) if far(o) else o for o in outs]
    size = sum(a.size * a.dtype.itemsize for a in flat) + sum(o.size * o.dtype.itemsize for o in outs)
    return pl.pallas_call(
        run,
        out_shape=tuple(outs) + tuple(sds(*x.shape, dtype=x.dtype) for x in through),
        in_specs=specs,
        out_specs=tuple(
            pl.BlockSpec(memory_space=pltpu.HBM if k in far_out else pltpu.VMEM) for k in range(n_outs)
        )
        + tuple(pl.BlockSpec(memory_space=pl.ANY) for _ in through),
        scratch_shapes=buffers + [pltpu.SemaphoreType.DMA((max(n_bufs, 1),))] + list(scratch),
        input_output_aliases={n_args + len(ties) + k: n_outs + k for k in range(len(through))},
        compiler_params=pltpu.CompilerParams(vmem_limit_bytes=VMEM_MB << 20),
        cost_estimate=pl.CostEstimate(flops=int(flops), bytes_accessed=int(size), transcendentals=0),
    )(*flat, *ties, *through)


def sds(*shape, dtype=f32):
    return jax.ShapeDtypeStruct(shape, dtype)


def nt_dot(x, y):
    return lax.dot_general(x, y, (((1,), (1,)), ((), ())), preferred_element_type=f32)


def tn_dot(x, y):
    return lax.dot_general(x, y, (((0,), (0,)), ((), ())), preferred_element_type=f32)


def sigmoid(v):
    return 0.5 + 0.5 * jnp.tanh(0.5 * v)


def pixel_mask(i, big):
    return None if (i // 4 < 2 and i % 4 < 2) else big


def masked(value, i, big):
    return value if pixel_mask(i, big) is None else value * big


def per_micro(value, nm):
    rows, lanes = value.shape
    return jnp.sum(value.reshape(nm, rows // nm, lanes), axis=1)


def spread_micro(value, im):
    nm, lanes = value.shape
    return jnp.broadcast_to(value[:, None, :], (nm, im // nm, lanes)).reshape(im, lanes)


def blk(ref, i, im):
    return ref[i * im : (i + 1) * im, :]


def norm_forward(p_ref, xhat_ref, inv_ref, big, nm):
    im = big.shape[0]
    total = per_micro(4.0 + 12.0 * big, nm)
    acc = jnp.zeros_like(big)
    for i in range(16):
        acc = acc + masked(blk(p_ref, i, im), i, big)
    mean = spread_micro(per_micro(acc, nm) / total, im)
    acc = jnp.zeros_like(big)
    for i in range(16):
        cen = blk(p_ref, i, im) - mean
        acc = acc + masked(cen * cen, i, big)
    inv = lax.rsqrt(per_micro(acc, nm) / total + EPSILON)
    inv_ref[...] = jnp.concatenate([inv, jnp.zeros((8 - nm, inv.shape[1]), f32)], axis=0)
    inv = spread_micro(inv, im)
    for i in range(16):
        xhat_ref[i * im : (i + 1) * im, :] = (blk(p_ref, i, im) - mean) * inv


def norm_backward(dy_ref, xhat_ref, inv_ref, gain, big, nm, out_ref):
    im = big.shape[0]
    total = per_micro(4.0 + 12.0 * big, nm)
    sum_dy = jnp.zeros_like(big)
    sum_dx = jnp.zeros_like(big)
    for i in range(16):
        dy = blk(dy_ref, i, im)
        sum_dy = sum_dy + dy
        sum_dx = sum_dx + dy * blk(xhat_ref, i, im)
    sum_dy = per_micro(sum_dy, nm)
    sum_dx = per_micro(sum_dx, nm)
    mean_dy = spread_micro(sum_dy / total, im)
    mean_dx = spread_micro(sum_dx / total, im)
    scale = spread_micro(inv_ref[0:nm, :] * gain, im)
    for i in range(16):
        off = masked(mean_dy + blk(xhat_ref, i, im) * mean_dx, i, big)
        grad = scale * (blk(dy_ref, i, im) - off)
        out_ref[i * im : (i + 1) * im, :] = grad.astype(bf16)
    return jnp.sum(sum_dx, axis=0, keepdims=True), jnp.sum(sum_dy, axis=0, keepdims=True)


def load_weights(q_ref, w_ref, ws):
    channels = 4 * L
    q = q_ref[0]
    for t in range(9):
        for j in range(4):
            start = pl.multiple_of(t * channels + (q ^ j) * L, L)
            ws[j * L : (j + 1) * L, t * L : (t + 1) * L] = w_ref[pl.ds(start, L), :]


def row_taps(r):
    return (3 * L if r == 3 else 0), (6 * L if r == 0 else 9 * L)


def conv_forward(q_ref, x_refs, w_ref, xs, ws, y, p, im):
    for j in range(4):
        xs[:, j * L : (j + 1) * L] = x_refs[j][...]
    xs.send()
    load_weights(q_ref, w_ref, ws)
    for r in range(4):
        lo, hi = row_taps(r)
        rows = slice(r * 4 * im, (r + 1) * 4 * im)
        y[rows, lo:hi] = jnp.dot(xs[rows, :], ws[:, lo:hi], preferred_element_type=f32)
    for r in range(4):
        for c in range(4):
            acc = None
            for t in range(9):
                ri, ci = r + t // 3 - 1, c + t % 3 - 1
                if 0 <= ri < 4 and 0 <= ci < 4:
                    i = ri * 4 + ci
                    term = y[i * im : (i + 1) * im, t * L : (t + 1) * L]
                    acc = term if acc is None else acc + term
            p[(r * 4 + c) * im : (r * 4 + c + 1) * im, :] = acc


def spread_taps(dp_ref, d, im, rows_at, all_taps):
    for r in range(4):
        lo, hi = (0, 9 * L) if all_taps else row_taps(r)
        for c in range(4):
            at = rows_at + (r * 4 + c) * im
            for t in range(lo // L, hi // L):
                ro, co = r - t // 3 + 1, c - t % 3 + 1
                if 0 <= ro < 4 and 0 <= co < 4:
                    value = blk(dp_ref, ro * 4 + co, im)
                else:
                    value = jnp.zeros((im, L), bf16)
                d[at : at + im, t * L : (t + 1) * L] = value


def conv_back_input(q_ref, dp_ref, w_ref, ws, d, outs, im):
    load_weights(q_ref, w_ref, ws)
    spread_taps(dp_ref, d, im, 0, False)
    for r in range(4):
        lo, hi = row_taps(r)
        rows = slice(r * 4 * im, (r + 1) * 4 * im)
        dx = nt_dot(d[rows, lo:hi], ws[:, lo:hi])
        for j in range(4):
            outs[j][rows, :] = dx[:, j * L : (j + 1) * L].astype(outs[j].dtype)


def load_plane(x, k, big, xs, im):
    wide = jnp.concatenate([big, big], axis=1).astype(bf16)
    for i in range(16):
        pixel = (2 * (i // 4) + k // 2) * 8 + 2 * (i % 4) + k % 2
        xs[i * im : (i + 1) * im, :] = masked(blk(x, pixel, im), i, wide)


def first_forward(nm, c_ref, x, w, w_short, params, big_ref, h, s, xh1, inv1, xh2, inv2, xs, wsc, y, p1, p2):
    big = big_ref[...]
    im = big.shape[0]
    cin = 2 * L
    col = 0
    for k, taps in enumerate(PLANE_TAPS):
        for n, t in enumerate(taps):
            src = w_short[...] if t < 0 else w[t * cin : (t + 1) * cin, :]
            wsc[:, (col + n) * L : (col + n + 1) * L] = src
        cols = slice(col * L, (col + len(taps)) * L)
        load_plane(x, k, big, xs, im)
        y[:, cols] = jnp.dot(xs[...], wsc[:, cols], preferred_element_type=f32)
        col += len(taps)
    for r in range(4):
        for c in range(4):
            o = r * 4 + c
            acc = None
            for n, t in enumerate(FIRST_COLS):
                if t < 0:
                    p2[o * im : (o + 1) * im, :] = y[o * im : (o + 1) * im, n * L : (n + 1) * L]
                    continue
                ri = r - 1 if t // 3 == 0 else r
                ci = c - 1 if t % 3 == 0 else c
                if ri >= 0 and ci >= 0:
                    i = ri * 4 + ci
                    term = y[i * im : (i + 1) * im, n * L : (n + 1) * L]
                    acc = term if acc is None else acc + term
            p1[o * im : (o + 1) * im, :] = acc
    norm_forward(p1, xh1, inv1, big, nm)
    norm_forward(p2, xh2, inv2, big, nm)
    for i in range(16):
        rows = slice(i * im, (i + 1) * im)
        v = blk(xh1, i, im) * params[0:1, :] + params[5:6, :]
        h[rows, :] = masked(v * sigmoid(v), i, big).astype(bf16)
        v = blk(xh2, i, im) * params[1:2, :] + params[6:7, :]
        s[rows, :] = masked(v, i, big).astype(bf16)


def second_forward(nm, q_ref, x0, x1, x2, x3, w, params, big_ref, s, out, xh, inv, xs, ws, y, p):
    big = big_ref[...]
    im = big.shape[0]
    conv_forward(q_ref, (x0, x1, x2, x3), w, xs, ws, y, p, im)
    norm_forward(p, xh, inv, big, nm)
    for i in range(16):
        rows = slice(i * im, (i + 1) * im)
        u = blk(xh, i, im) * params[2:3, :] + params[7:8, :]
        u = masked(u, i, big).astype(bf16).astype(f32)
        v = u + s[rows, :].astype(f32)
        out[rows, :] = masked(v * sigmoid(v), i, big).astype(bf16)


def third_forward(nm, q_ref, x0, x1, x2, x3, w, params, big_ref, out, xh, inv, xs, ws, y, p):
    big = big_ref[...]
    im = big.shape[0]
    conv_forward(q_ref, (x0, x1, x2, x3), w, xs, ws, y, p, im)
    norm_forward(p, xh, inv, big, nm)
    for i in range(16):
        rows = slice(i * im, (i + 1) * im)
        v = blk(xh, i, im) * params[3:4, :] + params[8:9, :]
        out[rows, :] = masked(v * sigmoid(v), i, big).astype(bf16)


def fourth_forward(
    nm, q_ref, x0, x1, x2, x3, w, params, big_ref, res, head, pooled, logits, xh, inv, xs, ws, y, p
):
    big = big_ref[...]
    im = big.shape[0]
    conv_forward(q_ref, (x0, x1, x2, x3), w, xs, ws, y, p, im)
    norm_forward(p, xh, inv, big, nm)
    acc = jnp.zeros_like(big)
    for i in range(16):
        rows = slice(i * im, (i + 1) * im)
        v = blk(xh, i, im) * params[4:5, :] + params[9:10, :] + res[rows, :].astype(f32)
        acc = acc + masked(v * sigmoid(v), i, big)
    pool = acc / (4.0 + 12.0 * big)
    pooled[...] = pool
    logits[...] = jnp.dot(pool.astype(bf16), head[...], preferred_element_type=f32)


def head_errors(mine, other, bias, labels, tasks, errors, stats):
    logits = mine[...] + other[...] + bias[0:1, :]
    lane = lax.broadcasted_iota(jnp.int32, logits.shape, 1)
    err = jnp.where(lane < tasks, sigmoid(logits) - labels[...], 0.0)
    errors[...] = err
    gram = lax.dot_general(err, err, (((0,), (0,)), ((), ())), precision=HIGHEST, preferred_element_type=f32)
    stats[0:tasks, :] = gram[0:tasks, :]
    stats[tasks:, :] = jnp.broadcast_to(jnp.sum(err, axis=0, keepdims=True), (stats.shape[0] - tasks, L))


def head_weights(count, tasks, stats, errors, head_all, head_mine, pooled, dz, bias_grad, head_grad):
    inner = tn_dot(head_all[...], head_all[...])
    gram = stats[0:tasks, :] * inner[0:tasks, :] / count
    rest = jnp.zeros((L - tasks, L), f32)

    def advance(step, weights):
        full = jnp.concatenate([weights, rest], axis=0)
        score = -jnp.dot(gram, full, precision=HIGHEST, preferred_element_type=f32) / SOFTMAX_HEAT
        power = jnp.exp(score - jnp.max(score, axis=0, keepdims=True))
        corner = power / jnp.sum(power, axis=0, keepdims=True)
        rate = 2.0 / (step.astype(f32) + 2.0)
        return (1.0 - rate) * weights + rate * corner

    weights = lax.fori_loop(0, FW_STEPS, advance, jnp.full((tasks, L), 1.0 / tasks, f32))
    row = lax.broadcasted_iota(jnp.int32, (tasks, L), 0)
    lane = lax.broadcasted_iota(jnp.int32, (tasks, L), 1)
    weight_row = jnp.sum(jnp.where(row == lane, weights, 0.0), axis=0, keepdims=True)
    scaled = errors[...] * weight_row
    dz[...] = lax.dot_general(
        scaled,
        head_mine[...].astype(f32),
        (((1,), (1,)), ((), ())),
        precision=HIGHEST,
        preferred_element_type=f32,
    )
    bias_grad[...] = jnp.broadcast_to(weight_row * stats[tasks : tasks + 1, :], bias_grad.shape)
    grad = lax.dot_general(
        scaled,
        pooled[...].astype(bf16).astype(f32),
        (((0,), (0,)), ((), ())),
        precision=HIGHEST,
        preferred_element_type=f32,
    )
    head_grad[...] = grad[0:tasks, :]


def fourth_backward(
    nm, q_ref, dz, xh, inv, res, w, params, big_ref, o0, o1, o2, o3, dp, d_res, norm, ws, d, dy
):
    big = big_ref[...]
    im = big.shape[0]
    out_grad = dz[...] / (4.0 + 12.0 * big)
    for i in range(16):
        rows = slice(i * im, (i + 1) * im)
        v = blk(xh, i, im) * params[4:5, :] + params[9:10, :] + res[rows, :].astype(f32)
        sig = sigmoid(v)
        grad = masked(out_grad * (sig * (1.0 + v * (1.0 - sig))), i, big)
        dy[rows, :] = grad
        d_res[rows, :] = grad.astype(bf16)
    dgain, dbias = norm_backward(dy, xh, inv, params[4:5, :], big, nm, dp)
    norm[...] = jnp.concatenate([dgain, dbias, jnp.zeros((6, L), f32)], axis=0)
    conv_back_input(q_ref, dp, w, ws, d, (o0, o1, o2, o3), im)


def third_backward(
    nm, q_ref, g0, g1, g2, xh, inv, w, params, big_ref, o0, o1, o2, o3, dp, norm, ws, d, dy
):
    big = big_ref[...]
    im = big.shape[0]
    for i in range(16):
        rows = slice(i * im, (i + 1) * im)
        grad = g0[rows, :] + g1[rows, :].astype(f32) + g2[rows, :].astype(f32)
        grad = grad.astype(bf16).astype(f32)
        v = blk(xh, i, im) * params[3:4, :] + params[8:9, :]
        sig = sigmoid(v)
        dy[rows, :] = masked(grad * (sig * (1.0 + v * (1.0 - sig))), i, big)
    dgain, dbias = norm_backward(dy, xh, inv, params[3:4, :], big, nm, dp)
    norm[...] = jnp.concatenate([dgain, dbias, jnp.zeros((6, L), f32)], axis=0)
    conv_back_input(q_ref, dp, w, ws, d, (o0, o1, o2, o3), im)


def second_backward(
    nm, q_ref, g0, g1, g2, d_res, s, xh, inv, w, params, big_ref, o0, o1, o2, o3, dp, ds, norm, ws, d, dy
):
    big = big_ref[...]
    im = big.shape[0]
    for i in range(16):
        rows = slice(i * im, (i + 1) * im)
        grad = g0[rows, :] + g1[rows, :].astype(f32) + g2[rows, :].astype(f32)
        grad = grad + d_res[rows, :].astype(f32)
        u = blk(xh, i, im) * params[2:3, :] + params[7:8, :]
        v = masked(u, i, big).astype(bf16).astype(f32) + s[rows, :].astype(f32)
        sig = sigmoid(v)
        grad = masked(grad * (sig * (1.0 + v * (1.0 - sig))), i, big).astype(bf16)
        ds[rows, :] = grad
        dy[rows, :] = grad.astype(f32)
    dgain, dbias = norm_backward(dy, xh, inv, params[2:3, :], big, nm, dp)
    norm[...] = jnp.concatenate([dgain, dbias, jnp.zeros((6, L), f32)], axis=0)
    conv_back_input(q_ref, dp, w, ws, d, (o0, o1, o2, o3), im)


def spread_first(dp1, dps, d, im, rows_at):
    for i in range(16):
        r, c = i // 4, i % 4
        at = rows_at + i * im
        for n, t in enumerate(FIRST_COLS):
            if t < 0:
                value = blk(dps, i, im)
            else:
                ro = r + 1 if t // 3 == 0 else r
                co = c + 1 if t % 3 == 0 else c
                value = blk(dp1, ro * 4 + co, im) if ro < 4 and co < 4 else jnp.zeros((im, L), bf16)
            d[at : at + im, n * L : (n + 1) * L] = value


def first_backward(
    nm, c_ref, g0, g1, g2, ds, xh1, inv1, xh2, inv2, w, w_short, params, big_ref, *refs,
):
    outs, (dp1, dps, norm, ws, d, dy) = refs[:4], refs[4:]
    big = big_ref[...]
    im = big.shape[0]
    half, part = c_ref[0], c_ref[1]
    cin = 2 * L
    for i in range(16):
        rows = slice(i * im, (i + 1) * im)
        grad = g0[rows, :] + g1[rows, :].astype(f32) + g2[rows, :].astype(f32)
        grad = grad.astype(bf16).astype(f32)
        v = blk(xh1, i, im) * params[0:1, :] + params[5:6, :]
        sig = sigmoid(v)
        dy[rows, :] = masked(grad * (sig * (1.0 + v * (1.0 - sig))), i, big)
    gain1, bias1 = norm_backward(dy, xh1, inv1, params[0:1, :], big, nm, dp1)
    for i in range(16):
        rows = slice(i * im, (i + 1) * im)
        dy[rows, :] = masked(ds[rows, :].astype(f32), i, big)
    gain2, bias2 = norm_backward(dy, xh2, inv2, params[1:2, :], big, nm, dps)
    norm[...] = jnp.concatenate([gain1, bias1, gain2, bias2, jnp.zeros((4, L), f32)], axis=0)
    wide = cin // 4
    for n, t in enumerate(FIRST_COLS):
        for j in range(4):
            start = (half ^ (j & 1)) * 2 * wide + (part ^ (j >> 1)) * wide
            if t < 0:
                src = w_short[pl.ds(pl.multiple_of(start, wide), wide), :]
            else:
                src = w[pl.ds(pl.multiple_of(t * cin + start, wide), wide), :]
            ws[j * wide : (j + 1) * wide, n * L : (n + 1) * L] = src
    spread_first(dp1, dps, d, im, 0)
    col = 0
    for k, taps in enumerate(PLANE_TAPS):
        cols = slice(col * L, (col + len(taps)) * L)
        dx = nt_dot(d[:, cols], ws[:, cols])
        pair, side = k // 2, k % 2
        rows = slice(pair * 16 * im, (pair + 1) * 16 * im)
        for j, ref in enumerate(outs):
            ref[rows, side * wide : (side + 1) * wide] = dx[:, j * wide : (j + 1) * wide].astype(ref.dtype)
        col += len(taps)


def weight_grad(block, q_ref, x, dp, out, d):
    im = dp.shape[0] // 16
    q, a = q_ref[0], q_ref[2]
    total = out.shape[0]
    spread_taps(dp, d, im, 0, True)
    step = L // 2 if block else L
    for n in range(3):
        cols = slice(n * 3 * L, (n + 1) * 3 * L)
        grad = tn_dot(x[...], d[:, cols]).astype(bf16)
        for t in range(3):
            for j in range(4):
                for part in range(L // step):
                    start = (3 * n + t) * 4 * L + (q ^ j) * L + part * step
                    if block:
                        at = start // block
                        start = ((at & 1) ^ a) * (total // 2) + (at // 2) * block + start % block
                    start = pl.multiple_of(start, step)
                    value = grad[j * L + part * step : j * L + (part + 1) * step, t * L : (t + 1) * L]
                    out[pl.ds(start, step), :] = value


def first_weight_grad(blocks, q_ref, x, dp1, dps, big_ref, *refs):
    if blocks:
        *smalls, out, xs, d = refs
        small = jnp.concatenate([v[...] for v in smalls], axis=0).astype(bf16)
        n1, n2 = blocks
        per = n1 + n2 + small.shape[0]
        total = out.shape[0]
        a = q_ref[2]
    else:
        out, out_short, xs, d = refs
    big = big_ref[...]
    im = big.shape[0]
    cin = 2 * L

    def place(at):
        return pl.multiple_of(((at & 1) ^ a) * (total // 2) + (at // 2) * per, 16)

    spread_first(dp1, dps, d, im, 0)
    col = 0
    for k, taps in enumerate(PLANE_TAPS):
        cols = slice(col * L, (col + len(taps)) * L)
        load_plane(x, k, big, xs, im)
        grad = tn_dot(xs[...], d[:, cols]).astype(bf16)
        for n, t in enumerate(taps):
            value = grad[:, n * L : (n + 1) * L]
            if not blocks:
                if t < 0:
                    out_short[...] = value
                else:
                    out[t * cin : (t + 1) * cin, :] = value
                continue
            size, base, row = (n2, n1, 0) if t < 0 else (n1, 0, t * cin)
            done = 0
            while done < cin:
                at, inner = (row + done) // size, (row + done) % size
                count = min(cin - done, size - inner)
                start = pl.multiple_of(place(at) + base + inner, 16)
                out[pl.ds(start, count), :] = value[done : done + count, :]
                done += count
        col += len(taps)
    if blocks:
        for at in range(cin // n2):
            start = pl.multiple_of(place(at) + n1 + n2, 16)
            out[pl.ds(start, small.shape[0]), :] = small


def sum_beside(n_z, x, x_got, y, y_got, out):
    at = 0
    sizes = (x_got.shape[0] // n_z, y_got.shape[0] // n_z)
    for z in range(n_z):
        for kept, got, rows in ((x, x_got, sizes[0]), (y, y_got, sizes[1])):
            cut = slice(z * rows, (z + 1) * rows)
            out[at : at + rows, :] = (kept[cut, :].astype(f32) + got[cut, :].astype(f32)).astype(bf16)
            at += rows


def add_low(x, y, out):
    out[...] = (x[...].astype(f32) + y[...].astype(f32)).astype(bf16)


def add_three(x, y, z, out):
    out[...] = (x[...] + y[...].astype(f32) + z[...].astype(f32)).astype(bf16)


def pick_a(sizes, a_ref, *refs):
    *arrays, keep, give = refs
    at, source = 0, 0
    for rows in sizes:
        for out, a in ((keep, a_ref[2]), (give, 1 - a_ref[2])):
            cut = pl.ds(pl.multiple_of(source + a * rows, 8), rows)
            out[at : at + rows, :] = arrays[0][cut, :]
        at, source = at + rows, source + 2 * rows
        if source == arrays[0].shape[0]:
            arrays, source = arrays[1:], 0


def flip(value, axis):
    return lax.ppermute(value, axis, [(i, i ^ 1) for i in range(lax.axis_size(axis))])


def swap_ac(value):
    return lax.ppermute(value, ("a", "c"), [(1, 2), (2, 1)])


def sum_over(value, axis):
    count = lax.axis_size(axis)
    if count & (count - 1):
        return lax.psum(value, axis)
    step = 1
    while step < count:
        value = value + lax.ppermute(value, axis, [(i, i ^ step) for i in range(count)])
        step *= 2
    return value


def gather_quarters(h):
    from_b = flip(h, "b")
    from_c = flip(h, "c")
    return (h, from_c, from_b, flip(from_b, "c"))


def scatter_quarters(parts):
    p0, p1, p2, p3 = parts
    first = flip(p1, "c")
    second = flip(p3, "c")
    send = (p2 + second.astype(f32)).astype(bf16)
    return (p0, first, flip(send, "b"), send)


def pack(q_ref, first, short, norms, heads, mine, give):
    q = q_ref[0]
    n1, n2 = first.shape[0], short.shape[0]
    for out, part in ((mine, q), (give, q ^ 1)):
        cols = pl.ds(pl.multiple_of(part * L, L), L)
        out[0:n1, :] = first[:, cols]
        out[n1 : n1 + n2, :] = short[:, cols]
        out[n1 + n2 :, :] = heads[...]
        out[n1 + n2 : n1 + n2 + norms.shape[0], L - norms.shape[1] :] = norms[...]


def pack_rest(q_ref, second, third, fourth, *outs):
    cols = pl.ds(pl.multiple_of(q_ref[1] * L, L), L)
    for out, src in zip(outs, (second, third, fourth)):
        out[...] = src[:, cols]


def relay(*refs):
    *parts, out = refs
    rows = parts[0].shape[0]
    for k, part in enumerate(parts):
        out[k * rows : (k + 1) * rows, :] = part[...]


def unpack(n1, n2, block, k_ref, mine, other, first, short, params, heads):
    here, q = k_ref[0], k_ref[1]
    rows = mine.shape[0] // 4
    for k in range(8):
        piece = (mine, other)[k % 2][k // 2 * rows : (k // 2 + 1) * rows, :]
        at = here ^ k
        first[pl.ds(pl.multiple_of(at * n1, 32), n1), :] = piece[0:n1, :]
        short[pl.ds(pl.multiple_of(at * n2, 32), n2), :] = piece[n1 : n1 + n2, :]
        head = piece[n1 + n2 : n1 + n2 + block, :]
        lane = lax.broadcasted_iota(jnp.int32, head.shape, 1)
        heads[pl.ds(pl.multiple_of(at * block, 32), block), :] = jnp.where(
            lane < L - block, head, jnp.zeros_like(head)
        )
        for side in range(L // block):
            @pl.when(at == q * (L // block) + side)
            def _():
                value = piece[n1 + n2 : n1 + n2 + 16, L - block :].astype(f32)
                params[:, side * block : (side + 1) * block] = value


def assemble(q_ref, p0, p1, p2, p3, *outs):
    q = q_ref[0]
    for j, part in enumerate((p0, p1, p2, p3)):
        cols = pl.ds(pl.multiple_of((q ^ j) * L, L), L)
        at = 0
        for out in outs:
            out[:, cols] = part[at : at + out.shape[0], :].astype(f32)
            at += out.shape[0]


def assemble_last(block, tasks, q_ref, p0, p1, p2, p3, *refs):
    *outs, gains, biases, heads, wide = refs
    assemble(q_ref, p0, p1, p2, p3, *outs, wide)
    start = q_ref[1] * block
    own = wide[:, pl.ds(pl.multiple_of(start // L * L, L), L)]
    value = own[:, :block]
    for k in range(1, L // block):
        value = jnp.where(start % L == k * block, own[:, k * block : (k + 1) * block], value)
    heads[...] = value[0:tasks, :]
    for out, side in ((gains, 0), (biases, 1)):
        rows = [tasks + side, tasks + 2 + side] + [tasks + 8 * k + side for k in (1, 2, 3)]
        out[...] = jnp.concatenate([value[r : r + 1, :] for r in rows], axis=0)


def input_grad_kernel(q_ref, order_ref, big_ref, parts, out):
    images = order_ref.shape[1]
    im = images
    wide = out.shape[1]
    spot = lax.broadcasted_iota(jnp.int32, (images, images), 1)
    pick = jnp.where(spot == jnp.transpose(jnp.broadcast_to(order_ref[0:1, :], (images, images))), 1.0, 0.0)
    pick = pick.astype(bf16)
    big = big_ref[0:1, :]
    for pr in range(2):
        for i in range(16):
            at = 16 * pr + i
            value = masked(tn_dot(blk(parts, at, im), pick), i, big)
            for pc in range(2):
                pixel = (2 * (i // 4) + pr) * 8 + 2 * (i % 4) + pc
                out[pixel, :, :] = value[pc * wide : (pc + 1) * wide, :]


def body(
    features, buckets, micro_order, labels, conv_first, conv_short, conv_second, conv_third, conv_fourth,
    norm_gains, norm_biases, head_weight, head_bias,
):
    ia, ib, iz, ic = (lax.axis_index(n) for n in ("a", "b", "z", "c"))
    n_group = lax.axis_size("z") * lax.axis_size("c")
    images, grid, _, cin = features.shape
    channels = conv_second.shape[1]
    tasks = head_weight.shape[1]
    quarter = 2 * ib + ic
    shared = 2 * ib + ia
    im = images
    nm = MICRO
    rows = 16 * im
    own = ia == ic
    q_arr = jnp.stack([quarter, own, ia, iz]).astype(jnp.int32)
    c_arr = jnp.stack([ic, ib]).astype(jnp.int32)

    block = channels // n_group
    r_first, r_short = conv_first.shape[0], conv_short.shape[0]
    n_z = lax.axis_size("z")

    small_rows = max(16, block)
    norms = jnp.concatenate([norm_gains, norm_biases], axis=0)
    norms = jnp.pad(norms, ((0, 6), (0, 0)))
    heads = jnp.pad(head_weight, ((0, small_rows - block), (0, L - tasks)))
    slot_rows = r_first + r_short + small_rows
    piece_t = sds(slot_rows, L, dtype=bf16)
    quarter_t = sds(conv_second.shape[0], L, dtype=bf16)
    pack_arr = jnp.stack([quarter, shared]).astype(jnp.int32)
    mine, give = call(pack, [piece_t, piece_t], (pack_arr, conv_first, conv_short, norms, heads))
    rest = call(
        pack_rest, [quarter_t] * 3, (pack_arr, conv_second, conv_third, conv_fourth), ties=(give,)
    )
    rest = [lax.all_gather(w, ("z", "c"), axis=0, tiled=True) for w in rest]
    piece = jnp.where(own, mine, flip(give, "c"))

    parts = [piece]
    if n_z == 4:
        parts += [lax.ppermute(piece, "z", [(i, i ^ m) for i in range(n_z)]) for m in range(1, n_z)]

    ints = jnp.concatenate(
        [
            labels,
            buckets[:, None],
            micro_order.reshape(images, 1),
            jnp.zeros((images, L - tasks - 2), jnp.int32),
        ],
        axis=1,
    )
    ints = jnp.where(own, ints, flip(ints, "c"))
    order = ints[:, tasks + 1]
    feats = jnp.where(own, features, flip(features, "c"))
    feats = feats[order].reshape(images, grid * grid, cin).transpose(1, 0, 2).reshape(4 * rows, cin)

    if n_z == 4:
        (stack,) = call(
            relay, [sds(n_z * slot_rows, L, dtype=bf16)], parts, scalars=0, ties=(feats,)
        )
        w_first, w_short, params, head_all, rest[0] = call(
            functools.partial(unpack, r_first, r_short, block),
            [
                sds(n_group * r_first, L, dtype=bf16),
                sds(n_group * r_short, L, dtype=bf16),
                sds(16, L),
                sds(channels, L, dtype=bf16),
            ],
            (jnp.stack([2 * iz + ia, quarter]).astype(jnp.int32), stack, flip(stack, "a")),
            through=(rest[0],),
        )
    else:
        packed = lax.all_gather(piece, ("z", "a"), axis=0)
        w_first = packed[:, :r_first].reshape(n_group * r_first, L)
        w_short = packed[:, r_first : r_first + r_short].reshape(n_group * r_short, L)
        small = packed[:, r_first + r_short :]
        head_all = small[:, :block].reshape(channels, L)
        lane = lax.broadcasted_iota(jnp.int32, head_all.shape, 1)
        head_all = jnp.where(lane < tasks, head_all, jnp.zeros_like(head_all))
        params = small[:, :16, L - block :].transpose(1, 0, 2).reshape(16, channels)
        params = lax.dynamic_slice_in_dim(params, quarter * L, L, 1).astype(f32)
    w_second, w_third, w_fourth = [Pick(w, swap_ac(w)) for w in rest]
    head_mine = lax.dynamic_slice_in_dim(head_all, quarter * L, L, 0)
    bias_row = jnp.broadcast_to(
        jnp.pad(head_bias.astype(f32), (0, L - tasks))[None, :], (8, L)
    )

    own_big = jnp.broadcast_to(buckets[None, :].astype(f32), (8, images))
    ints = ints[order]
    label_rows = ints.astype(f32)
    big = jnp.broadcast_to(ints[:, tasks : tasks + 1].astype(f32), (images, L))

    act = sds(rows, L, dtype=bf16)
    full = sds(rows, L)
    img = sds(im, L)
    micro = sds(8, L)
    kept = Keep(rows, L)
    low_kept = Keep(rows, L, dtype=bf16)
    vm = pltpu.VMEM
    conv_scratch = [vm((4 * L, 9 * L), bf16), vm((rows, 9 * L), f32), vm((rows, L), f32)]
    wide_kept = Keep(rows, 4 * L, dtype=bf16)
    back_scratch = [vm((4 * L, 9 * L), bf16), vm((rows, 9 * L), bf16), vm((rows, L), f32)]
    flops_conv = 2 * rows * 4 * L * 9 * L

    def run(kernel, outs, args, scratch, flops=flops_conv, ties=(), through=()):
        return call(functools.partial(kernel, nm), outs, args, scratch, 1, flops, ties, through)

    first = run(
        first_forward,
        [act, low_kept, kept, micro, kept, micro],
        (q_arr, feats, w_first, w_short, params, big),
        [vm((rows, cin), bf16), vm((cin, 10 * L), bf16), vm((rows, 10 * L), f32), vm((rows, L), f32), vm((rows, L), f32)],
    )
    h1 = gather_quarters(first[0])
    second = run(
        second_forward,
        [act, kept, micro, wide_kept],
        (q_arr, *h1, w_second, params, big, first[1]),
        conv_scratch,
    )
    x2 = gather_quarters(second[0])
    third = run(third_forward, [act, kept, micro, wide_kept], (q_arr, *x2, w_third, params, big), conv_scratch)
    h3 = gather_quarters(third[0])
    fourth = run(
        fourth_forward,
        [img, img, kept, micro, wide_kept],
        (q_arr, *h3, w_fourth, params, big, second[0], head_mine),
        conv_scratch,
    )
    pooled, logits = fourth[:2]

    logits = logits + flip(logits, "c")
    stat_rows = tasks + 8
    errors, stats = call(
        lambda mine, other, bias, lab, err, st: head_errors(mine, other, bias, lab, tasks, err, st),
        [sds(images, L), sds(stat_rows, L)],
        (logits, flip(logits, "b"), bias_row, label_rows),
        scalars=0,
    )
    stats = sum_over(sum_over(stats, "a"), "z")
    dz, bias_grad, head_grad = call(
        functools.partial(head_weights, float(images * n_group), tasks),
        [sds(images, L), sds(8, L), sds(tasks, L)],
        (stats, errors, head_all, head_mine, pooled),
        scalars=0,
    )

    direct = n_z == 4
    quads = [kept, low_kept, kept, low_kept]
    own_rows = 9 * channels // n_group
    shared_arr = shared[None].astype(jnp.int32)

    def grad_of(acts, grad, ties, block=0):
        return call(
            functools.partial(weight_grad, block),
            [Keep(9 * channels, L, dtype=bf16)],
            (q_arr, acts, grad),
            [vm((rows, 9 * L), bf16)],
            1,
            flops_conv,
            ties,
        )[0]

    def over_z(grad):
        return lax.psum_scatter(grad, "z", scatter_dimension=0, tiled=True)

    def other_half(blocks):
        return flip(blocks[blocks.shape[0] // 2 :], "a")

    def to_places(shard):
        parts = []
        for m in range(4):
            pairs = [
                (4 * i + 2 * j + k, 4 * (k ^ (m & 1)) + 2 * (j ^ (m >> 1)) + i)
                for i in range(2)
                for j in range(2)
                for k in range(2)
            ]
            parts.append(lax.ppermute(shard, ("a", "b", "c"), pairs))
        return parts

    b4 = run(
        fourth_backward,
        [*quads, low_kept, low_kept, sds(8, L)],
        (q_arr, dz, fourth[2], fourth[3], second[0], w_fourth, params, big),
        back_scratch,
    )
    g3 = scatter_quarters(b4[:4])
    dw4 = grad_of(fourth[4], b4[4], (g3[3],))
    *b3, dw4 = run(
        third_backward,
        [*quads, low_kept, sds(8, L)],
        (q_arr, *g3[:3], third[1], third[2], w_third, params, big),
        back_scratch,
        through=(dw4,),
    )
    r4 = over_z(dw4)
    g2 = scatter_quarters(b3[:4])
    dw3 = grad_of(third[3], b3[4], (g2[3],))
    *b2, dw3 = run(
        second_backward,
        [*quads, low_kept, low_kept, sds(8, L)],
        (q_arr, *g2[:3], b4[5], first[1], second[1], second[2], w_second, params, big),
        back_scratch,
        through=(dw3,),
    )
    r3 = over_z(dw3)
    g1 = scatter_quarters(b2[:4])
    dw2 = grad_of(second[3], b2[4], (g1[3],), own_rows if direct else 0)
    got2 = other_half(dw2)
    twice = [Keep(2 * rows, L), Keep(2 * rows, L, dtype=bf16)] * 2
    b1 = run(
        first_backward,
        [*twice, low_kept, low_kept, sds(8, L)],
        (c_arr, *g1[:3], b2[5], *first[2:], w_first, w_short, params, big),
        [vm((cin, 10 * L), bf16), vm((rows, 10 * L), bf16), vm((rows, L), f32)],
        ties=(dw2,),
    )

    p0, p1, p2, p3 = b1[:4]
    p1, p3 = flip(p1, "c"), flip(p3, "c")
    (send,) = call(add_low, [sds(2 * rows, L, dtype=bf16)], (p2, p3), scalars=0)
    across = flip(send, "b")
    smalls = [head_grad, b1[-1], b2[-1], b3[-1], b4[-1]]
    small_rows = sum(v.shape[0] for v in smalls)
    smalls.append(jnp.zeros((-small_rows % 16 or 16, L), f32))
    small_rows += smalls[-1].shape[0]
    slot_rows = r_first + r_short + small_rows
    grad_args = (q_arr, feats, b1[4], b1[5], big)
    grad_scratch = [vm((rows, cin), bf16), vm((rows, 10 * L), bf16)]

    def low(count):
        return sds(count, L, dtype=bf16)

    if direct:
        (slots,) = call(
            functools.partial(first_weight_grad, (r_first, r_short)),
            [Keep(n_group * slot_rows, L, dtype=bf16)],
            grad_args + tuple(smalls),
            grad_scratch,
            ties=(send,),
        )
        (total,) = call(add_three, [low(2 * rows)], (p0, p1, across), scalars=0, ties=(slots,))
        (dw21,) = call(
            functools.partial(sum_beside, n_z),
            [Keep(n_z * (own_rows + slot_rows), L, dtype=bf16)],
            (dw2, got2, slots, other_half(slots)),
            scalars=0,
            ties=(total,),
        )
        shard21 = over_z(dw21)
    else:
        dw1, dws = call(
            functools.partial(first_weight_grad, None),
            [sds(9 * cin, L, dtype=bf16), sds(cin, L, dtype=bf16)],
            grad_args,
            grad_scratch,
        )
        small = jnp.concatenate(smalls, axis=0).astype(bf16)
        dw21 = [
            dw2.reshape(n_group, own_rows, L),
            dw1.reshape(n_group, r_first, L),
            dws.reshape(n_group, r_short, L),
            jnp.broadcast_to(small[None], (n_group, *small.shape)),
        ]
        dw21 = jnp.concatenate(dw21, axis=1)
        shard21 = lax.psum_scatter(dw21, ("z", "a"), scatter_dimension=0)
        (total,) = call(add_three, [low(2 * rows)], (p0, p1, across), scalars=0)

    def give_a(shards, sizes, ties):
        count = sum(sizes)
        keep, give = call(
            functools.partial(pick_a, sizes), [low(count)] * 2, (q_arr, *shards), ties=ties
        )
        return keep, flip(give, "a")

    def sum_a(keep, got, ties=()):
        return call(add_low, [low(keep.shape[0])], (keep, got), scalars=0, ties=ties)[0]

    shard43 = sum_a(*give_a((r4, r3), (own_rows, own_rows), (dw21,)))
    places43 = to_places(shard43)
    swapped = swap_ac(total)
    conv_fourth_grad, conv_third_grad = call(
        assemble, [sds(own_rows, channels)] * 2, (shared_arr, *places43)
    )
    (input_grad,) = call(
        input_grad_kernel,
        [sds(grid * grid, cin // 4, images)],
        (q_arr, micro_order, own_big, Pick(total, swapped)),
        ties=(conv_third_grad,),
    )
    places = to_places(shard21)
    group = 2 * iz + ic
    group_arr = jnp.stack([shared, group]).astype(jnp.int32)
    wide_outs = [sds(own_rows, channels), sds(r_first, channels), sds(r_short, channels)]
    if direct:
        conv_second_grad, conv_first_grad, conv_short_grad, gains_grad, biases_grad, head_weight_grad = call(
            functools.partial(assemble_last, block, tasks),
            wide_outs + [sds(5, block), sds(5, block), sds(tasks, block)],
            (group_arr, *places),
            [vm((small_rows, channels), f32)],
        )
    else:
        conv_second_grad, conv_first_grad, conv_short_grad, wide_small = call(
            assemble, wide_outs + [sds(small_rows, channels)], (group_arr, *places)
        )
        own_small = lax.dynamic_slice_in_dim(wide_small, group * block, block, 1)
        head_weight_grad = own_small[:tasks]
        n1, n2, n3, n4 = (own_small[tasks + 8 * i : tasks + 8 * (i + 1)] for i in range(4))
        gains_grad = jnp.stack([n1[0], n1[2], n2[0], n3[0], n4[0]])
        biases_grad = jnp.stack([n1[1], n1[3], n2[1], n3[1], n4[1]])
    input_grad = input_grad.reshape(grid, grid, cin // 4, images).transpose(3, 0, 1, 2)

    moved = lax.ppermute(
        pooled,
        ("a", "b", "c"),
        [(4 * i + 2 * j + k, 4 * j + 2 * k + i) for i in range(2) for j in range(2) for k in range(2)],
    )
    spots = jnp.arange(images, dtype=jnp.int32)
    inverse = jnp.sum(
        jnp.where(micro_order[0][None, :] == spots[:, None], spots[None, :], 0), axis=1
    )
    pooled_out = moved[inverse]

    return (
        pooled_out,
        input_grad,
        conv_first_grad,
        conv_short_grad,
        conv_second_grad,
        conv_third_grad,
        conv_fourth_grad,
        gains_grad,
        biases_grad,
        head_weight_grad.T,
        bias_grad[0, :tasks],
    )


def solution(mesh):
    sections, groups = mesh.shape["section"], mesh.shape["dp"]
    fine = Mesh(mesh.devices.reshape(2, sections // 2, groups // 2, 2), ("a", "b", "z", "c"))
    dp, section = ("z", "c"), ("a", "b")
    return jax.shard_map(
        body,
        mesh=fine,
        in_specs=(
            P(dp, None, None, None),
            P(dp),
            P(dp, None),
            P(dp, None),
            P(dp, None),
            P(dp, None),
            P(dp, None),
            P(dp, None),
            P(dp, None),
            P(None, dp),
            P(None, dp),
            P(dp, None),
            P(),
        ),
        out_specs=(
            P(dp, section),
            P(dp, None, None, section),
            P(dp, None),
            P(dp, None),
            P(dp, None),
            P(dp, None),
            P(dp, None),
            P(None, dp),
            P(None, dp),
            P(dp, None),
            P(),
        ),
        check_vma=False,
    )
```

```python
import functools

import jax
import jax.numpy as jnp
from jax import lax
from jax.experimental import pallas as pl
from jax.experimental.pallas import tpu as pltpu
from jax.sharding import Mesh, PartitionSpec as P

MICRO = 6
FW_STEPS = 20
EPSILON = 1e-05
SOFTMAX_HEAT = 0.01
HIGHEST = lax.Precision.HIGHEST

f32 = jnp.float32
bf16 = jnp.bfloat16
L = 128

PLANE_TAPS = ((4, -1), (3, 5), (1, 7), (0, 2, 6, 8))
FIRST_COLS = tuple(tap for taps in PLANE_TAPS for tap in taps)


VMEM_MB = 52


class Keep:
    def __init__(self, *shape, dtype=f32):
        self.shape, self.dtype = shape, dtype


class Pick:
    def __init__(self, first, other):
        self.first, self.other = first, other
        self.shape, self.dtype, self.size = first.shape, first.dtype, first.size


class Buf:
    def __init__(self, ref, start, wait, out=False):
        self.ref, self.start, self.wait = ref, start, wait
        self.out, self.started, self.ready = out, not out, out
        self.shape, self.dtype = ref.shape, ref.dtype
        if not out:
            start()

    def get(self):
        if not self.ready:
            self.wait()
            self.ready = True

    def __getitem__(self, at):
        self.get()
        return self.ref[at]

    def __setitem__(self, at, value):
        self.ref[at] = value

    def send(self):
        if not self.started:
            self.start()
            self.started = True


def call(kernel, outs, args, scratch=(), scalars=1, flops=0, ties=(), through=()):
    def far(a):
        return isinstance(a, (Pick, Keep))

    flat, specs, places = [], [], []
    for k, a in enumerate(args):
        places.append(len(flat))
        if k < scalars:
            space = pltpu.SMEM
        else:
            space = pltpu.HBM if far(a) else pltpu.VMEM
        for x in (a.first, a.other) if isinstance(a, Pick) else (a,):
            flat.append(x)
            specs.append(pl.BlockSpec(memory_space=space))
    n_args = len(flat)
    specs += [pl.BlockSpec(memory_space=pl.ANY)] * (len(ties) + len(through))
    far_in = [k for k, a in enumerate(args) if k >= scalars and far(a)]
    far_out = [k for k, o in enumerate(outs) if far(o)]
    buffers = [pltpu.VMEM(args[k].shape, args[k].dtype) for k in far_in]
    buffers += [pltpu.VMEM(outs[k].shape, outs[k].dtype) for k in far_out]
    n_in = n_args + len(ties) + len(through)
    n_outs = len(outs)
    n_bufs = len(buffers)

    def run(*refs):
        ins, results = list(refs[:n_args]), list(refs[n_in : n_in + n_outs])
        rest = refs[n_in + n_outs + len(through) :]
        temps, sems, rest = rest[:n_bufs], rest[n_bufs], rest[n_bufs + 1 :]
        given = []
        for k in range(len(args)):
            src = ins[places[k]]
            if k in far_in:
                n = far_in.index(k)
                copy = pltpu.make_async_copy(src, temps[n], sems.at[n])
                start = copy.start
                if isinstance(args[k], Pick):
                    second = pltpu.make_async_copy(ins[places[k] + 1], temps[n], sems.at[n])

                    def start(copy=copy, second=second):
                        pl.when(ins[0][1] == 1)(copy.start)
                        pl.when(ins[0][1] == 0)(second.start)

                src = Buf(temps[n], start, copy.wait)
            given.append(src)
        made = []
        for k in range(n_outs):
            out = results[k]
            if k in far_out:
                n = len(far_in) + far_out.index(k)
                copy = pltpu.make_async_copy(temps[n], out, sems.at[n])
                out = Buf(temps[n], copy.start, copy.wait, out=True)
            made.append(out)
        kernel(*given, *made, *rest)
        for x in given:
            if isinstance(x, Buf):
                x.get()
        made = [x for x in made if isinstance(x, Buf)]
        for x in made:
            x.send()
        for x in made:
            x.wait()

    outs = [sds(*o.shape, dtype=o.dtype) if far(o) else o for o in outs]
    size = sum(a.size * a.dtype.itemsize for a in flat) + sum(o.size * o.dtype.itemsize for o in outs)
    return pl.pallas_call(
        run,
        out_shape=tuple(outs) + tuple(sds(*x.shape, dtype=x.dtype) for x in through),
        in_specs=specs,
        out_specs=tuple(
            pl.BlockSpec(memory_space=pltpu.HBM if k in far_out else pltpu.VMEM) for k in range(n_outs)
        )
        + tuple(pl.BlockSpec(memory_space=pl.ANY) for _ in through),
        scratch_shapes=buffers + [pltpu.SemaphoreType.DMA((max(n_bufs, 1),))] + list(scratch),
        input_output_aliases={n_args + len(ties) + k: n_outs + k for k in range(len(through))},
        compiler_params=pltpu.CompilerParams(vmem_limit_bytes=VMEM_MB << 20),
        cost_estimate=pl.CostEstimate(flops=int(flops), bytes_accessed=int(size), transcendentals=0),
    )(*flat, *ties, *through)


def sds(*shape, dtype=f32):
    return jax.ShapeDtypeStruct(shape, dtype)


def nt_dot(x, y):
    return lax.dot_general(x, y, (((1,), (1,)), ((), ())), preferred_element_type=f32)


def tn_dot(x, y):
    return lax.dot_general(x, y, (((0,), (0,)), ((), ())), preferred_element_type=f32)


def sigmoid(v):
    return 0.5 + 0.5 * jnp.tanh(0.5 * v)


def pixel_mask(i, big):
    return None if (i // 4 < 2 and i % 4 < 2) else big


def masked(value, i, big):
    return value if pixel_mask(i, big) is None else value * big


def per_micro(value, nm):
    rows, lanes = value.shape
    return jnp.sum(value.reshape(nm, rows // nm, lanes), axis=1)


def spread_micro(value, im):
    nm, lanes = value.shape
    return jnp.broadcast_to(value[:, None, :], (nm, im // nm, lanes)).reshape(im, lanes)


def blk(ref, i, im):
    return ref[i * im : (i + 1) * im, :]


def norm_forward(p_ref, xhat_ref, inv_ref, big, nm):
    im = big.shape[0]
    total = per_micro(4.0 + 12.0 * big, nm)
    acc = jnp.zeros_like(big)
    for i in range(16):
        acc = acc + masked(blk(p_ref, i, im), i, big)
    mean = spread_micro(per_micro(acc, nm) / total, im)
    acc = jnp.zeros_like(big)
    for i in range(16):
        cen = blk(p_ref, i, im) - mean
        acc = acc + masked(cen * cen, i, big)
    inv = lax.rsqrt(per_micro(acc, nm) / total + EPSILON)
    inv_ref[...] = jnp.concatenate([inv, jnp.zeros((8 - nm, inv.shape[1]), f32)], axis=0)
    inv = spread_micro(inv, im)
    for i in range(16):
        xhat_ref[i * im : (i + 1) * im, :] = (blk(p_ref, i, im) - mean) * inv


def norm_backward(dy_ref, xhat_ref, inv_ref, gain, big, nm, out_ref):
    im = big.shape[0]
    total = per_micro(4.0 + 12.0 * big, nm)
    sum_dy = jnp.zeros_like(big)
    sum_dx = jnp.zeros_like(big)
    for i in range(16):
        dy = blk(dy_ref, i, im)
        sum_dy = sum_dy + dy
        sum_dx = sum_dx + dy * blk(xhat_ref, i, im)
    sum_dy = per_micro(sum_dy, nm)
    sum_dx = per_micro(sum_dx, nm)
    mean_dy = spread_micro(sum_dy / total, im)
    mean_dx = spread_micro(sum_dx / total, im)
    scale = spread_micro(inv_ref[0:nm, :] * gain, im)
    for i in range(16):
        off = masked(mean_dy + blk(xhat_ref, i, im) * mean_dx, i, big)
        grad = scale * (blk(dy_ref, i, im) - off)
        out_ref[i * im : (i + 1) * im, :] = grad.astype(bf16)
    return jnp.sum(sum_dx, axis=0, keepdims=True), jnp.sum(sum_dy, axis=0, keepdims=True)


def load_weights(q_ref, w_ref, ws):
    channels = 4 * L
    q = q_ref[0]
    for t in range(9):
        for j in range(4):
            start = pl.multiple_of(t * channels + (q ^ j) * L, L)
            ws[j * L : (j + 1) * L, t * L : (t + 1) * L] = w_ref[pl.ds(start, L), :]


def row_taps(r):
    return (3 * L if r == 3 else 0), (6 * L if r == 0 else 9 * L)


def conv_forward(q_ref, x_refs, w_ref, xs, ws, y, p, im):
    for j in range(4):
        xs[:, j * L : (j + 1) * L] = x_refs[j][...]
    xs.send()
    load_weights(q_ref, w_ref, ws)
    for r in range(4):
        lo, hi = row_taps(r)
        rows = slice(r * 4 * im, (r + 1) * 4 * im)
        y[rows, lo:hi] = jnp.dot(xs[rows, :], ws[:, lo:hi], preferred_element_type=f32)
    for r in range(4):
        for c in range(4):
            acc = None
            for t in range(9):
                ri, ci = r + t // 3 - 1, c + t % 3 - 1
                if 0 <= ri < 4 and 0 <= ci < 4:
                    i = ri * 4 + ci
                    term = y[i * im : (i + 1) * im, t * L : (t + 1) * L]
                    acc = term if acc is None else acc + term
            p[(r * 4 + c) * im : (r * 4 + c + 1) * im, :] = acc


def spread_taps(dp_ref, d, im, rows_at, all_taps):
    for r in range(4):
        lo, hi = (0, 9 * L) if all_taps else row_taps(r)
        for c in range(4):
            at = rows_at + (r * 4 + c) * im
            for t in range(lo // L, hi // L):
                ro, co = r - t // 3 + 1, c - t % 3 + 1
                if 0 <= ro < 4 and 0 <= co < 4:
                    value = blk(dp_ref, ro * 4 + co, im)
                else:
                    value = jnp.zeros((im, L), bf16)
                d[at : at + im, t * L : (t + 1) * L] = value


def conv_back_input(q_ref, dp_ref, w_ref, ws, d, outs, im):
    load_weights(q_ref, w_ref, ws)
    spread_taps(dp_ref, d, im, 0, False)
    for r in range(4):
        lo, hi = row_taps(r)
        rows = slice(r * 4 * im, (r + 1) * 4 * im)
        dx = nt_dot(d[rows, lo:hi], ws[:, lo:hi])
        for j in range(4):
            outs[j][rows, :] = dx[:, j * L : (j + 1) * L].astype(outs[j].dtype)


def load_plane(x, k, big, xs, im):
    wide = jnp.concatenate([big, big], axis=1).astype(bf16)
    for i in range(16):
        pixel = (2 * (i // 4) + k // 2) * 8 + 2 * (i % 4) + k % 2
        xs[i * im : (i + 1) * im, :] = masked(blk(x, pixel, im), i, wide)


def first_forward(nm, c_ref, x, w, w_short, params, big_ref, h, s, xh1, inv1, xh2, inv2, xs, wsc, y, p1, p2):
    big = big_ref[...]
    im = big.shape[0]
    cin = 2 * L
    col = 0
    for k, taps in enumerate(PLANE_TAPS):
        for n, t in enumerate(taps):
            src = w_short[...] if t < 0 else w[t * cin : (t + 1) * cin, :]
            wsc[:, (col + n) * L : (col + n + 1) * L] = src
        cols = slice(col * L, (col + len(taps)) * L)
        load_plane(x, k, big, xs, im)
        y[:, cols] = jnp.dot(xs[...], wsc[:, cols], preferred_element_type=f32)
        col += len(taps)
    for r in range(4):
        for c in range(4):
            o = r * 4 + c
            acc = None
            for n, t in enumerate(FIRST_COLS):
                if t < 0:
                    p2[o * im : (o + 1) * im, :] = y[o * im : (o + 1) * im, n * L : (n + 1) * L]
                    continue
                ri = r - 1 if t // 3 == 0 else r
                ci = c - 1 if t % 3 == 0 else c
                if ri >= 0 and ci >= 0:
                    i = ri * 4 + ci
                    term = y[i * im : (i + 1) * im, n * L : (n + 1) * L]
                    acc = term if acc is None else acc + term
            p1[o * im : (o + 1) * im, :] = acc
    norm_forward(p1, xh1, inv1, big, nm)
    norm_forward(p2, xh2, inv2, big, nm)
    for i in range(16):
        rows = slice(i * im, (i + 1) * im)
        v = blk(xh1, i, im) * params[0:1, :] + params[5:6, :]
        h[rows, :] = masked(v * sigmoid(v), i, big).astype(bf16)
        v = blk(xh2, i, im) * params[1:2, :] + params[6:7, :]
        s[rows, :] = masked(v, i, big).astype(bf16)


def second_forward(nm, q_ref, x0, x1, x2, x3, w, params, big_ref, s, out, xh, inv, xs, ws, y, p):
    big = big_ref[...]
    im = big.shape[0]
    conv_forward(q_ref, (x0, x1, x2, x3), w, xs, ws, y, p, im)
    norm_forward(p, xh, inv, big, nm)
    for i in range(16):
        rows = slice(i * im, (i + 1) * im)
        u = blk(xh, i, im) * params[2:3, :] + params[7:8, :]
        u = masked(u, i, big).astype(bf16).astype(f32)
        v = u + s[rows, :].astype(f32)
        out[rows, :] = masked(v * sigmoid(v), i, big).astype(bf16)


def third_forward(nm, q_ref, x0, x1, x2, x3, w, params, big_ref, out, xh, inv, xs, ws, y, p):
    big = big_ref[...]
    im = big.shape[0]
    conv_forward(q_ref, (x0, x1, x2, x3), w, xs, ws, y, p, im)
    norm_forward(p, xh, inv, big, nm)
    for i in range(16):
        rows = slice(i * im, (i + 1) * im)
        v = blk(xh, i, im) * params[3:4, :] + params[8:9, :]
        out[rows, :] = masked(v * sigmoid(v), i, big).astype(bf16)


def fourth_forward(
    nm, q_ref, x0, x1, x2, x3, w, params, big_ref, res, head, pooled, logits, xh, inv, xs, ws, y, p
):
    big = big_ref[...]
    im = big.shape[0]
    conv_forward(q_ref, (x0, x1, x2, x3), w, xs, ws, y, p, im)
    norm_forward(p, xh, inv, big, nm)
    acc = jnp.zeros_like(big)
    for i in range(16):
        rows = slice(i * im, (i + 1) * im)
        v = blk(xh, i, im) * params[4:5, :] + params[9:10, :] + res[rows, :].astype(f32)
        acc = acc + masked(v * sigmoid(v), i, big)
    pool = acc / (4.0 + 12.0 * big)
    pooled[...] = pool
    logits[...] = jnp.dot(pool.astype(bf16), head[...], preferred_element_type=f32)


def head_errors(mine, other, bias, labels, tasks, errors, stats):
    logits = mine[...] + other[...] + bias[0:1, :]
    lane = lax.broadcasted_iota(jnp.int32, logits.shape, 1)
    err = jnp.where(lane < tasks, sigmoid(logits) - labels[...], 0.0)
    errors[...] = err
    gram = lax.dot_general(err, err, (((0,), (0,)), ((), ())), precision=HIGHEST, preferred_element_type=f32)
    stats[0:tasks, :] = gram[0:tasks, :]
    stats[tasks:, :] = jnp.broadcast_to(jnp.sum(err, axis=0, keepdims=True), (stats.shape[0] - tasks, L))


def head_weights(count, tasks, stats, errors, head_all, head_mine, pooled, dz, bias_grad, head_grad):
    inner = tn_dot(head_all[...], head_all[...])
    gram = stats[0:tasks, :] * inner[0:tasks, :] / count
    row = lax.broadcasted_iota(jnp.int32, (tasks, L), 0)
    lane = lax.broadcasted_iota(jnp.int32, (tasks, L), 1)
    weight_row = jnp.where(lane[0:1, :] < tasks, 1.0 / tasks, 0.0)
    for step in range(FW_STEPS):
        score = -jnp.sum(gram * weight_row, axis=1, keepdims=True) / SOFTMAX_HEAT
        power = jnp.exp(score - jnp.max(score, axis=0, keepdims=True))
        corner = power / jnp.sum(power, axis=0, keepdims=True)
        corner = jnp.sum(jnp.where(row == lane, corner, 0.0), axis=0, keepdims=True)
        rate = 2.0 / (step + 2.0)
        weight_row = (1.0 - rate) * weight_row + rate * corner
    scaled = errors[...] * weight_row
    dz[...] = lax.dot_general(
        scaled,
        head_mine[...].astype(f32),
        (((1,), (1,)), ((), ())),
        precision=HIGHEST,
        preferred_element_type=f32,
    )
    bias_grad[...] = jnp.broadcast_to(weight_row * stats[tasks : tasks + 1, :], bias_grad.shape)
    grad = lax.dot_general(
        scaled,
        pooled[...].astype(bf16).astype(f32),
        (((0,), (0,)), ((), ())),
        precision=HIGHEST,
        preferred_element_type=f32,
    )
    head_grad[...] = grad[0:tasks, :]


def fourth_backward(
    nm, q_ref, dz, xh, inv, res, w, params, big_ref, o0, o1, o2, o3, dp, d_res, norm, ws, d, dy
):
    big = big_ref[...]
    im = big.shape[0]
    out_grad = dz[...] / (4.0 + 12.0 * big)
    for i in range(16):
        rows = slice(i * im, (i + 1) * im)
        v = blk(xh, i, im) * params[4:5, :] + params[9:10, :] + res[rows, :].astype(f32)
        sig = sigmoid(v)
        grad = masked(out_grad * (sig * (1.0 + v * (1.0 - sig))), i, big)
        dy[rows, :] = grad
        d_res[rows, :] = grad.astype(bf16)
    dgain, dbias = norm_backward(dy, xh, inv, params[4:5, :], big, nm, dp)
    norm[...] = jnp.concatenate([dgain, dbias, jnp.zeros((6, L), f32)], axis=0)
    conv_back_input(q_ref, dp, w, ws, d, (o0, o1, o2, o3), im)


def heads_and_fourth(
    count, tasks, nm, q_ref, stats, errors, head_all, head_mine, pooled, xh, inv, res, w, params, big_ref,
    o0, o1, o2, o3, dp, d_res, norm, bias_grad, head_grad, ws, d, dy, dz,
):
    head_weights(count, tasks, stats, errors, head_all, head_mine, pooled, dz, bias_grad, head_grad)
    fourth_backward(
        nm, q_ref, dz, xh, inv, res, w, params, big_ref, o0, o1, o2, o3, dp, d_res, norm, ws, d, dy
    )


def third_backward(
    nm, q_ref, g0, g1, g2, xh, inv, w, params, big_ref, o0, o1, o2, o3, dp, norm, ws, d, dy
):
    big = big_ref[...]
    im = big.shape[0]
    for i in range(16):
        rows = slice(i * im, (i + 1) * im)
        grad = g0[rows, :].astype(f32) + g1[rows, :].astype(f32) + g2[rows, :].astype(f32)
        grad = grad.astype(bf16).astype(f32)
        v = blk(xh, i, im) * params[3:4, :] + params[8:9, :]
        sig = sigmoid(v)
        dy[rows, :] = masked(grad * (sig * (1.0 + v * (1.0 - sig))), i, big)
    dgain, dbias = norm_backward(dy, xh, inv, params[3:4, :], big, nm, dp)
    norm[...] = jnp.concatenate([dgain, dbias, jnp.zeros((6, L), f32)], axis=0)
    conv_back_input(q_ref, dp, w, ws, d, (o0, o1, o2, o3), im)


def second_backward(
    nm, q_ref, g0, g1, g2, d_res, s, xh, inv, w, params, big_ref, o0, o1, o2, o3, dp, ds, norm, ws, d, dy
):
    big = big_ref[...]
    im = big.shape[0]
    for i in range(16):
        rows = slice(i * im, (i + 1) * im)
        grad = g0[rows, :].astype(f32) + g1[rows, :].astype(f32) + g2[rows, :].astype(f32)
        grad = grad + d_res[rows, :].astype(f32)
        u = blk(xh, i, im) * params[2:3, :] + params[7:8, :]
        v = masked(u, i, big).astype(bf16).astype(f32) + s[rows, :].astype(f32)
        sig = sigmoid(v)
        grad = masked(grad * (sig * (1.0 + v * (1.0 - sig))), i, big).astype(bf16)
        ds[rows, :] = grad
        dy[rows, :] = grad.astype(f32)
    dgain, dbias = norm_backward(dy, xh, inv, params[2:3, :], big, nm, dp)
    norm[...] = jnp.concatenate([dgain, dbias, jnp.zeros((6, L), f32)], axis=0)
    conv_back_input(q_ref, dp, w, ws, d, (o0, o1, o2, o3), im)


def spread_first(dp1, dps, d, im, rows_at):
    for i in range(16):
        r, c = i // 4, i % 4
        at = rows_at + i * im
        for n, t in enumerate(FIRST_COLS):
            if t < 0:
                value = blk(dps, i, im)
            else:
                ro = r + 1 if t // 3 == 0 else r
                co = c + 1 if t % 3 == 0 else c
                value = blk(dp1, ro * 4 + co, im) if ro < 4 and co < 4 else jnp.zeros((im, L), bf16)
            d[at : at + im, n * L : (n + 1) * L] = value


def first_backward(
    nm, c_ref, g0, g1, g2, ds, xh1, inv1, xh2, inv2, w, w_short, params, big_ref, *refs,
):
    outs, (dp1, dps, norm, ws, d, dy) = refs[:5], refs[5:]
    big = big_ref[...]
    im = big.shape[0]
    half, part = c_ref[0], c_ref[1]
    cin = 2 * L
    for i in range(16):
        rows = slice(i * im, (i + 1) * im)
        grad = g0[rows, :].astype(f32) + g1[rows, :].astype(f32) + g2[rows, :].astype(f32)
        grad = grad.astype(bf16).astype(f32)
        v = blk(xh1, i, im) * params[0:1, :] + params[5:6, :]
        sig = sigmoid(v)
        dy[rows, :] = masked(grad * (sig * (1.0 + v * (1.0 - sig))), i, big)
    gain1, bias1 = norm_backward(dy, xh1, inv1, params[0:1, :], big, nm, dp1)
    for i in range(16):
        rows = slice(i * im, (i + 1) * im)
        dy[rows, :] = masked(ds[rows, :].astype(f32), i, big)
    gain2, bias2 = norm_backward(dy, xh2, inv2, params[1:2, :], big, nm, dps)
    norm[...] = jnp.concatenate([gain1, bias1, gain2, bias2, jnp.zeros((4, L), f32)], axis=0)
    wide = cin // 4
    for n, t in enumerate(FIRST_COLS):
        for j in range(4):
            start = (half ^ (j & 1)) * 2 * wide + (part ^ (j >> 1)) * wide
            if t < 0:
                src = w_short[pl.ds(pl.multiple_of(start, wide), wide), :]
            else:
                src = w[pl.ds(pl.multiple_of(t * cin + start, wide), wide), :]
            ws[j * wide : (j + 1) * wide, n * L : (n + 1) * L] = src
    spread_first(dp1, dps, d, im, 0)
    col = 0
    for k, taps in enumerate(PLANE_TAPS):
        cols = slice(col * L, (col + len(taps)) * L)
        dx = nt_dot(d[:, cols], ws[:, cols])
        pair, side = k // 2, k % 2
        for j in range(4):
            ref = outs[j] if j < 3 else outs[3 + pair]
            at = pair * 16 * im if j < 3 else 0
            rows = slice(at, at + 16 * im)
            ref[rows, side * wide : (side + 1) * wide] = dx[:, j * wide : (j + 1) * wide].astype(ref.dtype)
        col += len(taps)


def halves(whole, outs):
    rows = outs[0].shape[0]
    for k, out in enumerate(outs):
        out[...] = whole[k * rows : (k + 1) * rows, :]


def weight_grad(block, q_ref, x, dp, *refs):
    if block:
        *outs, d, out = refs
    else:
        out, d = refs
    im = dp.shape[0] // 16
    q, a = q_ref[0], q_ref[2]
    total = out.shape[0]
    spread_taps(dp, d, im, 0, True)
    step = L // 2 if block else L
    for n in range(3):
        cols = slice(n * 3 * L, (n + 1) * 3 * L)
        grad = tn_dot(x[...], d[:, cols]).astype(bf16)
        for t in range(3):
            for j in range(4):
                for part in range(L // step):
                    start = (3 * n + t) * 4 * L + (q ^ j) * L + part * step
                    if block:
                        at = start // block
                        start = ((at & 1) ^ a) * (total // 2) + (at // 2) * block + start % block
                    start = pl.multiple_of(start, step)
                    value = grad[j * L + part * step : j * L + (part + 1) * step, t * L : (t + 1) * L]
                    out[pl.ds(start, step), :] = value
    if block:
        halves(out, outs)


def first_weight_grad(blocks, q_ref, x, dp1, dps, big_ref, *refs):
    if blocks:
        *smalls, keep, give, xs, d, out = refs
        small = jnp.concatenate([v[...] for v in smalls], axis=0).astype(bf16)
        n1, n2 = blocks
        per = n1 + n2 + small.shape[0]
        total = out.shape[0]
        a = q_ref[2]
    else:
        out, out_short, xs, d = refs
    big = big_ref[...]
    im = big.shape[0]
    cin = 2 * L

    def place(at):
        return pl.multiple_of(((at & 1) ^ a) * (total // 2) + (at // 2) * per, 16)

    spread_first(dp1, dps, d, im, 0)
    col = 0
    for k, taps in enumerate(PLANE_TAPS):
        cols = slice(col * L, (col + len(taps)) * L)
        load_plane(x, k, big, xs, im)
        grad = tn_dot(xs[...], d[:, cols]).astype(bf16)
        for n, t in enumerate(taps):
            value = grad[:, n * L : (n + 1) * L]
            if not blocks:
                if t < 0:
                    out_short[...] = value
                else:
                    out[t * cin : (t + 1) * cin, :] = value
                continue
            size, base, row = (n2, n1, 0) if t < 0 else (n1, 0, t * cin)
            done = 0
            while done < cin:
                at, inner = (row + done) // size, (row + done) % size
                count = min(cin - done, size - inner)
                start = pl.multiple_of(place(at) + base + inner, 16)
                out[pl.ds(start, count), :] = value[done : done + count, :]
                done += count
        col += len(taps)
    if blocks:
        for at in range(cin // n2):
            start = pl.multiple_of(place(at) + n1 + n2, 16)
            out[pl.ds(start, small.shape[0]), :] = small
        halves(out, (keep, give))


def sum_beside(n_z, x, x_got, y, y_got, out):
    at = 0
    sizes = (x_got.shape[0] // n_z, y_got.shape[0] // n_z)
    for z in range(n_z):
        for kept, got, rows in ((x, x_got, sizes[0]), (y, y_got, sizes[1])):
            cut = slice(z * rows, (z + 1) * rows)
            out[at : at + rows, :] = (kept[cut, :].astype(f32) + got[cut, :].astype(f32)).astype(bf16)
            at += rows


def add_low(x, y, out):
    out[...] = (x[...].astype(f32) + y[...].astype(f32)).astype(bf16)


def add_halves(x, low, high, out):
    rows = low.shape[0]
    for k, y in enumerate((low, high)):
        cut = slice(k * rows, (k + 1) * rows)
        out[cut, :] = (x[cut, :].astype(f32) + y[...].astype(f32)).astype(bf16)


def add_three(x, y, z, out):
    out[...] = (x[...].astype(f32) + y[...].astype(f32) + z[...].astype(f32)).astype(bf16)


def pick_a(sizes, a_ref, *refs):
    *arrays, keep, give = refs
    at, source = 0, 0
    for rows in sizes:
        for out, a in ((keep, a_ref[2]), (give, 1 - a_ref[2])):
            cut = pl.ds(pl.multiple_of(source + a * rows, 8), rows)
            out[at : at + rows, :] = arrays[0][cut, :]
        at, source = at + rows, source + 2 * rows
        if source == arrays[0].shape[0]:
            arrays, source = arrays[1:], 0


def flip(value, axis):
    return lax.ppermute(value, axis, [(i, i ^ 1) for i in range(lax.axis_size(axis))])


def swap_ac(value):
    return lax.ppermute(value, ("a", "c"), [(1, 2), (2, 1)])


def sum_over(value, axis):
    count = lax.axis_size(axis)
    if count & (count - 1):
        return lax.psum(value, axis)
    step = 1
    while step < count:
        value = value + lax.ppermute(value, axis, [(i, i ^ step) for i in range(count)])
        step *= 2
    return value


def gather_quarters(h):
    from_b = flip(h, "b")
    from_c = flip(h, "c")
    return (h, from_c, from_b, flip(from_b, "c"))


def scatter_quarters(parts):
    p0, p1, p2, p3 = parts
    first = flip(p1, "c")
    second = flip(p3, "c")
    send = (p2.astype(f32) + second.astype(f32)).astype(bf16)
    return (p0, first, flip(send, "b"), send)


def pack(q_ref, first, short, norms, heads, mine, give):
    q = q_ref[0]
    n1, n2 = first.shape[0], short.shape[0]
    for out, part in ((mine, q), (give, q ^ 1)):
        cols = pl.ds(pl.multiple_of(part * L, L), L)
        out[0:n1, :] = first[:, cols]
        out[n1 : n1 + n2, :] = short[:, cols]
        out[n1 + n2 :, :] = heads[...]
        out[n1 + n2 : n1 + n2 + norms.shape[0], L - norms.shape[1] :] = norms[...]


def pack_rest(q_ref, second, third, fourth, *outs):
    cols = pl.ds(pl.multiple_of(q_ref[1] * L, L), L)
    for out, src in zip(outs, (second, third, fourth)):
        out[...] = src[:, cols]


def prepare(q_ref, order_ref, x, out, *bufs):
    images = order_ref.shape[1]
    pixels = out.shape[0] // images
    x.get()

    def move(j, carry):
        source = pl.ds(pl.multiple_of(order_ref[0, j] * pixels, pixels), pixels)
        target = pl.ds(pl.multiple_of(j * pixels, pixels), pixels)
        for k, buf in enumerate(bufs):
            buf[target, :] = x.ref[source, k * L : (k + 1) * L].astype(f32)
        return carry

    lax.fori_loop(0, images, move, 0, unroll=4)
    for p in range(pixels):
        for k, buf in enumerate(bufs):
            value = buf[pl.ds(p, images, stride=pixels), :].astype(bf16)
            out[p * images : (p + 1) * images, k * L : (k + 1) * L] = value


def relay(*refs):
    *parts, out = refs
    rows = parts[0].shape[0]
    for k, part in enumerate(parts):
        out[k * rows : (k + 1) * rows, :] = part[...]


def unpack(n1, n2, block, k_ref, mine, other, first, short, params, heads):
    here, q = k_ref[0], k_ref[1]
    rows = mine.shape[0] // 4
    for k in range(8):
        piece = (mine, other)[k % 2][k // 2 * rows : (k // 2 + 1) * rows, :]
        at = here ^ k
        first[pl.ds(pl.multiple_of(at * n1, 32), n1), :] = piece[0:n1, :]
        short[pl.ds(pl.multiple_of(at * n2, 32), n2), :] = piece[n1 : n1 + n2, :]
        head = piece[n1 + n2 : n1 + n2 + block, :]
        lane = lax.broadcasted_iota(jnp.int32, head.shape, 1)
        heads[pl.ds(pl.multiple_of(at * block, 32), block), :] = jnp.where(
            lane < L - block, head, jnp.zeros_like(head)
        )
        for side in range(L // block):
            @pl.when(at == q * (L // block) + side)
            def _():
                value = piece[n1 + n2 : n1 + n2 + 16, L - block :].astype(f32)
                params[:, side * block : (side + 1) * block] = value


def assemble(q_ref, p0, p1, p2, p3, *outs):
    q = q_ref[0]
    for j, part in enumerate((p0, p1, p2, p3)):
        cols = pl.ds(pl.multiple_of((q ^ j) * L, L), L)
        at = 0
        for out in outs:
            out[:, cols] = part[at : at + out.shape[0], :].astype(f32)
            at += out.shape[0]


def assemble_last(block, tasks, q_ref, p0, p1, p2, p3, *refs):
    *outs, gains, biases, heads, wide = refs
    assemble(q_ref, p0, p1, p2, p3, *outs, wide)
    start = q_ref[1] * block
    own = wide[:, pl.ds(pl.multiple_of(start // L * L, L), L)]
    value = own[:, :block]
    for k in range(1, L // block):
        value = jnp.where(start % L == k * block, own[:, k * block : (k + 1) * block], value)
    heads[...] = value[0:tasks, :]
    for out, side in ((gains, 0), (biases, 1)):
        rows = [tasks + side, tasks + 2 + side] + [tasks + 8 * k + side for k in (1, 2, 3)]
        out[...] = jnp.concatenate([value[r : r + 1, :] for r in rows], axis=0)


def input_grad_kernel(q_ref, order_ref, big_ref, parts, out):
    images = order_ref.shape[1]
    im = images
    wide = out.shape[1]
    spot = lax.broadcasted_iota(jnp.int32, (images, images), 1)
    pick = jnp.where(spot == jnp.transpose(jnp.broadcast_to(order_ref[0:1, :], (images, images))), 1.0, 0.0)
    pick = pick.astype(bf16)
    big = big_ref[0:1, :]
    for pr in range(2):
        for i in range(16):
            at = 16 * pr + i
            value = masked(tn_dot(blk(parts, at, im), pick), i, big)
            for pc in range(2):
                pixel = (2 * (i // 4) + pr) * 8 + 2 * (i % 4) + pc
                out[pixel, :, :] = value[pc * wide : (pc + 1) * wide, :]


def body(
    features, buckets, micro_order, labels, conv_first, conv_short, conv_second, conv_third, conv_fourth,
    norm_gains, norm_biases, head_weight, head_bias,
):
    ia, ib, iz, ic = (lax.axis_index(n) for n in ("a", "b", "z", "c"))
    n_group = lax.axis_size("z") * lax.axis_size("c")
    images, grid, _, cin = features.shape
    channels = conv_second.shape[1]
    tasks = head_weight.shape[1]
    quarter = 2 * ib + ic
    shared = 2 * ib + ia
    im = images
    nm = MICRO
    rows = 16 * im
    own = ia == ic
    q_arr = jnp.stack([quarter, own, ia, iz]).astype(jnp.int32)
    c_arr = jnp.stack([ic, ib]).astype(jnp.int32)

    block = channels // n_group
    r_first, r_short = conv_first.shape[0], conv_short.shape[0]
    n_z = lax.axis_size("z")

    small_rows = max(16, block)
    norms = jnp.concatenate([norm_gains, norm_biases], axis=0)
    norms = jnp.pad(norms, ((0, 6), (0, 0)))
    heads = jnp.pad(head_weight, ((0, small_rows - block), (0, L - tasks)))
    slot_rows = r_first + r_short + small_rows
    piece_t = sds(slot_rows, L, dtype=bf16)
    quarter_t = sds(conv_second.shape[0], L, dtype=bf16)
    pack_arr = jnp.stack([quarter, shared]).astype(jnp.int32)
    mine, give = call(pack, [piece_t, piece_t], (pack_arr, conv_first, conv_short, norms, heads))
    rest = call(
        pack_rest, [quarter_t] * 3, (pack_arr, conv_second, conv_third, conv_fourth), ties=(give,)
    )
    rest = [lax.all_gather(w, ("z", "c"), axis=0, tiled=True) for w in rest]
    piece = jnp.where(own, mine, flip(give, "c"))

    parts = [piece]
    if n_z == 4:
        parts += [lax.ppermute(piece, "z", [(i, i ^ m) for i in range(n_z)]) for m in range(1, n_z)]

    ints = jnp.concatenate(
        [
            labels,
            buckets[:, None],
            micro_order.reshape(images, 1),
            jnp.zeros((images, L - tasks - 2), jnp.int32),
        ],
        axis=1,
    )
    ints = jnp.where(own, ints, flip(ints, "c"))
    order = ints[:, tasks + 1]
    flat = features.reshape(images * grid * grid, cin)
    (feats,) = call(
        prepare,
        [sds(images * grid * grid, cin, dtype=bf16)],
        (q_arr, order[None], Pick(flat, flip(flat, "c"))),
        [pltpu.VMEM((images * grid * grid, L), f32)] * (cin // L),
        scalars=2,
    )

    if n_z == 4:
        (stack,) = call(
            relay, [sds(n_z * slot_rows, L, dtype=bf16)], parts, scalars=0, ties=(feats,)
        )
        w_first, w_short, params, head_all = call(
            functools.partial(unpack, r_first, r_short, block),
            [
                sds(n_group * r_first, L, dtype=bf16),
                sds(n_group * r_short, L, dtype=bf16),
                sds(16, L),
                sds(channels, L, dtype=bf16),
            ],
            (jnp.stack([2 * iz + ia, quarter]).astype(jnp.int32), stack, flip(stack, "a")),
        )
    else:
        packed = lax.all_gather(piece, ("z", "a"), axis=0)
        w_first = packed[:, :r_first].reshape(n_group * r_first, L)
        w_short = packed[:, r_first : r_first + r_short].reshape(n_group * r_short, L)
        small = packed[:, r_first + r_short :]
        head_all = small[:, :block].reshape(channels, L)
        lane = lax.broadcasted_iota(jnp.int32, head_all.shape, 1)
        head_all = jnp.where(lane < tasks, head_all, jnp.zeros_like(head_all))
        params = small[:, :16, L - block :].transpose(1, 0, 2).reshape(16, channels)
        params = lax.dynamic_slice_in_dim(params, quarter * L, L, 1).astype(f32)
    head_mine = lax.dynamic_slice_in_dim(head_all, quarter * L, L, 0)
    bias_row = jnp.broadcast_to(
        jnp.pad(head_bias.astype(f32), (0, L - tasks))[None, :], (8, L)
    )

    own_big = jnp.broadcast_to(buckets[None, :].astype(f32), (8, images))
    ints = ints[order]
    label_rows = ints.astype(f32)
    big = jnp.broadcast_to(ints[:, tasks : tasks + 1].astype(f32), (images, L))

    act = sds(rows, L, dtype=bf16)
    full = sds(rows, L)
    img = sds(im, L)
    micro = sds(8, L)
    kept = Keep(rows, L)
    low_kept = Keep(rows, L, dtype=bf16)
    vm = pltpu.VMEM
    conv_scratch = [vm((4 * L, 9 * L), bf16), vm((rows, 9 * L), f32), vm((rows, L), f32)]
    wide_kept = Keep(rows, 4 * L, dtype=bf16)
    back_scratch = [vm((4 * L, 9 * L), bf16), vm((rows, 9 * L), bf16), vm((rows, L), f32)]
    flops_conv = 2 * rows * 4 * L * 9 * L

    def run(kernel, outs, args, scratch, flops=flops_conv, ties=(), through=()):
        return call(functools.partial(kernel, nm), outs, args, scratch, 1, flops, ties, through)

    *first, w_second = run(
        first_forward,
        [act, low_kept, kept, micro, kept, micro],
        (q_arr, feats, w_first, w_short, params, big),
        [vm((rows, cin), bf16), vm((cin, 10 * L), bf16), vm((rows, 10 * L), f32), vm((rows, L), f32), vm((rows, L), f32)],
        through=(rest[0],),
    )
    w_second, w_third, w_fourth = [Pick(w, swap_ac(w)) for w in (w_second, rest[1], rest[2])]
    h1 = gather_quarters(first[0])
    second = run(
        second_forward,
        [act, kept, micro, wide_kept],
        (q_arr, *h1, w_second, params, big, first[1]),
        conv_scratch,
    )
    x2 = gather_quarters(second[0])
    third = run(third_forward, [act, kept, micro, wide_kept], (q_arr, *x2, w_third, params, big), conv_scratch)
    h3 = gather_quarters(third[0])
    fourth = run(
        fourth_forward,
        [img, img, kept, micro, wide_kept],
        (q_arr, *h3, w_fourth, params, big, second[0], head_mine),
        conv_scratch,
    )
    pooled, logits = fourth[:2]

    logits = logits + flip(logits, "c")
    stat_rows = tasks + 8
    errors, stats = call(
        lambda mine, other, bias, lab, err, st: head_errors(mine, other, bias, lab, tasks, err, st),
        [sds(images, L), sds(stat_rows, L)],
        (logits, flip(logits, "b"), bias_row, label_rows),
        scalars=0,
    )
    stats = sum_over(sum_over(stats, "a"), "z")
    direct = n_z == 4
    quads = [low_kept] * 4
    own_rows = 9 * channels // n_group
    shared_arr = shared[None].astype(jnp.int32)

    def grad_of(acts, grad, ties, block=0):
        whole = 9 * channels
        out = call(
            functools.partial(weight_grad, block),
            [Keep(whole // 2, L, dtype=bf16)] * 2 if block else [Keep(whole, L, dtype=bf16)],
            (q_arr, acts, grad),
            [vm((rows, 9 * L), bf16)] + ([vm((whole, L), bf16)] if block else []),
            1,
            flops_conv,
            ties,
        )
        return out if block else out[0]

    def over_z(grad):
        return lax.psum_scatter(grad, "z", scatter_dimension=0, tiled=True)

    def to_places(shard):
        parts = []
        for m in range(4):
            pairs = [
                (4 * i + 2 * j + k, 4 * (k ^ (m & 1)) + 2 * (j ^ (m >> 1)) + i)
                for i in range(2)
                for j in range(2)
                for k in range(2)
            ]
            parts.append(lax.ppermute(shard, ("a", "b", "c"), pairs))
        return parts

    *b4, bias_grad, head_grad = call(
        functools.partial(heads_and_fourth, float(images * n_group), tasks, nm),
        [*quads, low_kept, low_kept, sds(8, L), sds(8, L), sds(tasks, L)],
        (
            q_arr, stats, errors, head_all, head_mine, pooled,
            fourth[2], fourth[3], second[0], w_fourth, params, big,
        ),
        back_scratch + [vm((images, L), f32)],
        flops=flops_conv,
    )
    g3 = scatter_quarters(b4[:4])
    dw4 = grad_of(fourth[4], b4[4], (g3[3],))
    *b3, dw4 = run(
        third_backward,
        [*quads, low_kept, sds(8, L)],
        (q_arr, *g3[:3], third[1], third[2], w_third, params, big),
        back_scratch,
        through=(dw4,),
    )
    r4 = over_z(dw4)
    g2 = scatter_quarters(b3[:4])
    dw3 = grad_of(third[3], b3[4], (g2[3],))
    *b2, dw3 = run(
        second_backward,
        [*quads, low_kept, low_kept, sds(8, L)],
        (q_arr, *g2[:3], b4[5], first[1], second[1], second[2], w_second, params, big),
        back_scratch,
        through=(dw3,),
    )
    r3 = over_z(dw3)
    g1 = scatter_quarters(b2[:4])
    dw2 = grad_of(second[3], b2[4], (g1[3],), own_rows if direct else 0)
    if direct:
        dw2, give2 = dw2
        got2 = flip(give2, "a")
    twice = [Keep(2 * rows, L, dtype=bf16)] * 3 + [low_kept] * 2
    b1 = run(
        first_backward,
        [*twice, low_kept, low_kept, sds(8, L)],
        (c_arr, *g1[:3], b2[5], *first[2:], w_first, w_short, params, big),
        [vm((cin, 10 * L), bf16), vm((rows, 10 * L), bf16), vm((rows, L), f32)],
        ties=(dw2,),
    )

    p0, p1, p2, *p3 = b1[:5]
    p1, p3 = flip(p1, "c"), [flip(p, "c") for p in p3]
    (send,) = call(
        add_halves,
        [sds(2 * rows, L, dtype=bf16)],
        (p2, *p3),
        scalars=0,
        ties=(got2,) if direct else (),
    )
    across = flip(send, "b")
    smalls = [head_grad, b1[-1], b2[-1], b3[-1], b4[-1]]
    small_rows = sum(v.shape[0] for v in smalls)
    smalls.append(jnp.zeros((-small_rows % 16 or 16, L), f32))
    small_rows += smalls[-1].shape[0]
    slot_rows = r_first + r_short + small_rows
    grad_args = (q_arr, feats, b1[5], b1[6], big)
    grad_scratch = [vm((rows, cin), bf16), vm((rows, 10 * L), bf16)]

    def low(count):
        return sds(count, L, dtype=bf16)

    def give_a(shards, sizes, ties):
        count = sum(sizes)
        keep, give = call(
            functools.partial(pick_a, sizes), [low(count)] * 2, (q_arr, *shards), ties=ties
        )
        return keep, flip(give, "a")

    def sum_a(keep, got, ties=()):
        return call(add_low, [low(keep.shape[0])], (keep, got), scalars=0, ties=ties)[0]

    if direct:
        slots, give1 = call(
            functools.partial(first_weight_grad, (r_first, r_short)),
            [Keep(n_group * slot_rows // 2, L, dtype=bf16)] * 2,
            grad_args + tuple(smalls),
            grad_scratch + [vm((n_group * slot_rows, L), bf16)],
            ties=(send,),
        )
        got1 = flip(give1, "a")
        pair43 = give_a((r4, r3), (own_rows, own_rows), (slots,))
        (total,) = call(add_three, [low(2 * rows)], (p0, p1, across), scalars=0, ties=(pair43[0],))
        (dw21,) = call(
            functools.partial(sum_beside, n_z),
            [Keep(n_z * (own_rows + slot_rows), L, dtype=bf16)],
            (dw2, got2, slots, got1),
            scalars=0,
            ties=(total,),
        )
        shard21 = over_z(dw21)
    else:
        dw1, dws = call(
            functools.partial(first_weight_grad, None),
            [sds(9 * cin, L, dtype=bf16), sds(cin, L, dtype=bf16)],
            grad_args,
            grad_scratch,
        )
        small = jnp.concatenate(smalls, axis=0).astype(bf16)
        dw21 = [
            dw2.reshape(n_group, own_rows, L),
            dw1.reshape(n_group, r_first, L),
            dws.reshape(n_group, r_short, L),
            jnp.broadcast_to(small[None], (n_group, *small.shape)),
        ]
        dw21 = jnp.concatenate(dw21, axis=1)
        shard21 = lax.psum_scatter(dw21, ("z", "a"), scatter_dimension=0)
        pair43 = give_a((r4, r3), (own_rows, own_rows), ())
        (total,) = call(add_three, [low(2 * rows)], (p0, p1, across), scalars=0)

    shard43 = sum_a(*pair43, ties=(dw21,))
    places43 = to_places(shard43)
    swapped = swap_ac(total)
    conv_fourth_grad, conv_third_grad = call(
        assemble, [sds(own_rows, channels)] * 2, (shared_arr, *places43)
    )
    (input_grad,) = call(
        input_grad_kernel,
        [sds(grid * grid, cin // 4, images)],
        (q_arr, micro_order, own_big, Pick(total, swapped)),
        ties=(conv_third_grad,),
    )
    places = to_places(shard21)
    group = 2 * iz + ic
    group_arr = jnp.stack([shared, group]).astype(jnp.int32)
    wide_outs = [sds(own_rows, channels), sds(r_first, channels), sds(r_short, channels)]
    if direct:
        conv_second_grad, conv_first_grad, conv_short_grad, gains_grad, biases_grad, head_weight_grad = call(
            functools.partial(assemble_last, block, tasks),
            wide_outs + [sds(5, block), sds(5, block), sds(tasks, block)],
            (group_arr, *places),
            [vm((small_rows, channels), f32)],
        )
    else:
        conv_second_grad, conv_first_grad, conv_short_grad, wide_small = call(
            assemble, wide_outs + [sds(small_rows, channels)], (group_arr, *places)
        )
        own_small = lax.dynamic_slice_in_dim(wide_small, group * block, block, 1)
        head_weight_grad = own_small[:tasks]
        n1, n2, n3, n4 = (own_small[tasks + 8 * i : tasks + 8 * (i + 1)] for i in range(4))
        gains_grad = jnp.stack([n1[0], n1[2], n2[0], n3[0], n4[0]])
        biases_grad = jnp.stack([n1[1], n1[3], n2[1], n3[1], n4[1]])
    input_grad = input_grad.reshape(grid, grid, cin // 4, images).transpose(3, 0, 1, 2)

    moved = lax.ppermute(
        pooled,
        ("a", "b", "c"),
        [(4 * i + 2 * j + k, 4 * j + 2 * k + i) for i in range(2) for j in range(2) for k in range(2)],
    )
    spots = jnp.arange(images, dtype=jnp.int32)
    inverse = jnp.sum(
        jnp.where(micro_order[0][None, :] == spots[:, None], spots[None, :], 0), axis=1
    )
    pooled_out = moved[inverse]

    return (
        pooled_out,
        input_grad,
        conv_first_grad,
        conv_short_grad,
        conv_second_grad,
        conv_third_grad,
        conv_fourth_grad,
        gains_grad,
        biases_grad,
        head_weight_grad.T,
        bias_grad[0, :tasks],
    )


def solution(mesh):
    sections, groups = mesh.shape["section"], mesh.shape["dp"]
    fine = Mesh(mesh.devices.reshape(2, sections // 2, groups // 2, 2), ("a", "b", "z", "c"))
    dp, section = ("z", "c"), ("a", "b")
    return jax.shard_map(
        body,
        mesh=fine,
        in_specs=(
            P(dp, None, None, None),
            P(dp),
            P(dp, None),
            P(dp, None),
            P(dp, None),
            P(dp, None),
            P(dp, None),
            P(dp, None),
            P(dp, None),
            P(None, dp),
            P(None, dp),
            P(dp, None),
            P(),
        ),
        out_specs=(
            P(dp, section),
            P(dp, None, None, section),
            P(dp, None),
            P(dp, None),
            P(dp, None),
            P(dp, None),
            P(dp, None),
            P(None, dp),
            P(None, dp),
            P(dp, None),
            P(),
        ),
        check_vma=False,
    )
```

```python
import functools

import jax
import jax.numpy as jnp
from jax import lax
from jax.experimental import pallas as pl
from jax.experimental.pallas import tpu as pltpu
from jax.sharding import Mesh, PartitionSpec as P

MICRO = 6
FW_STEPS = 20
EPSILON = 1e-05
SOFTMAX_HEAT = 0.01
HIGHEST = lax.Precision.HIGHEST

f32 = jnp.float32
bf16 = jnp.bfloat16
L = 128

PLANE_TAPS = ((4, -1), (3, 5), (1, 7), (0, 2, 6, 8))
FIRST_COLS = tuple(tap for taps in PLANE_TAPS for tap in taps)


VMEM_MB = 51


class Keep:
    def __init__(self, *shape, dtype=f32):
        self.shape, self.dtype = shape, dtype


class Far:
    def __init__(self, x):
        self.first, self.shape, self.dtype, self.size = x, x.shape, x.dtype, x.size


class Pick:
    def __init__(self, first, other):
        self.first, self.other = first, other
        self.shape, self.dtype, self.size = first.shape, first.dtype, first.size


class Buf:
    def __init__(self, ref, start, wait, out=False):
        self.ref, self.start, self.wait = ref, start, wait
        self.out, self.started, self.ready = out, not out, out
        self.shape, self.dtype = ref.shape, ref.dtype
        if not out:
            start()

    def get(self):
        if not self.ready:
            self.wait()
            self.ready = True

    def __getitem__(self, at):
        self.get()
        return self.ref[at]

    def __setitem__(self, at, value):
        self.ref[at] = value

    def send(self):
        if not self.started:
            self.start()
            self.started = True


def call(kernel, outs, args, scratch=(), scalars=1, flops=0, ties=(), through=()):
    def far(a):
        return isinstance(a, (Far, Pick, Keep))

    flat, specs, places = [], [], []
    for k, a in enumerate(args):
        places.append(len(flat))
        if k < scalars:
            space = pltpu.SMEM
        else:
            space = pltpu.HBM if far(a) else pltpu.VMEM
        for x in (a.first, a.other) if isinstance(a, Pick) else (a.first,) if far(a) else (a,):
            flat.append(x)
            specs.append(pl.BlockSpec(memory_space=space))
    n_args = len(flat)
    specs += [pl.BlockSpec(memory_space=pl.ANY)] * (len(ties) + len(through))
    far_in = [k for k, a in enumerate(args) if k >= scalars and far(a)]
    far_out = [k for k, o in enumerate(outs) if far(o)]
    buffers = [pltpu.VMEM(args[k].shape, args[k].dtype) for k in far_in]
    buffers += [pltpu.VMEM(outs[k].shape, outs[k].dtype) for k in far_out]
    n_in = n_args + len(ties) + len(through)
    n_outs = len(outs)
    n_bufs = len(buffers)

    def run(*refs):
        ins, results = list(refs[:n_args]), list(refs[n_in : n_in + n_outs])
        rest = refs[n_in + n_outs + len(through) :]
        temps, sems, rest = rest[:n_bufs], rest[n_bufs], rest[n_bufs + 1 :]
        given = []
        for k in range(len(args)):
            src = ins[places[k]]
            if k in far_in:
                n = far_in.index(k)
                copy = pltpu.make_async_copy(src, temps[n], sems.at[n])
                start = copy.start
                if isinstance(args[k], Pick):
                    second = pltpu.make_async_copy(ins[places[k] + 1], temps[n], sems.at[n])

                    def start(copy=copy, second=second):
                        pl.when(ins[0][1] == 1)(copy.start)
                        pl.when(ins[0][1] == 0)(second.start)

                src = Buf(temps[n], start, copy.wait)
            given.append(src)
        made = []
        for k in range(n_outs):
            out = results[k]
            if k in far_out:
                n = len(far_in) + far_out.index(k)
                copy = pltpu.make_async_copy(temps[n], out, sems.at[n])
                out = Buf(temps[n], copy.start, copy.wait, out=True)
            made.append(out)
        kernel(*given, *made, *rest)
        for x in given:
            if isinstance(x, Buf):
                x.get()
        made = [x for x in made if isinstance(x, Buf)]
        for x in made:
            x.send()
        for x in made:
            x.wait()

    outs = [sds(*o.shape, dtype=o.dtype) if far(o) else o for o in outs]
    size = sum(a.size * a.dtype.itemsize for a in flat) + sum(o.size * o.dtype.itemsize for o in outs)
    return pl.pallas_call(
        run,
        out_shape=tuple(outs) + tuple(sds(*x.shape, dtype=x.dtype) for x in through),
        in_specs=specs,
        out_specs=tuple(
            pl.BlockSpec(memory_space=pltpu.HBM if k in far_out else pltpu.VMEM) for k in range(n_outs)
        )
        + tuple(pl.BlockSpec(memory_space=pl.ANY) for _ in through),
        scratch_shapes=buffers + [pltpu.SemaphoreType.DMA((max(n_bufs, 1),))] + list(scratch),
        input_output_aliases={n_args + len(ties) + k: n_outs + k for k in range(len(through))},
        compiler_params=pltpu.CompilerParams(vmem_limit_bytes=VMEM_MB << 20),
        cost_estimate=pl.CostEstimate(flops=int(flops), bytes_accessed=int(size), transcendentals=0),
    )(*flat, *ties, *through)


def sds(*shape, dtype=f32):
    return jax.ShapeDtypeStruct(shape, dtype)


def nt_dot(x, y):
    return lax.dot_general(x, y, (((1,), (1,)), ((), ())), preferred_element_type=f32)


def tn_dot(x, y):
    return lax.dot_general(x, y, (((0,), (0,)), ((), ())), preferred_element_type=f32)


def sigmoid(v):
    return 0.5 + 0.5 * jnp.tanh(0.5 * v)


def pixel_mask(i, big):
    return None if (i // 4 < 2 and i % 4 < 2) else big


def masked(value, i, big):
    return value if pixel_mask(i, big) is None else value * big


def per_micro(value, nm):
    rows, lanes = value.shape
    return jnp.sum(value.reshape(nm, rows // nm, lanes), axis=1)


def spread_micro(value, im):
    nm, lanes = value.shape
    return jnp.broadcast_to(value[:, None, :], (nm, im // nm, lanes)).reshape(im, lanes)


def blk(ref, i, im):
    return ref[i * im : (i + 1) * im, :]


def norm_forward(p_ref, xhat_ref, inv_ref, big, nm):
    im = big.shape[0]
    total = per_micro(4.0 + 12.0 * big, nm)
    acc = jnp.zeros_like(big)
    for i in range(16):
        acc = acc + masked(blk(p_ref, i, im), i, big)
    mean = spread_micro(per_micro(acc, nm) / total, im)
    acc = jnp.zeros_like(big)
    for i in range(16):
        cen = blk(p_ref, i, im) - mean
        acc = acc + masked(cen * cen, i, big)
    inv = lax.rsqrt(per_micro(acc, nm) / total + EPSILON)
    inv_ref[...] = jnp.concatenate([inv, jnp.zeros((8 - nm, inv.shape[1]), f32)], axis=0)
    inv = spread_micro(inv, im)
    for i in range(16):
        xhat = (blk(p_ref, i, im) - mean) * inv
        p_ref[i * im : (i + 1) * im, :] = xhat
        xhat_ref[i * im : (i + 1) * im, :] = xhat.astype(bf16)


def norm_backward(dy_ref, xhat_ref, inv_ref, gain, big, nm, out_ref):
    im = big.shape[0]
    total = per_micro(4.0 + 12.0 * big, nm)
    sum_dy = jnp.zeros_like(big)
    sum_dx = jnp.zeros_like(big)
    for i in range(16):
        dy = blk(dy_ref, i, im)
        sum_dy = sum_dy + dy
        sum_dx = sum_dx + dy * blk(xhat_ref, i, im).astype(f32)
    sum_dy = per_micro(sum_dy, nm)
    sum_dx = per_micro(sum_dx, nm)
    mean_dy = spread_micro(sum_dy / total, im)
    mean_dx = spread_micro(sum_dx / total, im)
    scale = spread_micro(inv_ref[0:nm, :] * gain, im)
    for i in range(16):
        off = masked(mean_dy + blk(xhat_ref, i, im).astype(f32) * mean_dx, i, big)
        grad = scale * (blk(dy_ref, i, im) - off)
        out_ref[i * im : (i + 1) * im, :] = grad.astype(bf16)
    return jnp.sum(sum_dx, axis=0, keepdims=True), jnp.sum(sum_dy, axis=0, keepdims=True)


def load_weights(q_ref, w_ref, ws):
    channels = 4 * L
    q = q_ref[0]
    for t in range(9):
        for j in range(4):
            start = pl.multiple_of(t * channels + (q ^ j) * L, L)
            ws[j * L : (j + 1) * L, t * L : (t + 1) * L] = w_ref[pl.ds(start, L), :]


def row_taps(r):
    return (3 * L if r == 3 else 0), (6 * L if r == 0 else 9 * L)


def conv_forward(q_ref, x_refs, w_ref, xs, ws, y, p, im):
    for j in (0, 1, 3, 2):
        xs[:, j * L : (j + 1) * L] = x_refs[j][...]
    xs.send()
    load_weights(q_ref, w_ref, ws)
    for r in range(4):
        lo, hi = row_taps(r)
        rows = slice(r * 4 * im, (r + 1) * 4 * im)
        y[rows, lo:hi] = jnp.dot(xs[rows, :], ws[:, lo:hi], preferred_element_type=f32)
    for r in range(4):
        for c in range(4):
            acc = None
            for t in range(9):
                ri, ci = r + t // 3 - 1, c + t % 3 - 1
                if 0 <= ri < 4 and 0 <= ci < 4:
                    i = ri * 4 + ci
                    term = y[i * im : (i + 1) * im, t * L : (t + 1) * L]
                    acc = term if acc is None else acc + term
            p[(r * 4 + c) * im : (r * 4 + c + 1) * im, :] = acc


def spread_taps(dp_ref, d, im, rows_at, all_taps):
    for r in range(4):
        lo, hi = (0, 9 * L) if all_taps else row_taps(r)
        for c in range(4):
            at = rows_at + (r * 4 + c) * im
            for t in range(lo // L, hi // L):
                ro, co = r - t // 3 + 1, c - t % 3 + 1
                if 0 <= ro < 4 and 0 <= co < 4:
                    value = blk(dp_ref, ro * 4 + co, im)
                else:
                    value = jnp.zeros((im, L), bf16)
                d[at : at + im, t * L : (t + 1) * L] = value


def conv_back_input(q_ref, dp_ref, w_ref, ws, d, outs, im):
    load_weights(q_ref, w_ref, ws)
    spread_taps(dp_ref, d, im, 0, False)
    for r in range(4):
        lo, hi = row_taps(r)
        rows = slice(r * 4 * im, (r + 1) * 4 * im)
        dx = nt_dot(d[rows, lo:hi], ws[:, lo:hi])
        for j in range(4):
            outs[j][rows, :] = dx[:, j * L : (j + 1) * L].astype(outs[j].dtype)


def load_plane(x, k, big, xs, im):
    wide = jnp.concatenate([big, big], axis=1).astype(bf16)
    for i in range(16):
        pixel = (2 * (i // 4) + k // 2) * 8 + 2 * (i % 4) + k % 2
        xs[i * im : (i + 1) * im, :] = masked(blk(x, pixel, im), i, wide)


def first_forward(nm, c_ref, x, w, w_short, params, big_ref, h, s, xh1, inv1, xh2, inv2, xs, wsc, y, p1, p2):
    big = big_ref[...]
    im = big.shape[0]
    cin = 2 * L
    col = 0
    for k, taps in enumerate(PLANE_TAPS):
        for n, t in enumerate(taps):
            src = w_short[...] if t < 0 else w[t * cin : (t + 1) * cin, :]
            wsc[:, (col + n) * L : (col + n + 1) * L] = src
        cols = slice(col * L, (col + len(taps)) * L)
        load_plane(x, k, big, xs, im)
        y[:, cols] = jnp.dot(xs[...], wsc[:, cols], preferred_element_type=f32)
        col += len(taps)
    for r in range(4):
        for c in range(4):
            o = r * 4 + c
            acc = None
            for n, t in enumerate(FIRST_COLS):
                if t < 0:
                    p2[o * im : (o + 1) * im, :] = y[o * im : (o + 1) * im, n * L : (n + 1) * L]
                    continue
                ri = r - 1 if t // 3 == 0 else r
                ci = c - 1 if t % 3 == 0 else c
                if ri >= 0 and ci >= 0:
                    i = ri * 4 + ci
                    term = y[i * im : (i + 1) * im, n * L : (n + 1) * L]
                    acc = term if acc is None else acc + term
            p1[o * im : (o + 1) * im, :] = acc
    norm_forward(p1, xh1, inv1, big, nm)
    norm_forward(p2, xh2, inv2, big, nm)
    for i in range(16):
        rows = slice(i * im, (i + 1) * im)
        v = blk(p1, i, im) * params[0:1, :] + params[5:6, :]
        h[rows, :] = masked(v * sigmoid(v), i, big).astype(bf16)
        v = blk(p2, i, im) * params[1:2, :] + params[6:7, :]
        s[rows, :] = masked(v, i, big).astype(bf16)


def second_forward(nm, q_ref, x0, x1, x2, x3, w, params, big_ref, s, out, xh, inv, xs, ws, y, p):
    big = big_ref[...]
    im = big.shape[0]
    conv_forward(q_ref, (x0, x1, x2, x3), w, xs, ws, y, p, im)
    norm_forward(p, xh, inv, big, nm)
    for i in range(16):
        rows = slice(i * im, (i + 1) * im)
        u = blk(p, i, im) * params[2:3, :] + params[7:8, :]
        u = masked(u, i, big).astype(bf16).astype(f32)
        v = u + s[rows, :].astype(f32)
        out[rows, :] = masked(v * sigmoid(v), i, big).astype(bf16)


def third_forward(nm, q_ref, x0, x1, x2, x3, w, params, big_ref, out, xh, inv, xs, ws, y, p):
    big = big_ref[...]
    im = big.shape[0]
    conv_forward(q_ref, (x0, x1, x2, x3), w, xs, ws, y, p, im)
    norm_forward(p, xh, inv, big, nm)
    for i in range(16):
        rows = slice(i * im, (i + 1) * im)
        v = blk(p, i, im) * params[3:4, :] + params[8:9, :]
        out[rows, :] = masked(v * sigmoid(v), i, big).astype(bf16)


def fourth_forward(
    nm, q_ref, x0, x1, x2, x3, w, params, big_ref, res, head, pooled, logits, xh, inv, xs, ws, y, p
):
    big = big_ref[...]
    im = big.shape[0]
    conv_forward(q_ref, (x0, x1, x2, x3), w, xs, ws, y, p, im)
    norm_forward(p, xh, inv, big, nm)
    acc = jnp.zeros_like(big)
    for i in range(16):
        rows = slice(i * im, (i + 1) * im)
        v = blk(p, i, im) * params[4:5, :] + params[9:10, :] + res[rows, :].astype(f32)
        acc = acc + masked(v * sigmoid(v), i, big)
    pool = acc / (4.0 + 12.0 * big)
    pooled[...] = pool
    logits[...] = jnp.dot(pool.astype(bf16), head[...], preferred_element_type=f32)


def head_errors(mine, other, bias, labels, tasks, errors, stats):
    logits = mine[...] + other[...] + bias[0:1, :]
    lane = lax.broadcasted_iota(jnp.int32, logits.shape, 1)
    err = jnp.where(lane < tasks, sigmoid(logits) - labels[...], 0.0)
    errors[...] = err
    gram = lax.dot_general(err, err, (((0,), (0,)), ((), ())), precision=HIGHEST, preferred_element_type=f32)
    stats[0:tasks, :] = gram[0:tasks, :]
    stats[tasks:, :] = jnp.broadcast_to(jnp.sum(err, axis=0, keepdims=True), (stats.shape[0] - tasks, L))


def head_weights(count, tasks, stats, errors, head_all, head_mine, pooled, dz, bias_grad, head_grad):
    inner = tn_dot(head_all[...], head_all[...])
    gram = stats[0:tasks, :] * inner[0:tasks, :] / count
    row = lax.broadcasted_iota(jnp.int32, (tasks, L), 0)
    lane = lax.broadcasted_iota(jnp.int32, (tasks, L), 1)
    weight_row = jnp.where(lane[0:1, :] < tasks, 1.0 / tasks, 0.0)
    for step in range(FW_STEPS):
        score = -jnp.sum(gram * weight_row, axis=1, keepdims=True) / SOFTMAX_HEAT
        power = jnp.exp(score - jnp.max(score, axis=0, keepdims=True))
        corner = power / jnp.sum(power, axis=0, keepdims=True)
        corner = jnp.sum(jnp.where(row == lane, corner, 0.0), axis=0, keepdims=True)
        rate = 2.0 / (step + 2.0)
        weight_row = (1.0 - rate) * weight_row + rate * corner
    scaled = errors[...] * weight_row
    dz[...] = lax.dot_general(
        scaled,
        head_mine[...].astype(f32),
        (((1,), (1,)), ((), ())),
        precision=HIGHEST,
        preferred_element_type=f32,
    )
    bias_grad[...] = jnp.broadcast_to(weight_row * stats[tasks : tasks + 1, :], bias_grad.shape)
    grad = lax.dot_general(
        scaled,
        pooled[...].astype(bf16).astype(f32),
        (((0,), (0,)), ((), ())),
        precision=HIGHEST,
        preferred_element_type=f32,
    )
    head_grad[...] = grad[0:tasks, :]


def fourth_backward(
    nm, q_ref, dz, xh, inv, res, w, params, big_ref, o0, o1, o2, o3, dp, d_res, norm, ws, d, dy
):
    big = big_ref[...]
    im = big.shape[0]
    out_grad = dz[...] / (4.0 + 12.0 * big)
    for i in range(16):
        rows = slice(i * im, (i + 1) * im)
        v = blk(xh, i, im).astype(f32) * params[4:5, :] + params[9:10, :] + res[rows, :].astype(f32)
        sig = sigmoid(v)
        grad = masked(out_grad * (sig * (1.0 + v * (1.0 - sig))), i, big)
        dy[rows, :] = grad
        d_res[rows, :] = grad.astype(bf16)
    dgain, dbias = norm_backward(dy, xh, inv, params[4:5, :], big, nm, dp)
    norm[...] = jnp.concatenate([dgain, dbias, jnp.zeros((6, L), f32)], axis=0)
    conv_back_input(q_ref, dp, w, ws, d, (o0, o1, o2, o3), im)


def heads_and_fourth(
    count, tasks, nm, q_ref, stats, errors, head_all, head_mine, pooled, xh, inv, res, w, params, big_ref,
    o0, o1, o2, o3, dp, d_res, norm, bias_grad, head_grad, ws, d, dy, dz,
):
    head_weights(count, tasks, stats, errors, head_all, head_mine, pooled, dz, bias_grad, head_grad)
    fourth_backward(
        nm, q_ref, dz, xh, inv, res, w, params, big_ref, o0, o1, o2, o3, dp, d_res, norm, ws, d, dy
    )


def third_backward(
    nm, q_ref, g0, g1, g2, xh, inv, w, params, big_ref, o0, o1, o2, o3, dp, norm, ws, d, dy
):
    big = big_ref[...]
    im = big.shape[0]
    for i in range(16):
        rows = slice(i * im, (i + 1) * im)
        grad = g0[rows, :].astype(f32) + g1[rows, :].astype(f32) + g2[rows, :].astype(f32)
        grad = grad.astype(bf16).astype(f32)
        v = blk(xh, i, im).astype(f32) * params[3:4, :] + params[8:9, :]
        sig = sigmoid(v)
        dy[rows, :] = masked(grad * (sig * (1.0 + v * (1.0 - sig))), i, big)
    dgain, dbias = norm_backward(dy, xh, inv, params[3:4, :], big, nm, dp)
    norm[...] = jnp.concatenate([dgain, dbias, jnp.zeros((6, L), f32)], axis=0)
    conv_back_input(q_ref, dp, w, ws, d, (o0, o1, o2, o3), im)


def second_backward(
    nm, q_ref, g0, g1, g2, d_res, s, xh, inv, w, params, big_ref, o0, o1, o2, o3, dp, ds, norm, ws, d, dy
):
    big = big_ref[...]
    im = big.shape[0]
    for i in range(16):
        rows = slice(i * im, (i + 1) * im)
        grad = g0[rows, :].astype(f32) + g1[rows, :].astype(f32) + g2[rows, :].astype(f32)
        grad = grad + d_res[rows, :].astype(f32)
        u = blk(xh, i, im).astype(f32) * params[2:3, :] + params[7:8, :]
        v = masked(u, i, big).astype(bf16).astype(f32) + s[rows, :].astype(f32)
        sig = sigmoid(v)
        grad = masked(grad * (sig * (1.0 + v * (1.0 - sig))), i, big).astype(bf16)
        ds[rows, :] = grad
        dy[rows, :] = grad.astype(f32)
    dgain, dbias = norm_backward(dy, xh, inv, params[2:3, :], big, nm, dp)
    norm[...] = jnp.concatenate([dgain, dbias, jnp.zeros((6, L), f32)], axis=0)
    conv_back_input(q_ref, dp, w, ws, d, (o0, o1, o2, o3), im)


def spread_first(dp1, dps, d, im, rows_at):
    for i in range(16):
        r, c = i // 4, i % 4
        at = rows_at + i * im
        for n, t in enumerate(FIRST_COLS):
            if t < 0:
                value = blk(dps, i, im)
            else:
                ro = r + 1 if t // 3 == 0 else r
                co = c + 1 if t % 3 == 0 else c
                value = blk(dp1, ro * 4 + co, im) if ro < 4 and co < 4 else jnp.zeros((im, L), bf16)
            d[at : at + im, n * L : (n + 1) * L] = value


def first_backward(
    nm, c_ref, g0, g1, g2, ds, xh1, inv1, xh2, inv2, w, w_short, params, big_ref, *refs,
):
    outs, (dp1, dps, norm, ws, d, dy) = refs[:5], refs[5:]
    big = big_ref[...]
    im = big.shape[0]
    half, part = c_ref[0], c_ref[1]
    cin = 2 * L
    for i in range(16):
        rows = slice(i * im, (i + 1) * im)
        grad = g0[rows, :].astype(f32) + g1[rows, :].astype(f32) + g2[rows, :].astype(f32)
        grad = grad.astype(bf16).astype(f32)
        v = blk(xh1, i, im).astype(f32) * params[0:1, :] + params[5:6, :]
        sig = sigmoid(v)
        dy[rows, :] = masked(grad * (sig * (1.0 + v * (1.0 - sig))), i, big)
    gain1, bias1 = norm_backward(dy, xh1, inv1, params[0:1, :], big, nm, dp1)
    for i in range(16):
        rows = slice(i * im, (i + 1) * im)
        dy[rows, :] = masked(ds[rows, :].astype(f32), i, big)
    gain2, bias2 = norm_backward(dy, xh2, inv2, params[1:2, :], big, nm, dps)
    norm[...] = jnp.concatenate([gain1, bias1, gain2, bias2, jnp.zeros((4, L), f32)], axis=0)
    wide = cin // 4
    for n, t in enumerate(FIRST_COLS):
        for j in range(4):
            start = (half ^ (j & 1)) * 2 * wide + (part ^ (j >> 1)) * wide
            if t < 0:
                src = w_short[pl.ds(pl.multiple_of(start, wide), wide), :]
            else:
                src = w[pl.ds(pl.multiple_of(t * cin + start, wide), wide), :]
            ws[j * wide : (j + 1) * wide, n * L : (n + 1) * L] = src
    spread_first(dp1, dps, d, im, 0)
    col = 0
    for k, taps in enumerate(PLANE_TAPS):
        cols = slice(col * L, (col + len(taps)) * L)
        dx = nt_dot(d[:, cols], ws[:, cols])
        pair, side = k // 2, k % 2
        for j in range(4):
            ref = outs[j] if j < 3 else outs[3 + pair]
            at = pair * 16 * im if j < 3 else 0
            rows = slice(at, at + 16 * im)
            ref[rows, side * wide : (side + 1) * wide] = dx[:, j * wide : (j + 1) * wide].astype(ref.dtype)
        col += len(taps)


def halves(whole, outs):
    rows = outs[0].shape[0]
    for k, out in enumerate(outs):
        out[...] = whole[k * rows : (k + 1) * rows, :]


def weight_grad(block, q_ref, x, dp, *refs):
    if block:
        *outs, d, out = refs
    else:
        out, d = refs
    im = dp.shape[0] // 16
    q, a = q_ref[0], q_ref[2]
    total = out.shape[0]
    spread_taps(dp, d, im, 0, True)
    step = L // 2 if block else L
    for n in range(3):
        cols = slice(n * 3 * L, (n + 1) * 3 * L)
        grad = tn_dot(x[...], d[:, cols]).astype(bf16)
        for t in range(3):
            for j in range(4):
                for part in range(L // step):
                    start = (3 * n + t) * 4 * L + (q ^ j) * L + part * step
                    if block:
                        at = start // block
                        start = ((at & 1) ^ a) * (total // 2) + (at // 2) * block + start % block
                    start = pl.multiple_of(start, step)
                    value = grad[j * L + part * step : j * L + (part + 1) * step, t * L : (t + 1) * L]
                    out[pl.ds(start, step), :] = value
    if block:
        halves(out, outs)


def first_weight_grad(blocks, q_ref, x, dp1, dps, big_ref, *refs):
    if blocks:
        *smalls, keep, give, xs, d, out = refs
        small = jnp.concatenate([v[...] for v in smalls], axis=0).astype(bf16)
        n1, n2 = blocks
        per = n1 + n2 + small.shape[0]
        total = out.shape[0]
        a = q_ref[2]
    else:
        out, out_short, xs, d = refs
    big = big_ref[...]
    im = big.shape[0]
    cin = 2 * L

    def place(at):
        return pl.multiple_of(((at & 1) ^ a) * (total // 2) + (at // 2) * per, 16)

    spread_first(dp1, dps, d, im, 0)
    col = 0
    for k, taps in enumerate(PLANE_TAPS):
        cols = slice(col * L, (col + len(taps)) * L)
        load_plane(x, k, big, xs, im)
        grad = tn_dot(xs[...], d[:, cols]).astype(bf16)
        for n, t in enumerate(taps):
            value = grad[:, n * L : (n + 1) * L]
            if not blocks:
                if t < 0:
                    out_short[...] = value
                else:
                    out[t * cin : (t + 1) * cin, :] = value
                continue
            size, base, row = (n2, n1, 0) if t < 0 else (n1, 0, t * cin)
            done = 0
            while done < cin:
                at, inner = (row + done) // size, (row + done) % size
                count = min(cin - done, size - inner)
                start = pl.multiple_of(place(at) + base + inner, 16)
                out[pl.ds(start, count), :] = value[done : done + count, :]
                done += count
        col += len(taps)
    if blocks:
        for at in range(cin // n2):
            start = pl.multiple_of(place(at) + n1 + n2, 16)
            out[pl.ds(start, small.shape[0]), :] = small
        halves(out, (keep, give))


def sum_beside(n_z, x, x_got, y, y_got, out):
    at = 0
    sizes = (x_got.shape[0] // n_z, y_got.shape[0] // n_z)
    for z in range(n_z):
        for kept, got, rows in ((x, x_got, sizes[0]), (y, y_got, sizes[1])):
            cut = slice(z * rows, (z + 1) * rows)
            out[at : at + rows, :] = (kept[cut, :].astype(f32) + got[cut, :].astype(f32)).astype(bf16)
            at += rows


def add_low(x, y, out):
    out[...] = (x[...].astype(f32) + y[...].astype(f32)).astype(bf16)


def add_halves(x, low, high, out):
    rows = low.shape[0]
    for k, y in enumerate((low, high)):
        cut = slice(k * rows, (k + 1) * rows)
        out[cut, :] = (x[cut, :].astype(f32) + y[...].astype(f32)).astype(bf16)


def add_three(x, y, z, out):
    out[...] = (x[...].astype(f32) + y[...].astype(f32) + z[...].astype(f32)).astype(bf16)


def pick_a(sizes, a_ref, *refs):
    *arrays, keep, give = refs
    at, source = 0, 0
    for rows in sizes:
        for out, a in ((keep, a_ref[2]), (give, 1 - a_ref[2])):
            cut = pl.ds(pl.multiple_of(source + a * rows, 8), rows)
            out[at : at + rows, :] = arrays[0][cut, :]
        at, source = at + rows, source + 2 * rows
        if source == arrays[0].shape[0]:
            arrays, source = arrays[1:], 0


def flip(value, axis):
    return lax.ppermute(value, axis, [(i, i ^ 1) for i in range(lax.axis_size(axis))])


def swap_ac(value):
    return lax.ppermute(value, ("a", "c"), [(1, 2), (2, 1)])


def sum_over(value, axis):
    count = lax.axis_size(axis)
    if count & (count - 1):
        return lax.psum(value, axis)
    step = 1
    while step < count:
        value = value + lax.ppermute(value, axis, [(i, i ^ step) for i in range(count)])
        step *= 2
    return value


def gather_quarters(h):
    from_b = flip(h, "b")
    from_c = flip(h, "c")
    return (h, from_c, Far(from_b), flip(from_b, "c"))


def scatter_quarters(parts):
    p0, p1, p2, p3 = parts
    first = flip(p1, "c")
    second = flip(p3, "c")
    send = (p2.astype(f32) + second.astype(f32)).astype(bf16)
    return (p0, first, Far(flip(send, "b")), send)


def pack(q_ref, first, short, norms, heads, mine, give):
    q = q_ref[0]
    n1, n2 = first.shape[0], short.shape[0]
    for out, part in ((mine, q), (give, q ^ 1)):
        cols = pl.ds(pl.multiple_of(part * L, L), L)
        out[0:n1, :] = first[:, cols]
        out[n1 : n1 + n2, :] = short[:, cols]
        out[n1 + n2 :, :] = heads[...]
        out[n1 + n2 : n1 + n2 + norms.shape[0], L - norms.shape[1] :] = norms[...]


def pack_rest(q_ref, *refs):
    cols = pl.ds(pl.multiple_of(q_ref[1] * L, L), L)
    count = len(refs) // 2
    for src, out in zip(refs[:count], refs[count:]):
        out[...] = src[:, cols]


def prepare(q_ref, order_ref, x, out, *bufs):
    images = order_ref.shape[1]
    pixels = out.shape[0] // images
    x.get()

    def move(j, carry):
        source = pl.ds(pl.multiple_of(order_ref[0, j] * pixels, pixels), pixels)
        target = pl.ds(pl.multiple_of(j * pixels, pixels), pixels)
        for k, buf in enumerate(bufs):
            buf[target, :] = x.ref[source, k * L : (k + 1) * L].astype(f32)
        return carry

    lax.fori_loop(0, images, move, 0, unroll=4)
    for p in range(pixels):
        for k, buf in enumerate(bufs):
            value = buf[pl.ds(p, images, stride=pixels), :].astype(bf16)
            out[p * images : (p + 1) * images, k * L : (k + 1) * L] = value


def relay(*refs):
    *parts, out = refs
    rows = parts[0].shape[0]
    for k, part in enumerate(parts):
        out[k * rows : (k + 1) * rows, :] = part[...]


def unpack(n1, n2, block, k_ref, mine, other, first, short, params, heads):
    here, q = k_ref[0], k_ref[1]
    rows = mine.shape[0] // 4
    for k in range(8):
        piece = (mine, other)[k % 2][k // 2 * rows : (k // 2 + 1) * rows, :]
        at = here ^ k
        first[pl.ds(pl.multiple_of(at * n1, 32), n1), :] = piece[0:n1, :]
        short[pl.ds(pl.multiple_of(at * n2, 32), n2), :] = piece[n1 : n1 + n2, :]
        head = piece[n1 + n2 : n1 + n2 + block, :]
        lane = lax.broadcasted_iota(jnp.int32, head.shape, 1)
        heads[pl.ds(pl.multiple_of(at * block, 32), block), :] = jnp.where(
            lane < L - block, head, jnp.zeros_like(head)
        )
        for side in range(L // block):
            @pl.when(at == q * (L // block) + side)
            def _():
                value = piece[n1 + n2 : n1 + n2 + 16, L - block :].astype(f32)
                params[:, side * block : (side + 1) * block] = value


def assemble(q_ref, p0, p1, p2, p3, *outs):
    q = q_ref[0]
    for j, part in enumerate((p0, p1, p2, p3)):
        cols = pl.ds(pl.multiple_of((q ^ j) * L, L), L)
        at = 0
        for out in outs:
            out[:, cols] = part[at : at + out.shape[0], :].astype(f32)
            at += out.shape[0]


def assemble_last(block, tasks, q_ref, p0, p1, p2, p3, *refs):
    *outs, gains, biases, heads, wide = refs
    assemble(q_ref, p0, p1, p2, p3, *outs, wide)
    start = q_ref[1] * block
    own = wide[:, pl.ds(pl.multiple_of(start // L * L, L), L)]
    value = own[:, :block]
    for k in range(1, L // block):
        value = jnp.where(start % L == k * block, own[:, k * block : (k + 1) * block], value)
    heads[...] = value[0:tasks, :]
    for out, side in ((gains, 0), (biases, 1)):
        rows = [tasks + side, tasks + 2 + side] + [tasks + 8 * k + side for k in (1, 2, 3)]
        out[...] = jnp.concatenate([value[r : r + 1, :] for r in rows], axis=0)


def input_grad_kernel(q_ref, order_ref, big_ref, parts, out):
    images = order_ref.shape[1]
    im = images
    wide = out.shape[1]
    spot = lax.broadcasted_iota(jnp.int32, (images, images), 1)
    pick = jnp.where(spot == jnp.transpose(jnp.broadcast_to(order_ref[0:1, :], (images, images))), 1.0, 0.0)
    pick = pick.astype(bf16)
    big = big_ref[0:1, :]
    for pr in range(2):
        for i in range(16):
            at = 16 * pr + i
            value = masked(tn_dot(blk(parts, at, im), pick), i, big)
            for pc in range(2):
                pixel = (2 * (i // 4) + pr) * 8 + 2 * (i % 4) + pc
                out[pixel, :, :] = value[pc * wide : (pc + 1) * wide, :]


def body(
    features, buckets, micro_order, labels, conv_first, conv_short, conv_second, conv_third, conv_fourth,
    norm_gains, norm_biases, head_weight, head_bias,
):
    ia, ib, iz, ic = (lax.axis_index(n) for n in ("a", "b", "z", "c"))
    n_group = lax.axis_size("z") * lax.axis_size("c")
    images, grid, _, cin = features.shape
    channels = conv_second.shape[1]
    tasks = head_weight.shape[1]
    quarter = 2 * ib + ic
    shared = 2 * ib + ia
    im = images
    nm = MICRO
    rows = 16 * im
    own = ia == ic
    q_arr = jnp.stack([quarter, own, ia, iz]).astype(jnp.int32)
    c_arr = jnp.stack([ic, ib]).astype(jnp.int32)

    block = channels // n_group
    r_first, r_short = conv_first.shape[0], conv_short.shape[0]
    n_z = lax.axis_size("z")

    small_rows = max(16, block)
    norms = jnp.concatenate([norm_gains, norm_biases], axis=0)
    norms = jnp.pad(norms, ((0, 6), (0, 0)))
    heads = jnp.pad(head_weight, ((0, small_rows - block), (0, L - tasks)))
    slot_rows = r_first + r_short + small_rows
    piece_t = sds(slot_rows, L, dtype=bf16)
    quarter_t = sds(conv_second.shape[0], L, dtype=bf16)
    pack_arr = jnp.stack([quarter, shared]).astype(jnp.int32)
    rest = call(pack_rest, [quarter_t], (pack_arr, conv_second))
    mine, give = call(
        pack, [piece_t, piece_t], (pack_arr, conv_first, conv_short, norms, heads), ties=rest
    )
    rest += call(pack_rest, [quarter_t] * 2, (pack_arr, conv_third, conv_fourth), ties=(give,))
    rest = [lax.all_gather(w, ("z", "c"), axis=0, tiled=True) for w in rest]
    piece = jnp.where(own, mine, flip(give, "c"))

    parts = [piece]
    if n_z == 4:
        parts += [lax.ppermute(piece, "z", [(i, i ^ m) for i in range(n_z)]) for m in range(1, n_z)]

    ints = jnp.concatenate(
        [
            labels,
            buckets[:, None],
            micro_order.reshape(images, 1),
            jnp.zeros((images, L - tasks - 2), jnp.int32),
        ],
        axis=1,
    )
    ints = jnp.where(own, ints, flip(ints, "c"))
    order = ints[:, tasks + 1]
    flat = features.reshape(images * grid * grid, cin)
    (feats,) = call(
        prepare,
        [sds(images * grid * grid, cin, dtype=bf16)],
        (q_arr, order[None], Pick(flat, flip(flat, "c"))),
        [pltpu.VMEM((images * grid * grid, L), f32)] * (cin // L),
        scalars=2,
    )

    if n_z == 4:
        (stack,) = call(
            relay, [sds(n_z * slot_rows, L, dtype=bf16)], parts, scalars=0, ties=(feats,)
        )
        w_first, w_short, params, head_all = call(
            functools.partial(unpack, r_first, r_short, block),
            [
                sds(n_group * r_first, L, dtype=bf16),
                sds(n_group * r_short, L, dtype=bf16),
                sds(16, L),
                sds(channels, L, dtype=bf16),
            ],
            (jnp.stack([2 * iz + ia, quarter]).astype(jnp.int32), stack, flip(stack, "a")),
        )
    else:
        packed = lax.all_gather(piece, ("z", "a"), axis=0)
        w_first = packed[:, :r_first].reshape(n_group * r_first, L)
        w_short = packed[:, r_first : r_first + r_short].reshape(n_group * r_short, L)
        small = packed[:, r_first + r_short :]
        head_all = small[:, :block].reshape(channels, L)
        lane = lax.broadcasted_iota(jnp.int32, head_all.shape, 1)
        head_all = jnp.where(lane < tasks, head_all, jnp.zeros_like(head_all))
        params = small[:, :16, L - block :].transpose(1, 0, 2).reshape(16, channels)
        params = lax.dynamic_slice_in_dim(params, quarter * L, L, 1).astype(f32)
    head_mine = lax.dynamic_slice_in_dim(head_all, quarter * L, L, 0)
    bias_row = jnp.broadcast_to(
        jnp.pad(head_bias.astype(f32), (0, L - tasks))[None, :], (8, L)
    )

    own_big = jnp.broadcast_to(buckets[None, :].astype(f32), (8, images))
    ints = ints[order]
    label_rows = ints.astype(f32)
    big = jnp.broadcast_to(ints[:, tasks : tasks + 1].astype(f32), (images, L))

    act = sds(rows, L, dtype=bf16)
    full = sds(rows, L)
    img = sds(im, L)
    micro = sds(8, L)
    low_kept = kept = Keep(rows, L, dtype=bf16)
    vm = pltpu.VMEM
    conv_scratch = [vm((4 * L, 9 * L), bf16), vm((rows, 9 * L), f32), vm((rows, L), f32)]
    wide_kept = Keep(rows, 4 * L, dtype=bf16)
    back_scratch = [vm((4 * L, 9 * L), bf16), vm((rows, 9 * L), bf16), vm((rows, L), f32)]
    flops_conv = 2 * rows * 4 * L * 9 * L

    def run(kernel, outs, args, scratch, flops=flops_conv, ties=(), through=()):
        return call(functools.partial(kernel, nm), outs, args, scratch, 1, flops, ties, through)

    *first, w_second = run(
        first_forward,
        [act, low_kept, kept, micro, kept, micro],
        (q_arr, feats, w_first, w_short, params, big),
        [vm((rows, cin), bf16), vm((cin, 10 * L), bf16), vm((rows, 10 * L), f32), vm((rows, L), f32), vm((rows, L), f32)],
        through=(rest[0],),
    )
    w_second, w_third, w_fourth = [Pick(w, swap_ac(w)) for w in (w_second, rest[1], rest[2])]
    h1 = gather_quarters(first[0])
    second = run(
        second_forward,
        [act, kept, micro, wide_kept],
        (q_arr, *h1, w_second, params, big, first[1]),
        conv_scratch,
    )
    x2 = gather_quarters(second[0])
    third = run(third_forward, [act, kept, micro, wide_kept], (q_arr, *x2, w_third, params, big), conv_scratch)
    h3 = gather_quarters(third[0])
    fourth = run(
        fourth_forward,
        [img, img, kept, micro, wide_kept],
        (q_arr, *h3, w_fourth, params, big, second[0], head_mine),
        conv_scratch,
    )
    pooled, logits = fourth[:2]

    logits = logits + flip(logits, "c")
    stat_rows = tasks + 8
    errors, stats = call(
        lambda mine, other, bias, lab, err, st: head_errors(mine, other, bias, lab, tasks, err, st),
        [sds(images, L), sds(stat_rows, L)],
        (logits, flip(logits, "b"), bias_row, label_rows),
        scalars=0,
    )
    stats = sum_over(sum_over(stats, "a"), "z")
    direct = n_z == 4
    quads = [low_kept] * 4
    own_rows = 9 * channels // n_group
    shared_arr = shared[None].astype(jnp.int32)

    def grad_of(acts, grad, ties, block=0):
        whole = 9 * channels
        out = call(
            functools.partial(weight_grad, block),
            [Keep(whole // 2, L, dtype=bf16)] * 2 if block else [Keep(whole, L, dtype=bf16)],
            (q_arr, acts, grad),
            [vm((rows, 9 * L), bf16)] + ([vm((whole, L), bf16)] if block else []),
            1,
            flops_conv,
            ties,
        )
        return out if block else out[0]

    def over_z(grad):
        return lax.psum_scatter(grad, "z", scatter_dimension=0, tiled=True)

    def to_places(shard):
        parts = []
        for m in range(4):
            pairs = [
                (4 * i + 2 * j + k, 4 * (k ^ (m & 1)) + 2 * (j ^ (m >> 1)) + i)
                for i in range(2)
                for j in range(2)
                for k in range(2)
            ]
            parts.append(lax.ppermute(shard, ("a", "b", "c"), pairs))
        return parts

    *b4, bias_grad, head_grad = call(
        functools.partial(heads_and_fourth, float(images * n_group), tasks, nm),
        [*quads, low_kept, low_kept, sds(8, L), sds(8, L), sds(tasks, L)],
        (
            q_arr, stats, errors, head_all, head_mine, pooled,
            fourth[2], fourth[3], second[0], w_fourth, params, big,
        ),
        back_scratch + [vm((images, L), f32)],
        flops=flops_conv,
    )
    g3 = scatter_quarters(b4[:4])
    dw4 = grad_of(fourth[4], b4[4], (g3[3],))
    *b3, dw4 = run(
        third_backward,
        [*quads, low_kept, sds(8, L)],
        (q_arr, *g3[:3], third[1], third[2], w_third, params, big),
        back_scratch,
        through=(dw4,),
    )
    r4 = over_z(dw4)
    g2 = scatter_quarters(b3[:4])
    dw3 = grad_of(third[3], b3[4], (g2[3],))
    *b2, dw3 = run(
        second_backward,
        [*quads, low_kept, low_kept, sds(8, L)],
        (q_arr, *g2[:3], b4[5], first[1], second[1], second[2], w_second, params, big),
        back_scratch,
        through=(dw3,),
    )
    r3 = over_z(dw3)
    g1 = scatter_quarters(b2[:4])
    dw2 = grad_of(second[3], b2[4], (g1[3],), own_rows if direct else 0)
    if direct:
        dw2, give2 = dw2
        got2 = flip(give2, "a")
    twice = [Keep(2 * rows, L, dtype=bf16)] * 3 + [low_kept] * 2
    b1 = run(
        first_backward,
        [*twice, low_kept, low_kept, sds(8, L)],
        (c_arr, *g1[:3], b2[5], *first[2:], w_first, w_short, params, big),
        [vm((cin, 10 * L), bf16), vm((rows, 10 * L), bf16), vm((rows, L), f32)],
        ties=(dw2,),
    )

    p0, p1, p2, *p3 = b1[:5]
    p1, p3 = flip(p1, "c"), [flip(p, "c") for p in p3]
    (send,) = call(
        add_halves,
        [sds(2 * rows, L, dtype=bf16)],
        (p2, *p3),
        scalars=0,
        ties=(got2,) if direct else (),
    )
    across = flip(send, "b")
    smalls = [head_grad, b1[-1], b2[-1], b3[-1], b4[-1]]
    small_rows = sum(v.shape[0] for v in smalls)
    smalls.append(jnp.zeros((-small_rows % 16 or 16, L), f32))
    small_rows += smalls[-1].shape[0]
    slot_rows = r_first + r_short + small_rows
    grad_args = (q_arr, feats, b1[5], b1[6], big)
    grad_scratch = [vm((rows, cin), bf16), vm((rows, 10 * L), bf16)]

    def low(count):
        return sds(count, L, dtype=bf16)

    def give_a(shards, sizes, ties):
        count = sum(sizes)
        keep, give = call(
            functools.partial(pick_a, sizes), [low(count)] * 2, (q_arr, *shards), ties=ties
        )
        return keep, flip(give, "a")

    def sum_a(keep, got, ties=()):
        return call(add_low, [low(keep.shape[0])], (keep, got), scalars=0, ties=ties)[0]

    if direct:
        slots, give1 = call(
            functools.partial(first_weight_grad, (r_first, r_short)),
            [Keep(n_group * slot_rows // 2, L, dtype=bf16)] * 2,
            grad_args + tuple(smalls),
            grad_scratch + [vm((n_group * slot_rows, L), bf16)],
            ties=(send,),
        )
        got1 = flip(give1, "a")
        pair43 = give_a((r4, r3), (own_rows, own_rows), (slots,))
        (total,) = call(add_three, [low(2 * rows)], (p0, p1, across), scalars=0, ties=(pair43[0],))
        (dw21,) = call(
            functools.partial(sum_beside, n_z),
            [Keep(n_z * (own_rows + slot_rows), L, dtype=bf16)],
            (dw2, got2, slots, got1),
            scalars=0,
            ties=(total,),
        )
        shard21 = over_z(dw21)
    else:
        dw1, dws = call(
            functools.partial(first_weight_grad, None),
            [sds(9 * cin, L, dtype=bf16), sds(cin, L, dtype=bf16)],
            grad_args,
            grad_scratch,
        )
        small = jnp.concatenate(smalls, axis=0).astype(bf16)
        dw21 = [
            dw2.reshape(n_group, own_rows, L),
            dw1.reshape(n_group, r_first, L),
            dws.reshape(n_group, r_short, L),
            jnp.broadcast_to(small[None], (n_group, *small.shape)),
        ]
        dw21 = jnp.concatenate(dw21, axis=1)
        shard21 = lax.psum_scatter(dw21, ("z", "a"), scatter_dimension=0)
        pair43 = give_a((r4, r3), (own_rows, own_rows), ())
        (total,) = call(add_three, [low(2 * rows)], (p0, p1, across), scalars=0)

    shard43 = sum_a(*pair43, ties=(dw21,))
    places43 = to_places(shard43)
    swapped = swap_ac(total)
    conv_fourth_grad, conv_third_grad = call(
        assemble, [sds(own_rows, channels)] * 2, (shared_arr, *places43)
    )
    (input_grad,) = call(
        input_grad_kernel,
        [sds(grid * grid, cin // 4, images)],
        (q_arr, micro_order, own_big, Pick(total, swapped)),
        ties=(conv_third_grad,),
    )
    places = to_places(shard21)
    group = 2 * iz + ic
    group_arr = jnp.stack([shared, group]).astype(jnp.int32)
    wide_outs = [sds(own_rows, channels), sds(r_first, channels), sds(r_short, channels)]
    if direct:
        conv_second_grad, conv_first_grad, conv_short_grad, gains_grad, biases_grad, head_weight_grad = call(
            functools.partial(assemble_last, block, tasks),
            wide_outs + [sds(5, block), sds(5, block), sds(tasks, block)],
            (group_arr, *places),
            [vm((small_rows, channels), f32)],
        )
    else:
        conv_second_grad, conv_first_grad, conv_short_grad, wide_small = call(
            assemble, wide_outs + [sds(small_rows, channels)], (group_arr, *places)
        )
        own_small = lax.dynamic_slice_in_dim(wide_small, group * block, block, 1)
        head_weight_grad = own_small[:tasks]
        n1, n2, n3, n4 = (own_small[tasks + 8 * i : tasks + 8 * (i + 1)] for i in range(4))
        gains_grad = jnp.stack([n1[0], n1[2], n2[0], n3[0], n4[0]])
        biases_grad = jnp.stack([n1[1], n1[3], n2[1], n3[1], n4[1]])
    input_grad = input_grad.reshape(grid, grid, cin // 4, images).transpose(3, 0, 1, 2)

    moved = lax.ppermute(
        pooled,
        ("a", "b", "c"),
        [(4 * i + 2 * j + k, 4 * j + 2 * k + i) for i in range(2) for j in range(2) for k in range(2)],
    )
    spots = jnp.arange(images, dtype=jnp.int32)
    inverse = jnp.sum(
        jnp.where(micro_order[0][None, :] == spots[:, None], spots[None, :], 0), axis=1
    )
    pooled_out = moved[inverse]

    return (
        pooled_out,
        input_grad,
        conv_first_grad,
        conv_short_grad,
        conv_second_grad,
        conv_third_grad,
        conv_fourth_grad,
        gains_grad,
        biases_grad,
        head_weight_grad.T,
        bias_grad[0, :tasks],
    )


def solution(mesh):
    sections, groups = mesh.shape["section"], mesh.shape["dp"]
    fine = Mesh(mesh.devices.reshape(2, sections // 2, groups // 2, 2), ("a", "b", "z", "c"))
    dp, section = ("z", "c"), ("a", "b")
    return jax.shard_map(
        body,
        mesh=fine,
        in_specs=(
            P(dp, None, None, None),
            P(dp),
            P(dp, None),
            P(dp, None),
            P(dp, None),
            P(dp, None),
            P(dp, None),
            P(dp, None),
            P(dp, None),
            P(None, dp),
            P(None, dp),
            P(dp, None),
            P(),
        ),
        out_specs=(
            P(dp, section),
            P(dp, None, None, section),
            P(dp, None),
            P(dp, None),
            P(dp, None),
            P(dp, None),
            P(dp, None),
            P(None, dp),
            P(None, dp),
            P(dp, None),
            P(),
        ),
        check_vma=False,
    )
```

```python
import functools

import jax
import jax.numpy as jnp
from jax import lax
from jax.experimental import pallas as pl
from jax.experimental.pallas import tpu as pltpu
from jax.sharding import Mesh, PartitionSpec as P

MICRO = 6
FW_STEPS = 20
EPSILON = 1e-05
SOFTMAX_HEAT = 0.01
HIGHEST = lax.Precision.HIGHEST

f32 = jnp.float32
bf16 = jnp.bfloat16
L = 128

PLANE_TAPS = ((4, -1), (3, 5), (1, 7), (0, 2, 6, 8))
FIRST_COLS = tuple(tap for taps in PLANE_TAPS for tap in taps)


def room(kernel, flops):
    name = getattr(kernel, "func", kernel).__name__
    if not flops:
        return 51 if name in ("prepare", "pack", "pack_rest", "relay", "unpack") else 28
    if name.endswith("weight_grad"):
        return 51
    return 51 if name.endswith("forward") else 51


class Keep:
    def __init__(self, *shape, dtype=f32):
        self.shape, self.dtype = shape, dtype


class Far:
    def __init__(self, x):
        self.first, self.shape, self.dtype, self.size = x, x.shape, x.dtype, x.size


class Half:
    def __init__(self, x):
        self.first, self.shape, self.dtype, self.size = x, (x.shape[0], L), x.dtype, x.size // 2


class Pick:
    def __init__(self, first, other):
        self.first, self.other = first, other
        self.shape, self.dtype, self.size = first.shape, first.dtype, first.size


class Buf:
    def __init__(self, ref, start, wait, out=False):
        self.ref, self.start, self.wait = ref, start, wait
        self.out, self.started, self.ready = out, not out, out
        self.shape, self.dtype = ref.shape, ref.dtype
        if not out:
            start()

    def get(self):
        if not self.ready:
            self.wait()
            self.ready = True

    def __getitem__(self, at):
        self.get()
        return self.ref[at]

    def __setitem__(self, at, value):
        self.ref[at] = value

    def send(self):
        if not self.started:
            self.start()
            self.started = True


def call(kernel, outs, args, scratch=(), scalars=1, flops=0, ties=(), through=()):
    def far(a):
        return isinstance(a, (Far, Half, Pick, Keep))

    flat, specs, places = [], [], []
    for k, a in enumerate(args):
        places.append(len(flat))
        if k < scalars:
            space = pltpu.SMEM
        else:
            space = pltpu.HBM if far(a) else pltpu.VMEM
        for x in (a.first, a.other) if isinstance(a, Pick) else (a.first,) if far(a) else (a,):
            flat.append(x)
            specs.append(pl.BlockSpec(memory_space=space))
    n_args = len(flat)
    specs += [pl.BlockSpec(memory_space=pl.ANY)] * (len(ties) + len(through))
    far_in = [k for k, a in enumerate(args) if k >= scalars and far(a)]
    far_out = [k for k, o in enumerate(outs) if far(o)]
    buffers = [pltpu.VMEM(args[k].shape, args[k].dtype) for k in far_in]
    buffers += [pltpu.VMEM(outs[k].shape, outs[k].dtype) for k in far_out]
    n_in = n_args + len(ties) + len(through)
    n_outs = len(outs)
    n_bufs = len(buffers)

    def run(*refs):
        ins, results = list(refs[:n_args]), list(refs[n_in : n_in + n_outs])
        rest = refs[n_in + n_outs + len(through) :]
        temps, sems, rest = rest[:n_bufs], rest[n_bufs], rest[n_bufs + 1 :]
        given = []
        for k in range(len(args)):
            src = ins[places[k]]
            if k in far_in:
                n = far_in.index(k)
                if isinstance(args[k], Half):
                    src = src.at[:, pl.ds(pl.multiple_of((ins[0][0] & 1) * L, L), L)]
                copy = pltpu.make_async_copy(src, temps[n], sems.at[n])
                start = copy.start
                if isinstance(args[k], Pick):
                    second = pltpu.make_async_copy(ins[places[k] + 1], temps[n], sems.at[n])

                    def start(copy=copy, second=second):
                        pl.when(ins[0][1] == 1)(copy.start)
                        pl.when(ins[0][1] == 0)(second.start)

                src = Buf(temps[n], start, copy.wait)
            given.append(src)
        made = []
        for k in range(n_outs):
            out = results[k]
            if k in far_out:
                n = len(far_in) + far_out.index(k)
                copy = pltpu.make_async_copy(temps[n], out, sems.at[n])
                out = Buf(temps[n], copy.start, copy.wait, out=True)
            made.append(out)
        kernel(*given, *made, *rest)
        for x in given:
            if isinstance(x, Buf):
                x.get()
        made = [x for x in made if isinstance(x, Buf)]
        for x in made:
            x.send()
        for x in made:
            x.wait()

    outs = [sds(*o.shape, dtype=o.dtype) if far(o) else o for o in outs]
    size = sum(a.size * a.dtype.itemsize for a in flat) + sum(o.size * o.dtype.itemsize for o in outs)
    return pl.pallas_call(
        run,
        out_shape=tuple(outs) + tuple(sds(*x.shape, dtype=x.dtype) for x in through),
        in_specs=specs,
        out_specs=tuple(
            pl.BlockSpec(memory_space=pltpu.HBM if k in far_out else pltpu.VMEM) for k in range(n_outs)
        )
        + tuple(pl.BlockSpec(memory_space=pl.ANY) for _ in through),
        scratch_shapes=buffers + [pltpu.SemaphoreType.DMA((max(n_bufs, 1),))] + list(scratch),
        input_output_aliases={n_args + len(ties) + k: n_outs + k for k in range(len(through))},
        compiler_params=pltpu.CompilerParams(vmem_limit_bytes=room(kernel, flops) << 20),
        cost_estimate=pl.CostEstimate(flops=int(flops), bytes_accessed=int(size), transcendentals=0),
    )(*flat, *ties, *through)


def sds(*shape, dtype=f32):
    return jax.ShapeDtypeStruct(shape, dtype)


def nt_dot(x, y):
    return lax.dot_general(x, y, (((1,), (1,)), ((), ())), preferred_element_type=f32)


def tn_dot(x, y):
    return lax.dot_general(x, y, (((0,), (0,)), ((), ())), preferred_element_type=f32)


def sigmoid(v):
    return 0.5 + 0.5 * jnp.tanh(0.5 * v)


def pixel_mask(i, big):
    return None if (i // 4 < 2 and i % 4 < 2) else big


def masked(value, i, big):
    return value if pixel_mask(i, big) is None else value * big


def per_micro(value, nm):
    rows, lanes = value.shape
    return jnp.sum(value.reshape(nm, rows // nm, lanes), axis=1)


def spread_micro(value, im):
    nm, lanes = value.shape
    return jnp.broadcast_to(value[:, None, :], (nm, im // nm, lanes)).reshape(im, lanes)


def blk(ref, i, im):
    return ref[i * im : (i + 1) * im, :]


def norm_forward(p_ref, xhat_ref, inv_ref, big, nm):
    im = big.shape[0]
    total = per_micro(4.0 + 12.0 * big, nm)
    acc = jnp.zeros_like(big)
    for i in range(16):
        acc = acc + masked(blk(p_ref, i, im), i, big)
    mean = spread_micro(per_micro(acc, nm) / total, im)
    acc = jnp.zeros_like(big)
    for i in range(16):
        cen = blk(p_ref, i, im) - mean
        acc = acc + masked(cen * cen, i, big)
    inv = lax.rsqrt(per_micro(acc, nm) / total + EPSILON)
    inv_ref[...] = jnp.concatenate([inv, jnp.zeros((8 - nm, inv.shape[1]), f32)], axis=0)
    inv = spread_micro(inv, im)
    for i in range(16):
        xhat = (blk(p_ref, i, im) - mean) * inv
        p_ref[i * im : (i + 1) * im, :] = xhat
        xhat_ref[i * im : (i + 1) * im, :] = xhat.astype(bf16)


def norm_backward(dy_ref, xhat_ref, inv_ref, gain, big, nm, out_ref):
    im = big.shape[0]
    total = per_micro(4.0 + 12.0 * big, nm)
    sum_dy = jnp.zeros_like(big)
    sum_dx = jnp.zeros_like(big)
    for i in range(16):
        dy = blk(dy_ref, i, im)
        sum_dy = sum_dy + dy
        sum_dx = sum_dx + dy * blk(xhat_ref, i, im).astype(f32)
    sum_dy = per_micro(sum_dy, nm)
    sum_dx = per_micro(sum_dx, nm)
    mean_dy = spread_micro(sum_dy / total, im)
    mean_dx = spread_micro(sum_dx / total, im)
    scale = spread_micro(inv_ref[0:nm, :] * gain, im)
    for i in range(16):
        off = masked(mean_dy + blk(xhat_ref, i, im).astype(f32) * mean_dx, i, big)
        grad = scale * (blk(dy_ref, i, im) - off)
        out_ref[i * im : (i + 1) * im, :] = grad.astype(bf16)
    return jnp.sum(sum_dx, axis=0, keepdims=True), jnp.sum(sum_dy, axis=0, keepdims=True)


def load_weights(q_ref, w_ref, ws):
    channels = 4 * L
    q = q_ref[0]
    for t in range(9):
        for j in range(4):
            start = pl.multiple_of(t * channels + (q ^ j) * L, L)
            ws[j * L : (j + 1) * L, t * L : (t + 1) * L] = w_ref[pl.ds(start, L), :]


def row_taps(r):
    return (3 * L if r == 3 else 0), (6 * L if r == 0 else 9 * L)


def conv_forward(q_ref, x_refs, w_ref, xs, ws, y, p, im):
    for j in (0, 1, 3, 2):
        xs[:, j * L : (j + 1) * L] = x_refs[j][...]
    xs.send()
    load_weights(q_ref, w_ref, ws)
    for r in range(4):
        lo, hi = row_taps(r)
        rows = slice(r * 4 * im, (r + 1) * 4 * im)
        y[rows, lo:hi] = jnp.dot(xs[rows, :], ws[:, lo:hi], preferred_element_type=f32)
    for r in range(4):
        for c in range(4):
            acc = None
            for t in range(9):
                ri, ci = r + t // 3 - 1, c + t % 3 - 1
                if 0 <= ri < 4 and 0 <= ci < 4:
                    i = ri * 4 + ci
                    term = y[i * im : (i + 1) * im, t * L : (t + 1) * L]
                    acc = term if acc is None else acc + term
            p[(r * 4 + c) * im : (r * 4 + c + 1) * im, :] = acc


def spread_taps(dp_ref, d, im, rows_at, all_taps):
    for r in range(4):
        lo, hi = (0, 9 * L) if all_taps else row_taps(r)
        for c in range(4):
            at = rows_at + (r * 4 + c) * im
            for t in range(lo // L, hi // L):
                ro, co = r - t // 3 + 1, c - t % 3 + 1
                if 0 <= ro < 4 and 0 <= co < 4:
                    value = blk(dp_ref, ro * 4 + co, im)
                else:
                    value = jnp.zeros((im, L), bf16)
                d[at : at + im, t * L : (t + 1) * L] = value


def conv_back_input(q_ref, dp_ref, w_ref, ws, d, outs, im):
    dp_ref.send()
    load_weights(q_ref, w_ref, ws)
    spread_taps(dp_ref, d, im, 0, False)
    for r in range(4):
        lo, hi = row_taps(r)
        rows = slice(r * 4 * im, (r + 1) * 4 * im)
        dx = nt_dot(d[rows, lo:hi], ws[:, lo:hi])
        for j in range(4):
            outs[j][rows, :] = dx[:, j * L : (j + 1) * L].astype(outs[j].dtype)


def load_plane(x, k, big, xs, im):
    wide = jnp.concatenate([big, big], axis=1).astype(bf16)
    for i in range(16):
        pixel = (2 * (i // 4) + k // 2) * 8 + 2 * (i % 4) + k % 2
        xs[i * im : (i + 1) * im, :] = masked(blk(x, pixel, im), i, wide)


def first_forward(nm, c_ref, x, w, w_short, params, big_ref, h, s, xh1, inv1, xh2, inv2, xs, wsc, y, p1, p2):
    big = big_ref[...]
    im = big.shape[0]
    cin = 2 * L
    col = 0
    for k, taps in enumerate(PLANE_TAPS):
        for n, t in enumerate(taps):
            src = w_short[...] if t < 0 else w[t * cin : (t + 1) * cin, :]
            wsc[:, (col + n) * L : (col + n + 1) * L] = src
        cols = slice(col * L, (col + len(taps)) * L)
        load_plane(x, k, big, xs, im)
        y[:, cols] = jnp.dot(xs[...], wsc[:, cols], preferred_element_type=f32)
        col += len(taps)
    for r in range(4):
        for c in range(4):
            o = r * 4 + c
            acc = None
            for n, t in enumerate(FIRST_COLS):
                if t < 0:
                    p2[o * im : (o + 1) * im, :] = y[o * im : (o + 1) * im, n * L : (n + 1) * L]
                    continue
                ri = r - 1 if t // 3 == 0 else r
                ci = c - 1 if t % 3 == 0 else c
                if ri >= 0 and ci >= 0:
                    i = ri * 4 + ci
                    term = y[i * im : (i + 1) * im, n * L : (n + 1) * L]
                    acc = term if acc is None else acc + term
            p1[o * im : (o + 1) * im, :] = acc
    norm_forward(p1, xh1, inv1, big, nm)
    norm_forward(p2, xh2, inv2, big, nm)
    for i in range(16):
        rows = slice(i * im, (i + 1) * im)
        v = blk(p1, i, im) * params[0:1, :] + params[5:6, :]
        h[rows, :] = masked(v * sigmoid(v), i, big).astype(bf16)
        v = blk(p2, i, im) * params[1:2, :] + params[6:7, :]
        s[rows, :] = masked(v, i, big).astype(bf16)


def second_forward(nm, q_ref, x0, x1, x2, x3, w, params, big_ref, s, out, xh, inv, xs, ws, y, p):
    big = big_ref[...]
    im = big.shape[0]
    conv_forward(q_ref, (x0, x1, x2, x3), w, xs, ws, y, p, im)
    norm_forward(p, xh, inv, big, nm)
    for i in range(16):
        rows = slice(i * im, (i + 1) * im)
        u = blk(p, i, im) * params[2:3, :] + params[7:8, :]
        u = masked(u, i, big).astype(bf16).astype(f32)
        v = u + s[rows, :].astype(f32)
        out[rows, :] = masked(v * sigmoid(v), i, big).astype(bf16)


def third_forward(nm, q_ref, x0, x1, x2, x3, w, params, big_ref, out, xh, inv, xs, ws, y, p):
    big = big_ref[...]
    im = big.shape[0]
    conv_forward(q_ref, (x0, x1, x2, x3), w, xs, ws, y, p, im)
    norm_forward(p, xh, inv, big, nm)
    for i in range(16):
        rows = slice(i * im, (i + 1) * im)
        v = blk(p, i, im) * params[3:4, :] + params[8:9, :]
        out[rows, :] = masked(v * sigmoid(v), i, big).astype(bf16)


def fourth_forward(
    nm, q_ref, x0, x1, x2, x3, w, params, big_ref, res, head, pooled, logits, xh, inv, xs, ws, y, p
):
    big = big_ref[...]
    im = big.shape[0]
    conv_forward(q_ref, (x0, x1, x2, x3), w, xs, ws, y, p, im)
    norm_forward(p, xh, inv, big, nm)
    acc = jnp.zeros_like(big)
    for i in range(16):
        rows = slice(i * im, (i + 1) * im)
        v = blk(p, i, im) * params[4:5, :] + params[9:10, :] + res[rows, :].astype(f32)
        acc = acc + masked(v * sigmoid(v), i, big)
    pool = acc / (4.0 + 12.0 * big)
    pooled[...] = pool
    logits[...] = jnp.dot(pool.astype(bf16), head[...], preferred_element_type=f32)


def head_errors(mine, other, bias, labels, tasks, errors, stats):
    logits = mine[...] + other[...] + bias[0:1, :]
    lane = lax.broadcasted_iota(jnp.int32, logits.shape, 1)
    err = jnp.where(lane < tasks, sigmoid(logits) - labels[...], 0.0)
    errors[...] = err
    gram = lax.dot_general(err, err, (((0,), (0,)), ((), ())), precision=HIGHEST, preferred_element_type=f32)
    stats[0:tasks, :] = gram[0:tasks, :]
    stats[tasks:, :] = jnp.broadcast_to(jnp.sum(err, axis=0, keepdims=True), (stats.shape[0] - tasks, L))


def head_weights(count, tasks, stats, errors, head_all, head_mine, pooled, dz, bias_grad, head_grad):
    inner = tn_dot(head_all[...], head_all[...])
    gram = stats[0:tasks, :] * inner[0:tasks, :] / count
    row = lax.broadcasted_iota(jnp.int32, (tasks, L), 0)
    lane = lax.broadcasted_iota(jnp.int32, (tasks, L), 1)
    weight_row = jnp.where(lane[0:1, :] < tasks, 1.0 / tasks, 0.0)
    for step in range(FW_STEPS):
        score = -jnp.sum(gram * weight_row, axis=1, keepdims=True) / SOFTMAX_HEAT
        power = jnp.exp(score - jnp.max(score, axis=0, keepdims=True))
        corner = power / jnp.sum(power, axis=0, keepdims=True)
        corner = jnp.sum(jnp.where(row == lane, corner, 0.0), axis=0, keepdims=True)
        rate = 2.0 / (step + 2.0)
        weight_row = (1.0 - rate) * weight_row + rate * corner
    scaled = errors[...] * weight_row
    dz[...] = lax.dot_general(
        scaled,
        head_mine[...].astype(f32),
        (((1,), (1,)), ((), ())),
        precision=HIGHEST,
        preferred_element_type=f32,
    )
    bias_grad[...] = jnp.broadcast_to(weight_row * stats[tasks : tasks + 1, :], bias_grad.shape)
    grad = lax.dot_general(
        scaled,
        pooled[...].astype(bf16).astype(f32),
        (((0,), (0,)), ((), ())),
        precision=HIGHEST,
        preferred_element_type=f32,
    )
    head_grad[...] = grad[0:tasks, :]


def fourth_backward(
    nm, q_ref, dz, xh, inv, res, w, params, big_ref, o0, o1, o2, o3, dp, d_res, norm, ws, d, dy
):
    big = big_ref[...]
    im = big.shape[0]
    out_grad = dz[...] / (4.0 + 12.0 * big)
    for i in range(16):
        rows = slice(i * im, (i + 1) * im)
        v = blk(xh, i, im).astype(f32) * params[4:5, :] + params[9:10, :] + res[rows, :].astype(f32)
        sig = sigmoid(v)
        grad = masked(out_grad * (sig * (1.0 + v * (1.0 - sig))), i, big)
        dy[rows, :] = grad
        d_res[rows, :] = grad.astype(bf16)
    dgain, dbias = norm_backward(dy, xh, inv, params[4:5, :], big, nm, dp)
    norm[...] = jnp.concatenate([dgain, dbias, jnp.zeros((6, L), f32)], axis=0)
    conv_back_input(q_ref, dp, w, ws, d, (o0, o1, o2, o3), im)


def heads_and_fourth(
    count, tasks, nm, q_ref, stats, errors, head_all, head_mine, pooled, xh, inv, res, w, params, big_ref,
    o0, o1, o2, o3, dp, d_res, norm, bias_grad, head_grad, ws, d, dy, dz,
):
    head_weights(count, tasks, stats, errors, head_all, head_mine, pooled, dz, bias_grad, head_grad)
    fourth_backward(
        nm, q_ref, dz, xh, inv, res, w, params, big_ref, o0, o1, o2, o3, dp, d_res, norm, ws, d, dy
    )


def third_backward(
    nm, q_ref, g0, g1, g2, xh, inv, w, params, big_ref, o0, o1, o2, o3, dp, norm, ws, d, dy
):
    big = big_ref[...]
    im = big.shape[0]
    for i in range(16):
        rows = slice(i * im, (i + 1) * im)
        grad = g0[rows, :].astype(f32) + g1[rows, :].astype(f32) + g2[rows, :].astype(f32)
        grad = grad.astype(bf16).astype(f32)
        v = blk(xh, i, im).astype(f32) * params[3:4, :] + params[8:9, :]
        sig = sigmoid(v)
        dy[rows, :] = masked(grad * (sig * (1.0 + v * (1.0 - sig))), i, big)
    dgain, dbias = norm_backward(dy, xh, inv, params[3:4, :], big, nm, dp)
    norm[...] = jnp.concatenate([dgain, dbias, jnp.zeros((6, L), f32)], axis=0)
    conv_back_input(q_ref, dp, w, ws, d, (o0, o1, o2, o3), im)


def second_backward(
    nm, q_ref, g0, g1, g2, d_res, s, xh, inv, w, params, big_ref, o0, o1, o2, o3, dp, ds, norm, ws, d, dy
):
    big = big_ref[...]
    im = big.shape[0]
    for i in range(16):
        rows = slice(i * im, (i + 1) * im)
        grad = g0[rows, :].astype(f32) + g1[rows, :].astype(f32) + g2[rows, :].astype(f32)
        grad = grad + d_res[rows, :].astype(f32)
        u = blk(xh, i, im).astype(f32) * params[2:3, :] + params[7:8, :]
        v = masked(u, i, big).astype(bf16).astype(f32) + s[rows, :].astype(f32)
        sig = sigmoid(v)
        grad = masked(grad * (sig * (1.0 + v * (1.0 - sig))), i, big).astype(bf16)
        ds[rows, :] = grad
        dy[rows, :] = grad.astype(f32)
    dgain, dbias = norm_backward(dy, xh, inv, params[2:3, :], big, nm, dp)
    norm[...] = jnp.concatenate([dgain, dbias, jnp.zeros((6, L), f32)], axis=0)
    conv_back_input(q_ref, dp, w, ws, d, (o0, o1, o2, o3), im)


def spread_first(dp1, dps, d, im, rows_at):
    for i in range(16):
        r, c = i // 4, i % 4
        at = rows_at + i * im
        for n, t in enumerate(FIRST_COLS):
            if t < 0:
                value = blk(dps, i, im)
            else:
                ro = r + 1 if t // 3 == 0 else r
                co = c + 1 if t % 3 == 0 else c
                value = blk(dp1, ro * 4 + co, im) if ro < 4 and co < 4 else jnp.zeros((im, L), bf16)
            d[at : at + im, n * L : (n + 1) * L] = value


def first_backward(
    nm, c_ref, g0, g1, g2, ds, xh1, inv1, xh2, inv2, w, w_short, params, big_ref, *refs,
):
    outs, (dp1, dps, norm, ws, d, dy) = refs[:5], refs[5:]
    big = big_ref[...]
    im = big.shape[0]
    half, part = c_ref[0], c_ref[1]
    cin = 2 * L
    for i in range(16):
        rows = slice(i * im, (i + 1) * im)
        grad = g0[rows, :].astype(f32) + g1[rows, :].astype(f32) + g2[rows, :].astype(f32)
        grad = grad.astype(bf16).astype(f32)
        v = blk(xh1, i, im).astype(f32) * params[0:1, :] + params[5:6, :]
        sig = sigmoid(v)
        dy[rows, :] = masked(grad * (sig * (1.0 + v * (1.0 - sig))), i, big)
    gain1, bias1 = norm_backward(dy, xh1, inv1, params[0:1, :], big, nm, dp1)
    for i in range(16):
        rows = slice(i * im, (i + 1) * im)
        dy[rows, :] = masked(ds[rows, :].astype(f32), i, big)
    gain2, bias2 = norm_backward(dy, xh2, inv2, params[1:2, :], big, nm, dps)
    norm[...] = jnp.concatenate([gain1, bias1, gain2, bias2, jnp.zeros((4, L), f32)], axis=0)
    wide = cin // 4
    for n, t in enumerate(FIRST_COLS):
        for j in range(4):
            start = (half ^ (j & 1)) * 2 * wide + (part ^ (j >> 1)) * wide
            if t < 0:
                src = w_short[pl.ds(pl.multiple_of(start, wide), wide), :]
            else:
                src = w[pl.ds(pl.multiple_of(t * cin + start, wide), wide), :]
            ws[j * wide : (j + 1) * wide, n * L : (n + 1) * L] = src
    spread_first(dp1, dps, d, im, 0)
    col = 0
    for k, taps in enumerate(PLANE_TAPS):
        cols = slice(col * L, (col + len(taps)) * L)
        dx = nt_dot(d[:, cols], ws[:, cols])
        pair, side = k // 2, k % 2
        for j in range(4):
            ref = outs[j] if j < 3 else outs[3 + pair]
            at = pair * 16 * im if j < 3 else 0
            rows = slice(at, at + 16 * im)
            ref[rows, side * wide : (side + 1) * wide] = dx[:, j * wide : (j + 1) * wide].astype(ref.dtype)
        col += len(taps)


def halves(whole, outs):
    rows = outs[0].shape[0]
    for k, out in enumerate(outs):
        out[...] = whole[k * rows : (k + 1) * rows, :]


def weight_grad(block, q_ref, x, dp, *refs):
    if block:
        *outs, d, out = refs
    else:
        out, d = refs
    im = dp.shape[0] // 16
    q, a = q_ref[0], q_ref[2]
    total = out.shape[0]
    spread_taps(dp, d, im, 0, True)
    step = L // 2 if block else L
    for n in range(3):
        cols = slice(n * 3 * L, (n + 1) * 3 * L)
        grad = tn_dot(x[...], d[:, cols]).astype(bf16)
        for t in range(3):
            for j in range(4):
                for part in range(L // step):
                    start = (3 * n + t) * 4 * L + (q ^ j) * L + part * step
                    if block:
                        at = start // block
                        start = ((at & 1) ^ a) * (total // 2) + (at // 2) * block + start % block
                    start = pl.multiple_of(start, step)
                    value = grad[j * L + part * step : j * L + (part + 1) * step, t * L : (t + 1) * L]
                    out[pl.ds(start, step), :] = value
    if block:
        halves(out, outs)


def first_weight_grad(blocks, q_ref, x, dp1, dps, big_ref, *refs):
    if blocks:
        *smalls, keep, give, xs, d, out = refs
        small = jnp.concatenate([v[...] for v in smalls], axis=0).astype(bf16)
        n1, n2 = blocks
        per = n1 + n2 + small.shape[0]
        total = out.shape[0]
        a = q_ref[2]
    else:
        out, out_short, xs, d = refs
    big = big_ref[...]
    im = big.shape[0]
    cin = 2 * L

    def place(at):
        return pl.multiple_of(((at & 1) ^ a) * (total // 2) + (at // 2) * per, 16)

    spread_first(dp1, dps, d, im, 0)
    col = 0
    for k, taps in enumerate(PLANE_TAPS):
        cols = slice(col * L, (col + len(taps)) * L)
        load_plane(x, k, big, xs, im)
        grad = tn_dot(xs[...], d[:, cols]).astype(bf16)
        for n, t in enumerate(taps):
            value = grad[:, n * L : (n + 1) * L]
            if not blocks:
                if t < 0:
                    out_short[...] = value
                else:
                    out[t * cin : (t + 1) * cin, :] = value
                continue
            size, base, row = (n2, n1, 0) if t < 0 else (n1, 0, t * cin)
            done = 0
            while done < cin:
                at, inner = (row + done) // size, (row + done) % size
                count = min(cin - done, size - inner)
                start = pl.multiple_of(place(at) + base + inner, 16)
                out[pl.ds(start, count), :] = value[done : done + count, :]
                done += count
        col += len(taps)
    if blocks:
        for at in range(cin // n2):
            start = pl.multiple_of(place(at) + n1 + n2, 16)
            out[pl.ds(start, small.shape[0]), :] = small
        halves(out, (keep, give))


def sum_beside(n_z, x, x_got, y, y_got, out):
    at = 0
    sizes = (x_got.shape[0] // n_z, y_got.shape[0] // n_z)
    for z in range(n_z):
        for kept, got, rows in ((x, x_got, sizes[0]), (y, y_got, sizes[1])):
            cut = slice(z * rows, (z + 1) * rows)
            out[at : at + rows, :] = (kept[cut, :].astype(f32) + got[cut, :].astype(f32)).astype(bf16)
            at += rows


def add_low(x, y, out):
    out[...] = (x[...].astype(f32) + y[...].astype(f32)).astype(bf16)


def add_halves(x, low, high, out):
    rows = low.shape[0]
    for k, y in enumerate((low, high)):
        cut = slice(k * rows, (k + 1) * rows)
        out[cut, :] = (x[cut, :].astype(f32) + y[...].astype(f32)).astype(bf16)


def add_three(x, y, z, out):
    out[...] = (x[...].astype(f32) + y[...].astype(f32) + z[...].astype(f32)).astype(bf16)


def pick_a(sizes, a_ref, *refs):
    *arrays, keep, give = refs
    at, source = 0, 0
    for rows in sizes:
        for out, a in ((keep, a_ref[2]), (give, 1 - a_ref[2])):
            cut = pl.ds(pl.multiple_of(source + a * rows, 8), rows)
            out[at : at + rows, :] = arrays[0][cut, :]
        at, source = at + rows, source + 2 * rows
        if source == arrays[0].shape[0]:
            arrays, source = arrays[1:], 0


def flip(value, axis):
    return lax.ppermute(value, axis, [(i, i ^ 1) for i in range(lax.axis_size(axis))])


def swap_ac(value):
    return lax.ppermute(value, ("a", "c"), [(1, 2), (2, 1)])


def sum_over(value, axis):
    count = lax.axis_size(axis)
    if count & (count - 1):
        return lax.psum(value, axis)
    step = 1
    while step < count:
        value = value + lax.ppermute(value, axis, [(i, i ^ step) for i in range(count)])
        step *= 2
    return value


def gather_quarters(h):
    from_b = flip(h, "b")
    from_c = flip(h, "c")
    return (h, from_c, Far(from_b), flip(from_b, "c"))


def scatter_quarters(parts):
    p0, p1, p2, p3 = parts
    first = flip(p1, "c")
    second = flip(p3, "c")
    send = (p2.astype(f32) + second.astype(f32)).astype(bf16)
    return (p0, first, Far(flip(send, "b")), send)


def pack(q_ref, first, short, norms, heads, mine, give):
    q = q_ref[0]
    n1, n2 = first.shape[0], short.shape[0]
    for out, part in ((mine, q), (give, q ^ 1)):
        cols = pl.ds(pl.multiple_of(part * L, L), L)
        out[0:n1, :] = first[:, cols]
        out[n1 : n1 + n2, :] = short[:, cols]
        out[n1 + n2 :, :] = heads[...]
        out[n1 + n2 : n1 + n2 + norms.shape[0], L - norms.shape[1] :] = norms[...]


def pack_rest(q_ref, *refs):
    count = len(refs) // 2
    for src, out in zip(refs[:count], refs[count:]):
        wide = out.shape[1]
        part = q_ref[1] if wide == L else q_ref[0] // 2
        out[...] = src[:, pl.ds(pl.multiple_of(part * wide, L), wide)]


def prepare(q_ref, order_ref, x, out, *bufs):
    images = order_ref.shape[1]
    pixels = out.shape[0] // images
    x.get()

    def move(j, carry):
        source = pl.ds(pl.multiple_of(order_ref[0, j] * pixels, pixels), pixels)
        target = pl.ds(pl.multiple_of(j * pixels, pixels), pixels)
        for k, buf in enumerate(bufs):
            buf[target, :] = x.ref[source, k * L : (k + 1) * L].astype(f32)
        return carry

    lax.fori_loop(0, images, move, 0, unroll=4)
    for p in range(pixels):
        for k, buf in enumerate(bufs):
            value = buf[pl.ds(p, images, stride=pixels), :].astype(bf16)
            out[p * images : (p + 1) * images, k * L : (k + 1) * L] = value


def relay(*refs):
    *parts, out = refs
    rows = parts[0].shape[0]
    for k, part in enumerate(parts):
        out[k * rows : (k + 1) * rows, :] = part[...]


def unpack(n1, n2, block, k_ref, mine, other, first, short, params, heads):
    here, q = k_ref[0], k_ref[1]
    rows = mine.shape[0] // 4
    for k in range(8):
        piece = (mine, other)[k % 2][k // 2 * rows : (k // 2 + 1) * rows, :]
        at = here ^ k
        first[pl.ds(pl.multiple_of(at * n1, 32), n1), :] = piece[0:n1, :]
        short[pl.ds(pl.multiple_of(at * n2, 32), n2), :] = piece[n1 : n1 + n2, :]
        head = piece[n1 + n2 : n1 + n2 + block, :]
        lane = lax.broadcasted_iota(jnp.int32, head.shape, 1)
        heads[pl.ds(pl.multiple_of(at * block, 32), block), :] = jnp.where(
            lane < L - block, head, jnp.zeros_like(head)
        )
        for side in range(L // block):
            @pl.when(at == q * (L // block) + side)
            def _():
                value = piece[n1 + n2 : n1 + n2 + 16, L - block :].astype(f32)
                params[:, side * block : (side + 1) * block] = value


def assemble(q_ref, p0, p1, p2, p3, *outs):
    q = q_ref[0]
    for j, part in enumerate((p0, p1, p2, p3)):
        cols = pl.ds(pl.multiple_of((q ^ j) * L, L), L)
        at = 0
        for out in outs:
            out[:, cols] = part[at : at + out.shape[0], :].astype(f32)
            at += out.shape[0]


def assemble_last(block, tasks, q_ref, p0, p1, p2, p3, *refs):
    *outs, gains, biases, heads, wide = refs
    assemble(q_ref, p0, p1, p2, p3, *outs, wide)
    start = q_ref[1] * block
    own = wide[:, pl.ds(pl.multiple_of(start // L * L, L), L)]
    value = own[:, :block]
    for k in range(1, L // block):
        value = jnp.where(start % L == k * block, own[:, k * block : (k + 1) * block], value)
    heads[...] = value[0:tasks, :]
    for out, side in ((gains, 0), (biases, 1)):
        rows = [tasks + side, tasks + 2 + side] + [tasks + 8 * k + side for k in (1, 2, 3)]
        out[...] = jnp.concatenate([value[r : r + 1, :] for r in rows], axis=0)


def input_grad_kernel(q_ref, order_ref, big_ref, parts, out):
    images = order_ref.shape[1]
    im = images
    wide = out.shape[1]
    spot = lax.broadcasted_iota(jnp.int32, (images, images), 1)
    pick = jnp.where(spot == jnp.transpose(jnp.broadcast_to(order_ref[0:1, :], (images, images))), 1.0, 0.0)
    pick = pick.astype(bf16)
    big = big_ref[0:1, :]
    for pr in range(2):
        for i in range(16):
            at = 16 * pr + i
            value = masked(tn_dot(blk(parts, at, im), pick), i, big)
            for pc in range(2):
                pixel = (2 * (i // 4) + pr) * 8 + 2 * (i % 4) + pc
                out[pixel, :, :] = value[pc * wide : (pc + 1) * wide, :]


def body(
    features, buckets, micro_order, labels, conv_first, conv_short, conv_second, conv_third, conv_fourth,
    norm_gains, norm_biases, head_weight, head_bias,
):
    ia, ib, iz, ic = (lax.axis_index(n) for n in ("a", "b", "z", "c"))
    n_group = lax.axis_size("z") * lax.axis_size("c")
    images, grid, _, cin = features.shape
    channels = conv_second.shape[1]
    tasks = head_weight.shape[1]
    quarter = 2 * ib + ic
    shared = 2 * ib + ia
    im = images
    nm = MICRO
    rows = 16 * im
    own = ia == ic
    q_arr = jnp.stack([quarter, own, ia, iz]).astype(jnp.int32)
    c_arr = jnp.stack([ic, ib]).astype(jnp.int32)

    block = channels // n_group
    r_first, r_short = conv_first.shape[0], conv_short.shape[0]
    n_z = lax.axis_size("z")

    small_rows = max(16, block)
    norms = jnp.concatenate([norm_gains, norm_biases], axis=0)
    norms = jnp.pad(norms, ((0, 6), (0, 0)))
    heads = jnp.pad(head_weight, ((0, small_rows - block), (0, L - tasks)))
    slot_rows = r_first + r_short + small_rows
    piece_t = sds(slot_rows, L, dtype=bf16)
    quarter_t = sds(conv_second.shape[0], L, dtype=bf16)
    pack_arr = jnp.stack([quarter, shared]).astype(jnp.int32)
    rest = call(pack_rest, [quarter_t], (pack_arr, conv_second))
    mine, give = call(
        pack, [piece_t, piece_t], (pack_arr, conv_first, conv_short, norms, heads), ties=rest
    )
    half_t = sds(conv_fourth.shape[0], 2 * L, dtype=bf16)
    rest += call(pack_rest, [quarter_t, half_t], (pack_arr, conv_third, conv_fourth), ties=(give,))
    rest = [lax.all_gather(w, ("z", "c"), axis=0, tiled=True) for w in rest]
    piece = jnp.where(own, mine, flip(give, "c"))

    parts = [piece]
    if n_z == 4:
        parts += [lax.ppermute(piece, "z", [(i, i ^ m) for i in range(n_z)]) for m in range(1, n_z)]

    ints = jnp.concatenate(
        [
            labels,
            buckets[:, None],
            micro_order.reshape(images, 1),
            jnp.zeros((images, L - tasks - 2), jnp.int32),
        ],
        axis=1,
    )
    ints = jnp.where(own, ints, flip(ints, "c"))
    order = ints[:, tasks + 1]
    flat = features.reshape(images * grid * grid, cin)
    (feats,) = call(
        prepare,
        [sds(images * grid * grid, cin, dtype=bf16)],
        (q_arr, order[None], Pick(flat, flip(flat, "c"))),
        [pltpu.VMEM((images * grid * grid, L), f32)] * (cin // L),
        scalars=2,
    )

    if n_z == 4:
        (stack,) = call(
            relay, [sds(n_z * slot_rows, L, dtype=bf16)], parts, scalars=0, ties=(feats,)
        )
        w_first, w_short, params, head_all = call(
            functools.partial(unpack, r_first, r_short, block),
            [
                sds(n_group * r_first, L, dtype=bf16),
                sds(n_group * r_short, L, dtype=bf16),
                sds(16, L),
                sds(channels, L, dtype=bf16),
            ],
            (jnp.stack([2 * iz + ia, quarter]).astype(jnp.int32), stack, flip(stack, "a")),
        )
    else:
        packed = lax.all_gather(piece, ("z", "a"), axis=0)
        w_first = packed[:, :r_first].reshape(n_group * r_first, L)
        w_short = packed[:, r_first : r_first + r_short].reshape(n_group * r_short, L)
        small = packed[:, r_first + r_short :]
        head_all = small[:, :block].reshape(channels, L)
        lane = lax.broadcasted_iota(jnp.int32, head_all.shape, 1)
        head_all = jnp.where(lane < tasks, head_all, jnp.zeros_like(head_all))
        params = small[:, :16, L - block :].transpose(1, 0, 2).reshape(16, channels)
        params = lax.dynamic_slice_in_dim(params, quarter * L, L, 1).astype(f32)
    head_mine = lax.dynamic_slice_in_dim(head_all, quarter * L, L, 0)
    bias_row = jnp.broadcast_to(
        jnp.pad(head_bias.astype(f32), (0, L - tasks))[None, :], (8, L)
    )

    own_big = jnp.broadcast_to(buckets[None, :].astype(f32), (8, images))
    ints = ints[order]
    label_rows = ints.astype(f32)
    big = jnp.broadcast_to(ints[:, tasks : tasks + 1].astype(f32), (images, L))

    act = sds(rows, L, dtype=bf16)
    full = sds(rows, L)
    img = sds(im, L)
    micro = sds(8, L)
    low_kept = kept = Keep(rows, L, dtype=bf16)
    vm = pltpu.VMEM
    conv_scratch = [vm((4 * L, 9 * L), bf16), vm((rows, 9 * L), f32), vm((rows, L), f32)]
    wide_kept = Keep(rows, 4 * L, dtype=bf16)
    back_scratch = [vm((4 * L, 9 * L), bf16), vm((rows, 9 * L), bf16), vm((rows, L), f32)]
    flops_conv = 2 * rows * 4 * L * 9 * L

    def run(kernel, outs, args, scratch, flops=flops_conv, ties=(), through=()):
        return call(functools.partial(kernel, nm), outs, args, scratch, 1, flops, ties, through)

    *first, w_second = run(
        first_forward,
        [act, low_kept, kept, micro, kept, micro],
        (q_arr, feats, w_first, w_short, params, big),
        [vm((rows, cin), bf16), vm((cin, 10 * L), bf16), vm((rows, 10 * L), f32), vm((rows, L), f32), vm((rows, L), f32)],
        through=(rest[0],),
    )
    w_second, w_third = [Pick(w, swap_ac(w)) for w in (w_second, rest[1])]
    w_fourth = Half(rest[2])
    h1 = gather_quarters(first[0])
    second = run(
        second_forward,
        [act, kept, micro, wide_kept],
        (q_arr, *h1, w_second, params, big, first[1]),
        conv_scratch,
    )
    x2 = gather_quarters(second[0])
    third = run(third_forward, [act, kept, micro, wide_kept], (q_arr, *x2, w_third, params, big), conv_scratch)
    h3 = gather_quarters(third[0])
    fourth = run(
        fourth_forward,
        [img, img, kept, micro, wide_kept],
        (q_arr, *h3, w_fourth, params, big, second[0], head_mine),
        conv_scratch,
    )
    pooled, logits = fourth[:2]

    logits = logits + flip(logits, "c")
    stat_rows = tasks + 8
    errors, stats = call(
        lambda mine, other, bias, lab, err, st: head_errors(mine, other, bias, lab, tasks, err, st),
        [sds(images, L), sds(stat_rows, L)],
        (logits, flip(logits, "b"), bias_row, label_rows),
        scalars=0,
    )
    stats = sum_over(sum_over(stats, "a"), "z")
    direct = n_z == 4
    quads = [low_kept] * 4
    own_rows = 9 * channels // n_group
    shared_arr = shared[None].astype(jnp.int32)

    def grad_of(acts, grad, ties, block=0):
        whole = 9 * channels
        out = call(
            functools.partial(weight_grad, block),
            [Keep(whole // 2, L, dtype=bf16)] * 2 if block else [Keep(whole, L, dtype=bf16)],
            (q_arr, acts, grad),
            [vm((rows, 9 * L), bf16)] + ([vm((whole, L), bf16)] if block else []),
            1,
            flops_conv,
            ties,
        )
        return out if block else out[0]

    def over_z(grad):
        return lax.psum_scatter(grad, "z", scatter_dimension=0, tiled=True)

    def to_places(shard):
        parts = []
        for m in range(4):
            pairs = [
                (4 * i + 2 * j + k, 4 * (k ^ (m & 1)) + 2 * (j ^ (m >> 1)) + i)
                for i in range(2)
                for j in range(2)
                for k in range(2)
            ]
            parts.append(lax.ppermute(shard, ("a", "b", "c"), pairs))
        return parts

    *b4, bias_grad, head_grad = call(
        functools.partial(heads_and_fourth, float(images * n_group), tasks, nm),
        [*quads, low_kept, low_kept, sds(8, L), sds(8, L), sds(tasks, L)],
        (
            q_arr, stats, errors, head_all, head_mine, pooled,
            fourth[2], fourth[3], second[0], w_fourth, params, big,
        ),
        back_scratch + [vm((images, L), f32)],
        flops=flops_conv,
    )
    g3 = scatter_quarters(b4[:4])
    dw4 = grad_of(fourth[4], b4[4], (g3[3],))
    *b3, dw4 = run(
        third_backward,
        [*quads, low_kept, sds(8, L)],
        (q_arr, *g3[:3], third[1], third[2], w_third, params, big),
        back_scratch,
        through=(dw4,),
    )
    r4 = over_z(dw4)
    g2 = scatter_quarters(b3[:4])
    dw3 = grad_of(third[3], b3[4], (g2[3],))
    *b2, dw3 = run(
        second_backward,
        [*quads, low_kept, low_kept, sds(8, L)],
        (q_arr, *g2[:3], b4[5], first[1], second[1], second[2], w_second, params, big),
        back_scratch,
        through=(dw3,),
    )
    r3 = over_z(dw3)
    g1 = scatter_quarters(b2[:4])
    dw2 = grad_of(second[3], b2[4], (g1[3],), own_rows if direct else 0)
    if direct:
        dw2, give2 = dw2
        got2 = flip(give2, "a")
    twice = [Keep(2 * rows, L, dtype=bf16)] * 3 + [low_kept] * 2
    b1 = run(
        first_backward,
        [*twice, low_kept, low_kept, sds(8, L)],
        (c_arr, *g1[:3], b2[5], *first[2:], w_first, w_short, params, big),
        [vm((cin, 10 * L), bf16), vm((rows, 10 * L), bf16), vm((rows, L), f32)],
        ties=(dw2,),
    )

    p0, p1, p2, *p3 = b1[:5]
    p1, p3 = flip(p1, "c"), [flip(p, "c") for p in p3]
    (send,) = call(
        add_halves,
        [sds(2 * rows, L, dtype=bf16)],
        (Far(p2), *p3),
        scalars=0,
        ties=(got2,) if direct else (),
    )
    across = flip(send, "b")
    smalls = [head_grad, b1[-1], b2[-1], b3[-1], b4[-1]]
    small_rows = sum(v.shape[0] for v in smalls)
    smalls.append(jnp.zeros((-small_rows % 16 or 16, L), f32))
    small_rows += smalls[-1].shape[0]
    slot_rows = r_first + r_short + small_rows
    grad_args = (q_arr, feats, b1[5], b1[6], big)
    grad_scratch = [vm((rows, cin), bf16), vm((rows, 10 * L), bf16)]

    def low(count):
        return sds(count, L, dtype=bf16)

    def give_a(shards, sizes, ties):
        count = sum(sizes)
        keep, give = call(
            functools.partial(pick_a, sizes),
            [low(count)] * 2,
            (q_arr, *shards),
            ties=ties,
        )
        return keep, flip(give, "a")

    def sum_a(keep, got, ties=()):
        return call(add_low, [low(keep.shape[0])], (Far(keep), Far(got)), scalars=0, ties=ties)[0]

    if direct:
        slots, give1 = call(
            functools.partial(first_weight_grad, (r_first, r_short)),
            [Keep(n_group * slot_rows // 2, L, dtype=bf16)] * 2,
            grad_args + tuple(smalls),
            grad_scratch + [vm((n_group * slot_rows, L), bf16)],
            ties=(send,),
        )
        got1 = flip(give1, "a")
        pair43 = give_a((r4, r3), (own_rows, own_rows), (slots,))
        (total,) = call(add_three, [low(2 * rows)], (Far(p0), Far(p1), Far(across)), scalars=0, ties=(pair43[0],))
        (dw21,) = call(
            functools.partial(sum_beside, n_z),
            [Keep(n_z * (own_rows + slot_rows), L, dtype=bf16)],
            (dw2, got2, slots, got1),
            scalars=0,
            ties=(total,),
        )
        shard21 = over_z(dw21)
    else:
        dw1, dws = call(
            functools.partial(first_weight_grad, None),
            [sds(9 * cin, L, dtype=bf16), sds(cin, L, dtype=bf16)],
            grad_args,
            grad_scratch,
        )
        small = jnp.concatenate(smalls, axis=0).astype(bf16)
        dw21 = [
            dw2.reshape(n_group, own_rows, L),
            dw1.reshape(n_group, r_first, L),
            dws.reshape(n_group, r_short, L),
            jnp.broadcast_to(small[None], (n_group, *small.shape)),
        ]
        dw21 = jnp.concatenate(dw21, axis=1)
        shard21 = lax.psum_scatter(dw21, ("z", "a"), scatter_dimension=0)
        pair43 = give_a((r4, r3), (own_rows, own_rows), ())
        (total,) = call(add_three, [low(2 * rows)], (Far(p0), Far(p1), Far(across)), scalars=0)

    shard43 = sum_a(*pair43, ties=(dw21,))
    places43 = to_places(shard43)
    swapped = swap_ac(total)
    conv_fourth_grad, conv_third_grad = call(
        assemble, [sds(own_rows, channels)] * 2, (shared_arr, *places43)
    )
    (input_grad,) = call(
        input_grad_kernel,
        [sds(grid * grid, cin // 4, images)],
        (q_arr, micro_order, own_big, Pick(total, swapped)),
        ties=(conv_third_grad,),
    )
    places = to_places(shard21)
    group = 2 * iz + ic
    group_arr = jnp.stack([shared, group]).astype(jnp.int32)
    wide_outs = [sds(own_rows, channels), sds(r_first, channels), sds(r_short, channels)]
    if direct:
        conv_second_grad, conv_first_grad, conv_short_grad, gains_grad, biases_grad, head_weight_grad = call(
            functools.partial(assemble_last, block, tasks),
            wide_outs + [sds(5, block), sds(5, block), sds(tasks, block)],
            (group_arr, *places),
            [vm((small_rows, channels), f32)],
        )
    else:
        conv_second_grad, conv_first_grad, conv_short_grad, wide_small = call(
            assemble, wide_outs + [sds(small_rows, channels)], (group_arr, *places)
        )
        own_small = lax.dynamic_slice_in_dim(wide_small, group * block, block, 1)
        head_weight_grad = own_small[:tasks]
        n1, n2, n3, n4 = (own_small[tasks + 8 * i : tasks + 8 * (i + 1)] for i in range(4))
        gains_grad = jnp.stack([n1[0], n1[2], n2[0], n3[0], n4[0]])
        biases_grad = jnp.stack([n1[1], n1[3], n2[1], n3[1], n4[1]])
    input_grad = input_grad.reshape(grid, grid, cin // 4, images).transpose(3, 0, 1, 2)

    moved = lax.ppermute(
        pooled,
        ("a", "b", "c"),
        [(4 * i + 2 * j + k, 4 * j + 2 * k + i) for i in range(2) for j in range(2) for k in range(2)],
    )
    spots = jnp.arange(images, dtype=jnp.int32)
    inverse = jnp.sum(
        jnp.where(micro_order[0][None, :] == spots[:, None], spots[None, :], 0), axis=1
    )
    pooled_out = moved[inverse]

    return (
        pooled_out,
        input_grad,
        conv_first_grad,
        conv_short_grad,
        conv_second_grad,
        conv_third_grad,
        conv_fourth_grad,
        gains_grad,
        biases_grad,
        head_weight_grad.T,
        bias_grad[0, :tasks],
    )


def solution(mesh):
    sections, groups = mesh.shape["section"], mesh.shape["dp"]
    fine = Mesh(mesh.devices.reshape(2, sections // 2, groups // 2, 2), ("a", "b", "z", "c"))
    dp, section = ("z", "c"), ("a", "b")
    return jax.shard_map(
        body,
        mesh=fine,
        in_specs=(
            P(dp, None, None, None),
            P(dp),
            P(dp, None),
            P(dp, None),
            P(dp, None),
            P(dp, None),
            P(dp, None),
            P(dp, None),
            P(dp, None),
            P(None, dp),
            P(None, dp),
            P(dp, None),
            P(),
        ),
        out_specs=(
            P(dp, section),
            P(dp, None, None, section),
            P(dp, None),
            P(dp, None),
            P(dp, None),
            P(dp, None),
            P(dp, None),
            P(None, dp),
            P(None, dp),
            P(dp, None),
            P(),
        ),
        check_vma=False,
    )
```

```python
import functools

import jax
import jax.numpy as jnp
from jax import lax
from jax.experimental import pallas as pl
from jax.experimental.pallas import tpu as pltpu
from jax.sharding import Mesh, PartitionSpec as P

MICRO = 6
FW_STEPS = 20
EPSILON = 1e-05
SOFTMAX_HEAT = 0.01
HIGHEST = lax.Precision.HIGHEST

f32 = jnp.float32
bf16 = jnp.bfloat16
L = 128

PLANE_TAPS = ((4, -1), (3, 5), (1, 7), (0, 2, 6, 8))
FIRST_COLS = tuple(tap for taps in PLANE_TAPS for tap in taps)


def room(kernel, flops):
    if flops:
        return 50
    name = getattr(kernel, "func", kernel).__name__
    return 51 if name in ("prepare", "pack", "pack_rest", "relay", "unpack") else 28


class Keep:
    def __init__(self, *shape, dtype=f32):
        self.shape, self.dtype = shape, dtype


class Far:
    def __init__(self, x):
        self.first, self.shape, self.dtype, self.size = x, x.shape, x.dtype, x.size


class Half:
    def __init__(self, x):
        self.first, self.shape, self.dtype, self.size = x, (x.shape[0], L), x.dtype, x.size // 2


class Pick:
    def __init__(self, first, other):
        self.first, self.other = first, other
        self.shape, self.dtype, self.size = first.shape, first.dtype, first.size


class Buf:
    def __init__(self, ref, start, wait, out=False):
        self.ref, self.start, self.wait = ref, start, wait
        self.out, self.started, self.ready = out, not out, out
        self.shape, self.dtype = ref.shape, ref.dtype
        if not out:
            start()

    def get(self):
        if not self.ready:
            self.wait()
            self.ready = True

    def __getitem__(self, at):
        self.get()
        return self.ref[at]

    def __setitem__(self, at, value):
        self.ref[at] = value

    def send(self):
        if not self.started:
            self.start()
            self.started = True


def call(kernel, outs, args, scratch=(), scalars=1, flops=0, ties=(), through=()):
    def far(a):
        return isinstance(a, (Far, Half, Pick, Keep))

    flat, specs, places = [], [], []
    for k, a in enumerate(args):
        places.append(len(flat))
        if k < scalars:
            space = pltpu.SMEM
        else:
            space = pltpu.HBM if far(a) else pltpu.VMEM
        for x in (a.first, a.other) if isinstance(a, Pick) else (a.first,) if far(a) else (a,):
            flat.append(x)
            specs.append(pl.BlockSpec(memory_space=space))
    n_args = len(flat)
    specs += [pl.BlockSpec(memory_space=pl.ANY)] * (len(ties) + len(through))
    far_in = [k for k, a in enumerate(args) if k >= scalars and far(a)]
    far_out = [k for k, o in enumerate(outs) if far(o)]
    buffers = [pltpu.VMEM(args[k].shape, args[k].dtype) for k in far_in]
    buffers += [pltpu.VMEM(outs[k].shape, outs[k].dtype) for k in far_out]
    n_in = n_args + len(ties) + len(through)
    n_outs = len(outs)
    n_bufs = len(buffers)

    def run(*refs):
        ins, results = list(refs[:n_args]), list(refs[n_in : n_in + n_outs])
        rest = refs[n_in + n_outs + len(through) :]
        temps, sems, rest = rest[:n_bufs], rest[n_bufs], rest[n_bufs + 1 :]
        given = []
        for k in range(len(args)):
            src = ins[places[k]]
            if k in far_in:
                n = far_in.index(k)
                if isinstance(args[k], Half):
                    src = src.at[:, pl.ds(pl.multiple_of((ins[0][0] & 1) * L, L), L)]
                copy = pltpu.make_async_copy(src, temps[n], sems.at[n])
                start = copy.start
                if isinstance(args[k], Pick):
                    second = pltpu.make_async_copy(ins[places[k] + 1], temps[n], sems.at[n])

                    def start(copy=copy, second=second):
                        pl.when(ins[0][1] == 1)(copy.start)
                        pl.when(ins[0][1] == 0)(second.start)

                src = Buf(temps[n], start, copy.wait)
            given.append(src)
        made = []
        for k in range(n_outs):
            out = results[k]
            if k in far_out:
                n = len(far_in) + far_out.index(k)
                copy = pltpu.make_async_copy(temps[n], out, sems.at[n])
                out = Buf(temps[n], copy.start, copy.wait, out=True)
            made.append(out)
        kernel(*given, *made, *rest)
        for x in given:
            if isinstance(x, Buf):
                x.get()
        made = [x for x in made if isinstance(x, Buf)]
        for x in made:
            x.send()
        for x in made:
            x.wait()

    outs = [sds(*o.shape, dtype=o.dtype) if far(o) else o for o in outs]
    size = sum(a.size * a.dtype.itemsize for a in flat) + sum(o.size * o.dtype.itemsize for o in outs)
    return pl.pallas_call(
        run,
        out_shape=tuple(outs) + tuple(sds(*x.shape, dtype=x.dtype) for x in through),
        in_specs=specs,
        out_specs=tuple(
            pl.BlockSpec(memory_space=pltpu.HBM if k in far_out else pltpu.VMEM) for k in range(n_outs)
        )
        + tuple(pl.BlockSpec(memory_space=pl.ANY) for _ in through),
        scratch_shapes=buffers + [pltpu.SemaphoreType.DMA((max(n_bufs, 1),))] + list(scratch),
        input_output_aliases={n_args + len(ties) + k: n_outs + k for k in range(len(through))},
        compiler_params=pltpu.CompilerParams(vmem_limit_bytes=room(kernel, flops) << 20),
        cost_estimate=pl.CostEstimate(flops=int(flops), bytes_accessed=int(size), transcendentals=0),
    )(*flat, *ties, *through)


def sds(*shape, dtype=f32):
    return jax.ShapeDtypeStruct(shape, dtype)


def nt_dot(x, y):
    return lax.dot_general(x, y, (((1,), (1,)), ((), ())), preferred_element_type=f32)


def tn_dot(x, y):
    return lax.dot_general(x, y, (((0,), (0,)), ((), ())), preferred_element_type=f32)


def sigmoid(v):
    return 0.5 + 0.5 * jnp.tanh(0.5 * v)


def pixel_mask(i, big):
    return None if (i // 4 < 2 and i % 4 < 2) else big


def masked(value, i, big):
    return value if pixel_mask(i, big) is None else value * big


def per_micro(value, nm):
    rows, lanes = value.shape
    return jnp.sum(value.reshape(nm, rows // nm, lanes), axis=1)


def spread_micro(value, im):
    nm, lanes = value.shape
    return jnp.broadcast_to(value[:, None, :], (nm, im // nm, lanes)).reshape(im, lanes)


def blk(ref, i, im):
    return ref[i * im : (i + 1) * im, :]


def norm_forward(p_ref, xhat_ref, inv_ref, big, nm):
    im = big.shape[0]
    total = per_micro(4.0 + 12.0 * big, nm)
    acc = jnp.zeros_like(big)
    for i in range(16):
        acc = acc + masked(blk(p_ref, i, im), i, big)
    mean = spread_micro(per_micro(acc, nm) / total, im)
    acc = jnp.zeros_like(big)
    for i in range(16):
        cen = blk(p_ref, i, im) - mean
        acc = acc + masked(cen * cen, i, big)
    inv = lax.rsqrt(per_micro(acc, nm) / total + EPSILON)
    inv_ref[...] = jnp.concatenate([inv, jnp.zeros((8 - nm, inv.shape[1]), f32)], axis=0)
    inv = spread_micro(inv, im)
    for i in range(16):
        xhat = (blk(p_ref, i, im) - mean) * inv
        p_ref[i * im : (i + 1) * im, :] = xhat
        xhat_ref[i * im : (i + 1) * im, :] = xhat.astype(bf16)


def norm_backward(dy_ref, xhat_ref, inv_ref, gain, big, nm, out_ref):
    im = big.shape[0]
    total = per_micro(4.0 + 12.0 * big, nm)
    sum_dy = jnp.zeros_like(big)
    sum_dx = jnp.zeros_like(big)
    for i in range(16):
        dy = blk(dy_ref, i, im)
        sum_dy = sum_dy + dy
        sum_dx = sum_dx + dy * blk(xhat_ref, i, im).astype(f32)
    sum_dy = per_micro(sum_dy, nm)
    sum_dx = per_micro(sum_dx, nm)
    mean_dy = spread_micro(sum_dy / total, im)
    mean_dx = spread_micro(sum_dx / total, im)
    scale = spread_micro(inv_ref[0:nm, :] * gain, im)
    for i in range(16):
        off = masked(mean_dy + blk(xhat_ref, i, im).astype(f32) * mean_dx, i, big)
        grad = scale * (blk(dy_ref, i, im) - off)
        out_ref[i * im : (i + 1) * im, :] = grad.astype(bf16)
    return jnp.sum(sum_dx, axis=0, keepdims=True), jnp.sum(sum_dy, axis=0, keepdims=True)


def load_weights(q_ref, w_ref, ws):
    channels = 4 * L
    q = q_ref[0]
    for t in range(9):
        for j in range(4):
            start = pl.multiple_of(t * channels + (q ^ j) * L, L)
            ws[j * L : (j + 1) * L, t * L : (t + 1) * L] = w_ref[pl.ds(start, L), :]


def row_taps(r):
    return (3 * L if r == 3 else 0), (6 * L if r == 0 else 9 * L)


def conv_forward(q_ref, x_refs, w_ref, xs, ws, y, p, im):
    for j in (0, 1, 3, 2):
        xs[:, j * L : (j + 1) * L] = x_refs[j][...]
    xs.send()
    load_weights(q_ref, w_ref, ws)
    for r in range(4):
        lo, hi = row_taps(r)
        rows = slice(r * 4 * im, (r + 1) * 4 * im)
        y[rows, lo:hi] = jnp.dot(xs[rows, :], ws[:, lo:hi], preferred_element_type=f32)
    for r in range(4):
        for c in range(4):
            acc = None
            for t in range(9):
                ri, ci = r + t // 3 - 1, c + t % 3 - 1
                if 0 <= ri < 4 and 0 <= ci < 4:
                    i = ri * 4 + ci
                    term = y[i * im : (i + 1) * im, t * L : (t + 1) * L]
                    acc = term if acc is None else acc + term
            p[(r * 4 + c) * im : (r * 4 + c + 1) * im, :] = acc


def spread_taps(dp_ref, d, im, rows_at, all_taps):
    for r in range(4):
        lo, hi = (0, 9 * L) if all_taps else row_taps(r)
        for c in range(4):
            at = rows_at + (r * 4 + c) * im
            for t in range(lo // L, hi // L):
                ro, co = r - t // 3 + 1, c - t % 3 + 1
                if 0 <= ro < 4 and 0 <= co < 4:
                    value = blk(dp_ref, ro * 4 + co, im)
                else:
                    value = jnp.zeros((im, L), bf16)
                d[at : at + im, t * L : (t + 1) * L] = value


def conv_back_input(q_ref, dp_ref, w_ref, ws, d, outs, im):
    dp_ref.send()
    load_weights(q_ref, w_ref, ws)
    spread_taps(dp_ref, d, im, 0, False)
    for r in range(4):
        lo, hi = row_taps(r)
        rows = slice(r * 4 * im, (r + 1) * 4 * im)
        dx = nt_dot(d[rows, lo:hi], ws[:, lo:hi])
        for j in range(4):
            outs[j][rows, :] = dx[:, j * L : (j + 1) * L].astype(outs[j].dtype)


def load_plane(x, k, big, xs, im):
    wide = jnp.concatenate([big, big], axis=1).astype(bf16)
    for i in range(16):
        pixel = (2 * (i // 4) + k // 2) * 8 + 2 * (i % 4) + k % 2
        xs[i * im : (i + 1) * im, :] = masked(blk(x, pixel, im), i, wide)


def first_forward(nm, c_ref, x, w, w_short, params, big_ref, h, s, xh1, inv1, xh2, inv2, xs, wsc, y, p1, p2):
    big = big_ref[...]
    im = big.shape[0]
    cin = 2 * L
    col = 0
    for k, taps in enumerate(PLANE_TAPS):
        for n, t in enumerate(taps):
            src = w_short[...] if t < 0 else w[t * cin : (t + 1) * cin, :]
            wsc[:, (col + n) * L : (col + n + 1) * L] = src
        cols = slice(col * L, (col + len(taps)) * L)
        load_plane(x, k, big, xs, im)
        y[:, cols] = jnp.dot(xs[...], wsc[:, cols], preferred_element_type=f32)
        col += len(taps)
    for r in range(4):
        for c in range(4):
            o = r * 4 + c
            acc = None
            for n, t in enumerate(FIRST_COLS):
                if t < 0:
                    p2[o * im : (o + 1) * im, :] = y[o * im : (o + 1) * im, n * L : (n + 1) * L]
                    continue
                ri = r - 1 if t // 3 == 0 else r
                ci = c - 1 if t % 3 == 0 else c
                if ri >= 0 and ci >= 0:
                    i = ri * 4 + ci
                    term = y[i * im : (i + 1) * im, n * L : (n + 1) * L]
                    acc = term if acc is None else acc + term
            p1[o * im : (o + 1) * im, :] = acc
    norm_forward(p1, xh1, inv1, big, nm)
    norm_forward(p2, xh2, inv2, big, nm)
    for i in range(16):
        rows = slice(i * im, (i + 1) * im)
        v = blk(p1, i, im) * params[0:1, :] + params[5:6, :]
        h[rows, :] = masked(v * sigmoid(v), i, big).astype(bf16)
        v = blk(p2, i, im) * params[1:2, :] + params[6:7, :]
        s[rows, :] = masked(v, i, big).astype(bf16)


def second_forward(nm, q_ref, x0, x1, x2, x3, w, params, big_ref, s, out, xh, inv, xs, ws, y, p):
    big = big_ref[...]
    im = big.shape[0]
    conv_forward(q_ref, (x0, x1, x2, x3), w, xs, ws, y, p, im)
    norm_forward(p, xh, inv, big, nm)
    for i in range(16):
        rows = slice(i * im, (i + 1) * im)
        u = blk(p, i, im) * params[2:3, :] + params[7:8, :]
        u = masked(u, i, big).astype(bf16).astype(f32)
        v = u + s[rows, :].astype(f32)
        out[rows, :] = masked(v * sigmoid(v), i, big).astype(bf16)


def third_forward(nm, q_ref, x0, x1, x2, x3, w, params, big_ref, out, xh, inv, xs, ws, y, p):
    big = big_ref[...]
    im = big.shape[0]
    conv_forward(q_ref, (x0, x1, x2, x3), w, xs, ws, y, p, im)
    norm_forward(p, xh, inv, big, nm)
    for i in range(16):
        rows = slice(i * im, (i + 1) * im)
        v = blk(p, i, im) * params[3:4, :] + params[8:9, :]
        out[rows, :] = masked(v * sigmoid(v), i, big).astype(bf16)


def fourth_forward(
    nm, q_ref, x0, x1, x2, x3, w, params, big_ref, res, head, pooled, logits, xh, inv, xs, ws, y, p
):
    big = big_ref[...]
    im = big.shape[0]
    conv_forward(q_ref, (x0, x1, x2, x3), w, xs, ws, y, p, im)
    norm_forward(p, xh, inv, big, nm)
    acc = jnp.zeros_like(big)
    for i in range(16):
        rows = slice(i * im, (i + 1) * im)
        v = blk(p, i, im) * params[4:5, :] + params[9:10, :] + res[rows, :].astype(f32)
        acc = acc + masked(v * sigmoid(v), i, big)
    pool = acc / (4.0 + 12.0 * big)
    pooled[...] = pool
    logits[...] = jnp.dot(pool.astype(bf16), head[...], preferred_element_type=f32)


def head_errors(mine, other, bias, labels, tasks, errors, stats):
    logits = mine[...] + other[...] + bias[0:1, :]
    lane = lax.broadcasted_iota(jnp.int32, logits.shape, 1)
    err = jnp.where(lane < tasks, sigmoid(logits) - labels[...], 0.0)
    errors[...] = err
    gram = lax.dot_general(err, err, (((0,), (0,)), ((), ())), precision=HIGHEST, preferred_element_type=f32)
    stats[0:tasks, :] = gram[0:tasks, :]
    stats[tasks:, :] = jnp.broadcast_to(jnp.sum(err, axis=0, keepdims=True), (stats.shape[0] - tasks, L))


def head_weights(count, tasks, stats, errors, head_all, head_mine, pooled, dz, bias_grad, head_grad):
    inner = tn_dot(head_all[...], head_all[...])
    gram = stats[0:tasks, :] * inner[0:tasks, :] / count
    row = lax.broadcasted_iota(jnp.int32, (tasks, L), 0)
    lane = lax.broadcasted_iota(jnp.int32, (tasks, L), 1)
    weight_row = jnp.where(lane[0:1, :] < tasks, 1.0 / tasks, 0.0)
    for step in range(FW_STEPS):
        score = -jnp.sum(gram * weight_row, axis=1, keepdims=True) / SOFTMAX_HEAT
        power = jnp.exp(score - jnp.max(score, axis=0, keepdims=True))
        corner = power / jnp.sum(power, axis=0, keepdims=True)
        corner = jnp.sum(jnp.where(row == lane, corner, 0.0), axis=0, keepdims=True)
        rate = 2.0 / (step + 2.0)
        weight_row = (1.0 - rate) * weight_row + rate * corner
    scaled = errors[...] * weight_row
    dz[...] = lax.dot_general(
        scaled,
        head_mine[...].astype(f32),
        (((1,), (1,)), ((), ())),
        precision=HIGHEST,
        preferred_element_type=f32,
    )
    bias_grad[...] = jnp.broadcast_to(weight_row * stats[tasks : tasks + 1, :], bias_grad.shape)
    grad = lax.dot_general(
        scaled,
        pooled[...].astype(bf16).astype(f32),
        (((0,), (0,)), ((), ())),
        precision=HIGHEST,
        preferred_element_type=f32,
    )
    head_grad[...] = grad[0:tasks, :]


def fourth_backward(
    nm, q_ref, dz, xh, inv, res, w, params, big_ref, o0, o1, o2, o3, dp, d_res, norm, ws, d, dy
):
    big = big_ref[...]
    im = big.shape[0]
    out_grad = dz[...] / (4.0 + 12.0 * big)
    for i in range(16):
        rows = slice(i * im, (i + 1) * im)
        v = blk(xh, i, im).astype(f32) * params[4:5, :] + params[9:10, :] + res[rows, :].astype(f32)
        sig = sigmoid(v)
        grad = masked(out_grad * (sig * (1.0 + v * (1.0 - sig))), i, big)
        dy[rows, :] = grad
        d_res[rows, :] = grad.astype(bf16)
    dgain, dbias = norm_backward(dy, xh, inv, params[4:5, :], big, nm, dp)
    norm[...] = jnp.concatenate([dgain, dbias, jnp.zeros((6, L), f32)], axis=0)
    conv_back_input(q_ref, dp, w, ws, d, (o0, o1, o2, o3), im)


def heads_and_fourth(
    count, tasks, nm, q_ref, stats, errors, head_all, head_mine, pooled, xh, inv, res, w, params, big_ref,
    o0, o1, o2, o3, dp, d_res, norm, bias_grad, head_grad, ws, d, dy, dz,
):
    head_weights(count, tasks, stats, errors, head_all, head_mine, pooled, dz, bias_grad, head_grad)
    fourth_backward(
        nm, q_ref, dz, xh, inv, res, w, params, big_ref, o0, o1, o2, o3, dp, d_res, norm, ws, d, dy
    )


def third_backward(
    nm, q_ref, g0, g1, g2, xh, inv, w, params, big_ref, o0, o1, o2, o3, dp, norm, ws, d, dy
):
    big = big_ref[...]
    im = big.shape[0]
    for i in range(16):
        rows = slice(i * im, (i + 1) * im)
        grad = g0[rows, :].astype(f32) + g1[rows, :].astype(f32) + g2[rows, :].astype(f32)
        grad = grad.astype(bf16).astype(f32)
        v = blk(xh, i, im).astype(f32) * params[3:4, :] + params[8:9, :]
        sig = sigmoid(v)
        dy[rows, :] = masked(grad * (sig * (1.0 + v * (1.0 - sig))), i, big)
    dgain, dbias = norm_backward(dy, xh, inv, params[3:4, :], big, nm, dp)
    norm[...] = jnp.concatenate([dgain, dbias, jnp.zeros((6, L), f32)], axis=0)
    conv_back_input(q_ref, dp, w, ws, d, (o0, o1, o2, o3), im)


def second_backward(
    nm, q_ref, g0, g1, g2, d_res, s, xh, inv, w, params, big_ref, o0, o1, o2, o3, dp, ds, norm, ws, d, dy
):
    big = big_ref[...]
    im = big.shape[0]
    for i in range(16):
        rows = slice(i * im, (i + 1) * im)
        grad = g0[rows, :].astype(f32) + g1[rows, :].astype(f32) + g2[rows, :].astype(f32)
        grad = grad + d_res[rows, :].astype(f32)
        u = blk(xh, i, im).astype(f32) * params[2:3, :] + params[7:8, :]
        v = masked(u, i, big).astype(bf16).astype(f32) + s[rows, :].astype(f32)
        sig = sigmoid(v)
        grad = masked(grad * (sig * (1.0 + v * (1.0 - sig))), i, big).astype(bf16)
        ds[rows, :] = grad
        dy[rows, :] = grad.astype(f32)
    dgain, dbias = norm_backward(dy, xh, inv, params[2:3, :], big, nm, dp)
    norm[...] = jnp.concatenate([dgain, dbias, jnp.zeros((6, L), f32)], axis=0)
    conv_back_input(q_ref, dp, w, ws, d, (o0, o1, o2, o3), im)


def spread_first(dp1, dps, d, im, rows_at):
    for i in range(16):
        r, c = i // 4, i % 4
        at = rows_at + i * im
        for n, t in enumerate(FIRST_COLS):
            if t < 0:
                value = blk(dps, i, im)
            else:
                ro = r + 1 if t // 3 == 0 else r
                co = c + 1 if t % 3 == 0 else c
                value = blk(dp1, ro * 4 + co, im) if ro < 4 and co < 4 else jnp.zeros((im, L), bf16)
            d[at : at + im, n * L : (n + 1) * L] = value


def first_backward(
    nm, c_ref, g0, g1, g2, ds, xh1, inv1, xh2, inv2, w, w_short, params, big_ref, *refs,
):
    outs, (dp1, dps, norm, ws, d, dy) = refs[:5], refs[5:]
    big = big_ref[...]
    im = big.shape[0]
    half, part = c_ref[0], c_ref[1]
    cin = 2 * L
    for i in range(16):
        rows = slice(i * im, (i + 1) * im)
        grad = g0[rows, :].astype(f32) + g1[rows, :].astype(f32) + g2[rows, :].astype(f32)
        grad = grad.astype(bf16).astype(f32)
        v = blk(xh1, i, im).astype(f32) * params[0:1, :] + params[5:6, :]
        sig = sigmoid(v)
        dy[rows, :] = masked(grad * (sig * (1.0 + v * (1.0 - sig))), i, big)
    gain1, bias1 = norm_backward(dy, xh1, inv1, params[0:1, :], big, nm, dp1)
    for i in range(16):
        rows = slice(i * im, (i + 1) * im)
        dy[rows, :] = masked(ds[rows, :].astype(f32), i, big)
    gain2, bias2 = norm_backward(dy, xh2, inv2, params[1:2, :], big, nm, dps)
    norm[...] = jnp.concatenate([gain1, bias1, gain2, bias2, jnp.zeros((4, L), f32)], axis=0)
    wide = cin // 4
    for n, t in enumerate(FIRST_COLS):
        for j in range(4):
            start = (half ^ (j & 1)) * 2 * wide + (part ^ (j >> 1)) * wide
            if t < 0:
                src = w_short[pl.ds(pl.multiple_of(start, wide), wide), :]
            else:
                src = w[pl.ds(pl.multiple_of(t * cin + start, wide), wide), :]
            ws[j * wide : (j + 1) * wide, n * L : (n + 1) * L] = src
    spread_first(dp1, dps, d, im, 0)
    col = 0
    for k, taps in enumerate(PLANE_TAPS):
        cols = slice(col * L, (col + len(taps)) * L)
        dx = nt_dot(d[:, cols], ws[:, cols])
        pair, side = k // 2, k % 2
        for j in range(4):
            ref = outs[j] if j < 3 else outs[3 + pair]
            at = pair * 16 * im if j < 3 else 0
            rows = slice(at, at + 16 * im)
            ref[rows, side * wide : (side + 1) * wide] = dx[:, j * wide : (j + 1) * wide].astype(ref.dtype)
        col += len(taps)


def halves(whole, outs):
    rows = outs[0].shape[0]
    for k, out in enumerate(outs):
        out[...] = whole[k * rows : (k + 1) * rows, :]


def weight_grad(block, q_ref, x, dp, *refs):
    if block:
        *outs, d, out = refs
    else:
        out, d = refs
    im = dp.shape[0] // 16
    q, a = q_ref[0], q_ref[2]
    total = out.shape[0]
    spread_taps(dp, d, im, 0, True)
    step = L // 2 if block else L
    for n in range(3):
        cols = slice(n * 3 * L, (n + 1) * 3 * L)
        grad = tn_dot(x[...], d[:, cols]).astype(bf16)
        for t in range(3):
            for j in range(4):
                for part in range(L // step):
                    start = (3 * n + t) * 4 * L + (q ^ j) * L + part * step
                    if block:
                        at = start // block
                        start = ((at & 1) ^ a) * (total // 2) + (at // 2) * block + start % block
                    start = pl.multiple_of(start, step)
                    value = grad[j * L + part * step : j * L + (part + 1) * step, t * L : (t + 1) * L]
                    out[pl.ds(start, step), :] = value
    if block:
        halves(out, outs)


def first_weight_grad(blocks, q_ref, x, dp1, dps, big_ref, *refs):
    if blocks:
        *smalls, keep, give, xs, d, out = refs
        small = jnp.concatenate([v[...] for v in smalls], axis=0).astype(bf16)
        n1, n2 = blocks
        per = n1 + n2 + small.shape[0]
        total = out.shape[0]
        a = q_ref[2]
    else:
        out, out_short, xs, d = refs
    big = big_ref[...]
    im = big.shape[0]
    cin = 2 * L

    def place(at):
        return pl.multiple_of(((at & 1) ^ a) * (total // 2) + (at // 2) * per, 16)

    spread_first(dp1, dps, d, im, 0)
    col = 0
    for k, taps in enumerate(PLANE_TAPS):
        cols = slice(col * L, (col + len(taps)) * L)
        load_plane(x, k, big, xs, im)
        grad = tn_dot(xs[...], d[:, cols]).astype(bf16)
        for n, t in enumerate(taps):
            value = grad[:, n * L : (n + 1) * L]
            if not blocks:
                if t < 0:
                    out_short[...] = value
                else:
                    out[t * cin : (t + 1) * cin, :] = value
                continue
            size, base, row = (n2, n1, 0) if t < 0 else (n1, 0, t * cin)
            done = 0
            while done < cin:
                at, inner = (row + done) // size, (row + done) % size
                count = min(cin - done, size - inner)
                start = pl.multiple_of(place(at) + base + inner, 16)
                out[pl.ds(start, count), :] = value[done : done + count, :]
                done += count
        col += len(taps)
    if blocks:
        for at in range(cin // n2):
            start = pl.multiple_of(place(at) + n1 + n2, 16)
            out[pl.ds(start, small.shape[0]), :] = small
        halves(out, (keep, give))


def sum_beside(n_z, x, x_got, y, y_got, out):
    at = 0
    sizes = (x_got.shape[0] // n_z, y_got.shape[0] // n_z)
    for z in range(n_z):
        for kept, got, rows in ((x, x_got, sizes[0]), (y, y_got, sizes[1])):
            cut = slice(z * rows, (z + 1) * rows)
            out[at : at + rows, :] = (kept[cut, :].astype(f32) + got[cut, :].astype(f32)).astype(bf16)
            at += rows


def add_low(x, y, out):
    out[...] = (x[...].astype(f32) + y[...].astype(f32)).astype(bf16)


def add_halves(x, low, high, out):
    rows = low.shape[0]
    for k, y in enumerate((low, high)):
        cut = slice(k * rows, (k + 1) * rows)
        out[cut, :] = (x[cut, :].astype(f32) + y[...].astype(f32)).astype(bf16)


def add_three(x, y, z, out):
    out[...] = (x[...].astype(f32) + y[...].astype(f32) + z[...].astype(f32)).astype(bf16)


def pick_a(sizes, a_ref, *refs):
    *arrays, keep, give = refs
    at, source = 0, 0
    for rows in sizes:
        for out, a in ((keep, a_ref[2]), (give, 1 - a_ref[2])):
            cut = pl.ds(pl.multiple_of(source + a * rows, 8), rows)
            out[at : at + rows, :] = arrays[0][cut, :]
        at, source = at + rows, source + 2 * rows
        if source == arrays[0].shape[0]:
            arrays, source = arrays[1:], 0


def flip(value, axis):
    return lax.ppermute(value, axis, [(i, i ^ 1) for i in range(lax.axis_size(axis))])


def swap_ac(value):
    return lax.ppermute(value, ("a", "c"), [(1, 2), (2, 1)])


def sum_over(value, axis):
    count = lax.axis_size(axis)
    if count & (count - 1):
        return lax.psum(value, axis)
    step = 1
    while step < count:
        value = value + lax.ppermute(value, axis, [(i, i ^ step) for i in range(count)])
        step *= 2
    return value


def gather_quarters(h):
    from_b = flip(h, "b")
    from_c = flip(h, "c")
    return (h, from_c, Far(from_b), flip(from_b, "c"))


def scatter_quarters(parts):
    p0, p1, p2, p3 = parts
    first = flip(p1, "c")
    second = flip(p3, "c")
    send = (p2.astype(f32) + second.astype(f32)).astype(bf16)
    return (p0, first, Far(flip(send, "b")), send)


def pack(q_ref, first, short, norms, heads, mine, give):
    q = q_ref[0]
    n1, n2 = first.shape[0], short.shape[0]
    for out, part in ((mine, q), (give, q ^ 1)):
        cols = pl.ds(pl.multiple_of(part * L, L), L)
        out[0:n1, :] = first[:, cols]
        out[n1 : n1 + n2, :] = short[:, cols]
        out[n1 + n2 :, :] = heads[...]
        out[n1 + n2 : n1 + n2 + norms.shape[0], L - norms.shape[1] :] = norms[...]


def pack_rest(q_ref, *refs):
    count = len(refs) // 2
    for src, out in zip(refs[:count], refs[count:]):
        wide = out.shape[1]
        part = q_ref[1] if wide == L else q_ref[0] // 2
        out[...] = src[:, pl.ds(pl.multiple_of(part * wide, L), wide)]


def prepare(q_ref, order_ref, x, out, *bufs):
    images = order_ref.shape[1]
    pixels = out.shape[0] // images
    x.get()

    def move(j, carry):
        source = pl.ds(pl.multiple_of(order_ref[0, j] * pixels, pixels), pixels)
        target = pl.ds(pl.multiple_of(j * pixels, pixels), pixels)
        for k, buf in enumerate(bufs):
            buf[target, :] = x.ref[source, k * L : (k + 1) * L].astype(f32)
        return carry

    lax.fori_loop(0, images, move, 0, unroll=4)
    for p in range(pixels):
        for k, buf in enumerate(bufs):
            value = buf[pl.ds(p, images, stride=pixels), :].astype(bf16)
            out[p * images : (p + 1) * images, k * L : (k + 1) * L] = value


def relay(*refs):
    *parts, out = refs
    rows = parts[0].shape[0]
    for k, part in enumerate(parts):
        out[k * rows : (k + 1) * rows, :] = part[...]


def unpack(n1, n2, block, k_ref, mine, other, first, short, params, heads):
    here, q = k_ref[0], k_ref[1]
    rows = mine.shape[0] // 4
    for k in range(8):
        piece = (mine, other)[k % 2][k // 2 * rows : (k // 2 + 1) * rows, :]
        at = here ^ k
        first[pl.ds(pl.multiple_of(at * n1, 32), n1), :] = piece[0:n1, :]
        short[pl.ds(pl.multiple_of(at * n2, 32), n2), :] = piece[n1 : n1 + n2, :]
        head = piece[n1 + n2 : n1 + n2 + block, :]
        lane = lax.broadcasted_iota(jnp.int32, head.shape, 1)
        heads[pl.ds(pl.multiple_of(at * block, 32), block), :] = jnp.where(
            lane < L - block, head, jnp.zeros_like(head)
        )
        for side in range(L // block):
            @pl.when(at == q * (L // block) + side)
            def _():
                value = piece[n1 + n2 : n1 + n2 + 16, L - block :].astype(f32)
                params[:, side * block : (side + 1) * block] = value


def assemble(q_ref, p0, p1, p2, p3, *outs):
    q = q_ref[0]
    for j, part in enumerate((p0, p1, p2, p3)):
        cols = pl.ds(pl.multiple_of((q ^ j) * L, L), L)
        at = 0
        for out in outs:
            out[:, cols] = part[at : at + out.shape[0], :].astype(f32)
            at += out.shape[0]


def assemble_last(block, tasks, q_ref, p0, p1, p2, p3, *refs):
    *outs, gains, biases, heads, wide = refs
    assemble(q_ref, p0, p1, p2, p3, *outs, wide)
    start = q_ref[1] * block
    own = wide[:, pl.ds(pl.multiple_of(start // L * L, L), L)]
    value = own[:, :block]
    for k in range(1, L // block):
        value = jnp.where(start % L == k * block, own[:, k * block : (k + 1) * block], value)
    heads[...] = value[0:tasks, :]
    for out, side in ((gains, 0), (biases, 1)):
        rows = [tasks + side, tasks + 2 + side] + [tasks + 8 * k + side for k in (1, 2, 3)]
        out[...] = jnp.concatenate([value[r : r + 1, :] for r in rows], axis=0)


def input_grad_kernel(q_ref, order_ref, big_ref, parts, out):
    images = order_ref.shape[1]
    im = images
    wide = out.shape[1]
    spot = lax.broadcasted_iota(jnp.int32, (images, images), 1)
    pick = jnp.where(spot == jnp.transpose(jnp.broadcast_to(order_ref[0:1, :], (images, images))), 1.0, 0.0)
    pick = pick.astype(bf16)
    big = big_ref[0:1, :]
    for pr in range(2):
        for i in range(16):
            at = 16 * pr + i
            value = masked(tn_dot(blk(parts, at, im), pick), i, big)
            for pc in range(2):
                pixel = (2 * (i // 4) + pr) * 8 + 2 * (i % 4) + pc
                out[pixel, :, :] = value[pc * wide : (pc + 1) * wide, :]


def body(
    features, buckets, micro_order, labels, conv_first, conv_short, conv_second, conv_third, conv_fourth,
    norm_gains, norm_biases, head_weight, head_bias,
):
    ia, ib, iz, ic = (lax.axis_index(n) for n in ("a", "b", "z", "c"))
    n_group = lax.axis_size("z") * lax.axis_size("c")
    images, grid, _, cin = features.shape
    channels = conv_second.shape[1]
    tasks = head_weight.shape[1]
    quarter = 2 * ib + ic
    shared = 2 * ib + ia
    im = images
    nm = MICRO
    rows = 16 * im
    own = ia == ic
    q_arr = jnp.stack([quarter, own, ia, iz]).astype(jnp.int32)
    c_arr = jnp.stack([ic, ib]).astype(jnp.int32)

    block = channels // n_group
    r_first, r_short = conv_first.shape[0], conv_short.shape[0]
    n_z = lax.axis_size("z")

    small_rows = max(16, block)
    norms = jnp.concatenate([norm_gains, norm_biases], axis=0)
    norms = jnp.pad(norms, ((0, 6), (0, 0)))
    heads = jnp.pad(head_weight, ((0, small_rows - block), (0, L - tasks)))
    slot_rows = r_first + r_short + small_rows
    piece_t = sds(slot_rows, L, dtype=bf16)
    quarter_t = sds(conv_second.shape[0], L, dtype=bf16)
    pack_arr = jnp.stack([quarter, shared]).astype(jnp.int32)
    rest = call(pack_rest, [quarter_t], (pack_arr, conv_second))
    mine, give = call(
        pack, [piece_t, piece_t], (pack_arr, conv_first, conv_short, norms, heads), ties=rest
    )
    half_t = sds(conv_fourth.shape[0], 2 * L, dtype=bf16)
    rest += call(pack_rest, [quarter_t, half_t], (pack_arr, conv_third, conv_fourth), ties=(give,))
    rest = [lax.all_gather(w, ("z", "c"), axis=0, tiled=True) for w in rest]
    piece = jnp.where(own, mine, flip(give, "c"))

    parts = [piece]
    if n_z == 4:
        parts += [lax.ppermute(piece, "z", [(i, i ^ m) for i in range(n_z)]) for m in range(1, n_z)]

    ints = jnp.concatenate(
        [
            labels,
            buckets[:, None],
            micro_order.reshape(images, 1),
            jnp.zeros((images, L - tasks - 2), jnp.int32),
        ],
        axis=1,
    )
    ints = jnp.where(own, ints, flip(ints, "c"))
    order = ints[:, tasks + 1]
    flat = features.reshape(images * grid * grid, cin)
    (feats,) = call(
        prepare,
        [sds(images * grid * grid, cin, dtype=bf16)],
        (q_arr, order[None], Pick(flat, flip(flat, "c"))),
        [pltpu.VMEM((images * grid * grid, L), f32)] * (cin // L),
        scalars=2,
    )

    if n_z == 4:
        (stack,) = call(
            relay, [sds(n_z * slot_rows, L, dtype=bf16)], parts, scalars=0, ties=(feats,)
        )
        w_first, w_short, params, head_all = call(
            functools.partial(unpack, r_first, r_short, block),
            [
                sds(n_group * r_first, L, dtype=bf16),
                sds(n_group * r_short, L, dtype=bf16),
                sds(16, L),
                sds(channels, L, dtype=bf16),
            ],
            (jnp.stack([2 * iz + ia, quarter]).astype(jnp.int32), stack, flip(stack, "a")),
        )
    else:
        packed = lax.all_gather(piece, ("z", "a"), axis=0)
        w_first = packed[:, :r_first].reshape(n_group * r_first, L)
        w_short = packed[:, r_first : r_first + r_short].reshape(n_group * r_short, L)
        small = packed[:, r_first + r_short :]
        head_all = small[:, :block].reshape(channels, L)
        lane = lax.broadcasted_iota(jnp.int32, head_all.shape, 1)
        head_all = jnp.where(lane < tasks, head_all, jnp.zeros_like(head_all))
        params = small[:, :16, L - block :].transpose(1, 0, 2).reshape(16, channels)
        params = lax.dynamic_slice_in_dim(params, quarter * L, L, 1).astype(f32)
    head_mine = lax.dynamic_slice_in_dim(head_all, quarter * L, L, 0)
    bias_row = jnp.broadcast_to(
        jnp.pad(head_bias.astype(f32), (0, L - tasks))[None, :], (8, L)
    )

    own_big = jnp.broadcast_to(buckets[None, :].astype(f32), (8, images))
    ints = ints[order]
    label_rows = ints.astype(f32)
    big = jnp.broadcast_to(ints[:, tasks : tasks + 1].astype(f32), (images, L))

    act = sds(rows, L, dtype=bf16)
    full = sds(rows, L)
    img = sds(im, L)
    micro = sds(8, L)
    low_kept = kept = Keep(rows, L, dtype=bf16)
    vm = pltpu.VMEM
    conv_scratch = [vm((4 * L, 9 * L), bf16), vm((rows, 9 * L), f32), vm((rows, L), f32)]
    wide_kept = Keep(rows, 4 * L, dtype=bf16)
    back_scratch = [vm((4 * L, 9 * L), bf16), vm((rows, 9 * L), bf16), vm((rows, L), f32)]
    flops_conv = 2 * rows * 4 * L * 9 * L

    def run(kernel, outs, args, scratch, flops=flops_conv, ties=(), through=()):
        return call(functools.partial(kernel, nm), outs, args, scratch, 1, flops, ties, through)

    *first, w_second = run(
        first_forward,
        [act, low_kept, kept, micro, kept, micro],
        (q_arr, feats, w_first, w_short, params, big),
        [vm((rows, cin), bf16), vm((cin, 10 * L), bf16), vm((rows, 10 * L), f32), vm((rows, L), f32), vm((rows, L), f32)],
        through=(rest[0],),
    )
    w_second, w_third = [Pick(w, swap_ac(w)) for w in (w_second, rest[1])]
    w_fourth = Half(rest[2])
    h1 = gather_quarters(first[0])
    second = run(
        second_forward,
        [act, kept, micro, wide_kept],
        (q_arr, *h1, w_second, params, big, first[1]),
        conv_scratch,
    )
    x2 = gather_quarters(second[0])
    third = run(third_forward, [act, kept, micro, wide_kept], (q_arr, *x2, w_third, params, big), conv_scratch)
    h3 = gather_quarters(third[0])
    fourth = run(
        fourth_forward,
        [img, img, kept, micro, wide_kept],
        (q_arr, *h3, w_fourth, params, big, second[0], head_mine),
        conv_scratch,
    )
    pooled, logits = fourth[:2]

    logits = logits + flip(logits, "c")
    stat_rows = tasks + 8
    errors, stats = call(
        lambda mine, other, bias, lab, err, st: head_errors(mine, other, bias, lab, tasks, err, st),
        [sds(images, L), sds(stat_rows, L)],
        (logits, flip(logits, "b"), bias_row, label_rows),
        scalars=0,
    )
    stats = sum_over(sum_over(stats, "a"), "z")
    direct = n_z == 4
    quads = [low_kept] * 4
    own_rows = 9 * channels // n_group
    shared_arr = shared[None].astype(jnp.int32)

    def grad_of(acts, grad, ties, block=0):
        whole = 9 * channels
        out = call(
            functools.partial(weight_grad, block),
            [Keep(whole // 2, L, dtype=bf16)] * 2 if block else [Keep(whole, L, dtype=bf16)],
            (q_arr, acts, grad),
            [vm((rows, 9 * L), bf16)] + ([vm((whole, L), bf16)] if block else []),
            1,
            flops_conv,
            ties,
        )
        return out if block else out[0]

    def over_z(grad):
        return lax.psum_scatter(grad, "z", scatter_dimension=0, tiled=True)

    def to_places(shard):
        parts = []
        for m in range(4):
            pairs = [
                (4 * i + 2 * j + k, 4 * (k ^ (m & 1)) + 2 * (j ^ (m >> 1)) + i)
                for i in range(2)
                for j in range(2)
                for k in range(2)
            ]
            parts.append(lax.ppermute(shard, ("a", "b", "c"), pairs))
        return parts

    *b4, bias_grad, head_grad = call(
        functools.partial(heads_and_fourth, float(images * n_group), tasks, nm),
        [*quads, low_kept, low_kept, sds(8, L), sds(8, L), sds(tasks, L)],
        (
            q_arr, stats, errors, head_all, head_mine, pooled,
            fourth[2], fourth[3], second[0], w_fourth, params, big,
        ),
        back_scratch + [vm((images, L), f32)],
        flops=flops_conv,
    )
    g3 = scatter_quarters(b4[:4])
    dw4 = grad_of(fourth[4], b4[4], (g3[3],))
    *b3, dw4 = run(
        third_backward,
        [*quads, low_kept, sds(8, L)],
        (q_arr, *g3[:3], third[1], third[2], w_third, params, big),
        back_scratch,
        through=(dw4,),
    )
    r4 = over_z(dw4)
    g2 = scatter_quarters(b3[:4])
    dw3 = grad_of(third[3], b3[4], (g2[3],))
    *b2, dw3 = run(
        second_backward,
        [*quads, low_kept, low_kept, sds(8, L)],
        (q_arr, *g2[:3], b4[5], first[1], second[1], second[2], w_second, params, big),
        back_scratch,
        through=(dw3,),
    )
    r3 = over_z(dw3)
    g1 = scatter_quarters(b2[:4])
    dw2 = grad_of(second[3], b2[4], (g1[3],), own_rows if direct else 0)
    if direct:
        dw2, give2 = dw2
        got2 = flip(give2, "a")
    twice = [Keep(2 * rows, L, dtype=bf16)] * 3 + [low_kept] * 2
    b1 = run(
        first_backward,
        [*twice, low_kept, low_kept, sds(8, L)],
        (c_arr, *g1[:3], b2[5], *first[2:], w_first, w_short, params, big),
        [vm((cin, 10 * L), bf16), vm((rows, 10 * L), bf16), vm((rows, L), f32)],
        ties=(dw2,),
    )

    p0, p1, p2, *p3 = b1[:5]
    p1, p3 = flip(p1, "c"), [flip(p, "c") for p in p3]
    (send,) = call(
        add_halves,
        [sds(2 * rows, L, dtype=bf16)],
        (Far(p2), *p3),
        scalars=0,
        ties=(got2,) if direct else (),
    )
    across = flip(send, "b")
    smalls = [head_grad, b1[-1], b2[-1], b3[-1], b4[-1]]
    small_rows = sum(v.shape[0] for v in smalls)
    smalls.append(jnp.zeros((-small_rows % 16 or 16, L), f32))
    small_rows += smalls[-1].shape[0]
    slot_rows = r_first + r_short + small_rows
    grad_args = (q_arr, feats, b1[5], b1[6], big)
    grad_scratch = [vm((rows, cin), bf16), vm((rows, 10 * L), bf16)]

    def low(count):
        return sds(count, L, dtype=bf16)

    def give_a(shards, sizes, ties):
        count = sum(sizes)
        keep, give = call(
            functools.partial(pick_a, sizes),
            [low(count)] * 2,
            (q_arr, *shards),
            ties=ties,
        )
        return keep, flip(give, "a")

    def sum_a(keep, got, ties=()):
        return call(add_low, [low(keep.shape[0])], (Far(keep), Far(got)), scalars=0, ties=ties)[0]

    if direct:
        slots, give1 = call(
            functools.partial(first_weight_grad, (r_first, r_short)),
            [Keep(n_group * slot_rows // 2, L, dtype=bf16)] * 2,
            grad_args + tuple(smalls),
            grad_scratch + [vm((n_group * slot_rows, L), bf16)],
            ties=(send,),
        )
        got1 = flip(give1, "a")
        pair43 = give_a((r4, r3), (own_rows, own_rows), (slots,))
        (total,) = call(add_three, [low(2 * rows)], (Far(p0), Far(p1), Far(across)), scalars=0, ties=(pair43[0],))
        (dw21,) = call(
            functools.partial(sum_beside, n_z),
            [Keep(n_z * (own_rows + slot_rows), L, dtype=bf16)],
            (dw2, got2, slots, got1),
            scalars=0,
            ties=(total,),
        )
        shard21 = over_z(dw21)
    else:
        dw1, dws = call(
            functools.partial(first_weight_grad, None),
            [sds(9 * cin, L, dtype=bf16), sds(cin, L, dtype=bf16)],
            grad_args,
            grad_scratch,
        )
        small = jnp.concatenate(smalls, axis=0).astype(bf16)
        dw21 = [
            dw2.reshape(n_group, own_rows, L),
            dw1.reshape(n_group, r_first, L),
            dws.reshape(n_group, r_short, L),
            jnp.broadcast_to(small[None], (n_group, *small.shape)),
        ]
        dw21 = jnp.concatenate(dw21, axis=1)
        shard21 = lax.psum_scatter(dw21, ("z", "a"), scatter_dimension=0)
        pair43 = give_a((r4, r3), (own_rows, own_rows), ())
        (total,) = call(add_three, [low(2 * rows)], (Far(p0), Far(p1), Far(across)), scalars=0)

    shard43 = sum_a(*pair43, ties=(dw21,))
    places43 = to_places(shard43)
    swapped = swap_ac(total)
    conv_fourth_grad, conv_third_grad = call(
        assemble, [sds(own_rows, channels)] * 2, (shared_arr, *places43)
    )
    (input_grad,) = call(
        input_grad_kernel,
        [sds(grid * grid, cin // 4, images)],
        (q_arr, micro_order, own_big, Pick(total, swapped)),
        ties=(conv_third_grad,),
    )
    places = to_places(shard21)
    group = 2 * iz + ic
    group_arr = jnp.stack([shared, group]).astype(jnp.int32)
    wide_outs = [sds(own_rows, channels), sds(r_first, channels), sds(r_short, channels)]
    if direct:
        conv_second_grad, conv_first_grad, conv_short_grad, gains_grad, biases_grad, head_weight_grad = call(
            functools.partial(assemble_last, block, tasks),
            wide_outs + [sds(5, block), sds(5, block), sds(tasks, block)],
            (group_arr, *places),
            [vm((small_rows, channels), f32)],
        )
    else:
        conv_second_grad, conv_first_grad, conv_short_grad, wide_small = call(
            assemble, wide_outs + [sds(small_rows, channels)], (group_arr, *places)
        )
        own_small = lax.dynamic_slice_in_dim(wide_small, group * block, block, 1)
        head_weight_grad = own_small[:tasks]
        n1, n2, n3, n4 = (own_small[tasks + 8 * i : tasks + 8 * (i + 1)] for i in range(4))
        gains_grad = jnp.stack([n1[0], n1[2], n2[0], n3[0], n4[0]])
        biases_grad = jnp.stack([n1[1], n1[3], n2[1], n3[1], n4[1]])
    input_grad = input_grad.reshape(grid, grid, cin // 4, images).transpose(3, 0, 1, 2)

    moved = lax.ppermute(
        pooled,
        ("a", "b", "c"),
        [(4 * i + 2 * j + k, 4 * j + 2 * k + i) for i in range(2) for j in range(2) for k in range(2)],
    )
    spots = jnp.arange(images, dtype=jnp.int32)
    inverse = jnp.sum(
        jnp.where(micro_order[0][None, :] == spots[:, None], spots[None, :], 0), axis=1
    )
    pooled_out = moved[inverse]

    return (
        pooled_out,
        input_grad,
        conv_first_grad,
        conv_short_grad,
        conv_second_grad,
        conv_third_grad,
        conv_fourth_grad,
        gains_grad,
        biases_grad,
        head_weight_grad.T,
        bias_grad[0, :tasks],
    )


def solution(mesh):
    sections, groups = mesh.shape["section"], mesh.shape["dp"]
    fine = Mesh(mesh.devices.reshape(2, sections // 2, groups // 2, 2), ("a", "b", "z", "c"))
    dp, section = ("z", "c"), ("a", "b")
    return jax.shard_map(
        body,
        mesh=fine,
        in_specs=(
            P(dp, None, None, None),
            P(dp),
            P(dp, None),
            P(dp, None),
            P(dp, None),
            P(dp, None),
            P(dp, None),
            P(dp, None),
            P(dp, None),
            P(None, dp),
            P(None, dp),
            P(dp, None),
            P(),
        ),
        out_specs=(
            P(dp, section),
            P(dp, None, None, section),
            P(dp, None),
            P(dp, None),
            P(dp, None),
            P(dp, None),
            P(dp, None),
            P(None, dp),
            P(None, dp),
            P(dp, None),
            P(),
        ),
        check_vma=False,
    )
```
